512 devices in a mesh: seq: 64 (over y, z), head: 8 (over x, core).
Axes of the slice: x: 4, y: 4, z: 16, core: 2. Of those that a mesh axis runs over, the one named last changes fastest.
Arguments:
- query_rows: bfloat16 [32768, 1024], P(('seq', 'head')), may hold values from -6 to 6
- key_rows: bfloat16 [32768, 1024], P(('seq', 'head')), may hold values from -6 to 6
- value_rows: bfloat16 [32768, 1024], P(('seq', 'head')), may hold values from -6 to 6
- out_grad: bfloat16 [32768, 1024], P(('seq', 'head')), may hold values from -6 to 6
- random_ids: int32 [512, 3], replicated, may hold values from 0 to 511, as said below
- global_ids: int32 [2], replicated, may hold values from 0 to 511, as said below
Outputs:
- attn_out: bfloat16 [32768, 1024], P(('seq', 'head'))
- query_grad: bfloat16 [32768, 1024], P(('seq', 'head'))
- key_grad: bfloat16 [32768, 1024], P(('seq', 'head'))
- value_grad: bfloat16 [32768, 1024], P(('seq', 'head'))
The draws below stay inside these ranges and needn't reach their ends.
Inputs may be any that keep to these rules, and one draw needn't show every extreme that they name: `global_ids`: the two are different, and one of them is block 511. Group g holds query and key blocks g * 8 to g * 8 + 7. For every group, count per group (itself included) the key blocks it reads there: the block just before the group and the block just after it (each once, where present), each of the two global blocks once, and every entry of its rows of random_ids. No count exceeds 3, and for every group some count is exactly 3.
All inputs are finite; a program needn't handle non-finite values.
Results may differ from the reference program's by a relative error of at most 0.0069.
Values may be sent and summed in bfloat16 or wider, within the bound.
A program may use at most 64 MiB of HBM per device.

```python
import jax
import jax.numpy as jnp
from jax import lax

HEADS = 8
HD = 128
BLOCK = 64
QB_DEV = 8
NB = 512
SEQ = 32768
MOST = 3


def base_rows(key, salt):
    sub_key = jax.random.fold_in(key, salt)
    return jnp.clip(jax.random.normal(sub_key, (SEQ, HEADS * HD), jnp.float32), -6.0, 6.0)


def draw_query_rows(key, part):
    rows = base_rows(key, 11)
    return rows.astype(jnp.bfloat16)


def draw_key_rows(key, part):
    rows = base_rows(key, 12)
    return rows.astype(jnp.bfloat16)


def draw_global_ids(key, part):
    pair_key = jax.random.fold_in(key, 501)
    other_block = jax.random.randint(jax.random.fold_in(pair_key, 1), (), 0, NB - 1).astype(jnp.int32)
    flip_bit = jax.random.randint(jax.random.fold_in(pair_key, 2), (), 0, 2).astype(jnp.int32)
    last_block = jnp.int32(NB - 1)
    first_id = jnp.where(flip_bit == 1, last_block, other_block)
    second_id = jnp.where(flip_bit == 1, other_block, last_block)
    return jnp.stack([first_id, second_id]).astype(jnp.int32)


def draw_random_ids(key, part):
    group_total = NB // QB_DEV
    global_pair = draw_global_ids(key, part)
    group_key = jax.random.fold_in(key, 502)
    seat_total = group_total * MOST
    request_count = 3 * QB_DEV

    def one_group(group_index):
        sub_key = jax.random.fold_in(group_key, group_index)
        owner_all = jnp.arange(group_total, dtype=jnp.int32)
        fixed_load = ((owner_all == group_index - 1) & (group_index > 0)).astype(jnp.int32) + ((owner_all == group_index + 1) & (group_index < group_total - 1)).astype(jnp.int32) + (owner_all == global_pair[0] // QB_DEV).astype(jnp.int32) + (owner_all == global_pair[1] // QB_DEV).astype(jnp.int32)
        full_owner = jax.random.randint(jax.random.fold_in(sub_key, 1), (), 0, group_total).astype(jnp.int32)
        need_full = MOST - fixed_load[full_owner]
        seat_owner = jnp.repeat(owner_all, MOST)
        seat_place = jnp.tile(jnp.arange(MOST, dtype=jnp.int32), group_total)
        open_seat = (seat_owner != full_owner) & (seat_place < MOST - fixed_load[seat_owner])
        seat_scores = jax.random.randint(jax.random.fold_in(sub_key, 2), (seat_total,), 0, 1 << 16) * seat_total + jnp.arange(seat_total, dtype=jnp.int32)
        seat_scores = jnp.where(open_seat, seat_scores, seat_scores + (1 << 30))
        seat_order = jnp.argsort(seat_scores)
        chosen = seat_owner[seat_order]
        request_index = jnp.arange(request_count, dtype=jnp.int32)
        picked = chosen[jnp.clip(request_index - need_full, 0, seat_total - 1)]
        owner_list = jnp.where(request_index < need_full, full_owner, picked)
        owner_list = jax.random.permutation(jax.random.fold_in(sub_key, 3), owner_list)
        inner_block = jax.random.randint(jax.random.fold_in(sub_key, 4), (request_count,), 0, QB_DEV)
        return (owner_list * QB_DEV + inner_block).reshape(QB_DEV, 3)
    id_table = jax.vmap(one_group)(jnp.arange(group_total, dtype=jnp.int32))
    return id_table.reshape(NB, 3).astype(jnp.int32)


def levels(own_key, extent, split, smallest, high):
    gain = 1.0
    for axis_at, blocks in split:
        draws = jax.random.uniform(jax.random.fold_in(jax.random.fold_in(own_key, 6), axis_at), (blocks,), jnp.float32, smallest / len(split), high / len(split))
        gain = gain * jnp.repeat(jnp.exp(draws), extent[axis_at] // blocks).reshape((-1,) + (1,) * (len(extent) - 1 - axis_at))
    return gain


def normal_values(rng, shape, spread, bound, split=(), held_as=jnp.bfloat16):
    level = levels(rng, shape, split, -0.22, 0.18) if split else 1.0
    values = jax.random.normal(rng, shape, jnp.float32) * spread * level
    return jnp.minimum(jnp.maximum(values, -bound), bound).astype(held_as)


def setup_inputs(seed: int = 0) -> dict:
    arg_keys = jax.random.split(jax.random.key(seed), 7)
    return {
        "query_rows": draw_query_rows(jax.random.fold_in(arg_keys[6], 71), 0),
        "key_rows": draw_key_rows(jax.random.fold_in(arg_keys[6], 71), 0),
        "value_rows": normal_values(arg_keys[2], (SEQ, HEADS * HD), 1.0, 6.0, ((0, 512),)),
        "out_grad": normal_values(arg_keys[3], (SEQ, HEADS * HD), 1.0, 6.0, ((0, 512),)),
        "random_ids": draw_random_ids(jax.random.fold_in(arg_keys[6], 71), 0),
        "global_ids": draw_global_ids(jax.random.fold_in(arg_keys[6], 71), 0),
    }


def block_math(query_blk, grad_blk, key_sel, value_sel, slot_ok, score_scale):
    scores = jnp.einsum("qbhd,qjkhd->qhbjk", query_blk.astype(jnp.float32), key_sel.astype(jnp.float32)) * score_scale
    scores = jnp.where(slot_ok[:, None, None, :, None], scores, -jnp.inf)
    row_max = jnp.max(scores, axis=(3, 4), keepdims=True)
    expo = jnp.exp(scores - row_max)
    weights = expo / jnp.sum(expo, axis=(3, 4), keepdims=True)
    prob_bf = weights.astype(jnp.bfloat16)
    attention = jnp.einsum("qhbjk,qjkhd->qbhd", prob_bf.astype(jnp.float32), value_sel.astype(jnp.float32))
    row_delta = jnp.sum(grad_blk.astype(jnp.float32) * attention, axis=3)
    dprobs = jnp.einsum("qbhd,qjkhd->qhbjk", grad_blk.astype(jnp.float32), value_sel.astype(jnp.float32))
    delta_t = jnp.transpose(row_delta, (0, 2, 1))[:, :, :, None, None]
    dscores = (weights * (dprobs - delta_t)).astype(jnp.bfloat16)
    query_grad = jnp.einsum("qhbjk,qjkhd->qbhd", dscores.astype(jnp.float32), key_sel.astype(jnp.float32)) * score_scale
    key_terms = jnp.einsum("qhbjk,qbhd->qjkhd", dscores.astype(jnp.float32), query_blk.astype(jnp.float32)) * score_scale
    value_terms = jnp.einsum("qhbjk,qbhd->qjkhd", prob_bf.astype(jnp.float32), grad_blk.astype(jnp.float32))
    return attention, query_grad, key_terms, value_terms


def reference(query_rows, key_rows, value_rows, out_grad, random_ids, global_ids):
    seq_total = query_rows.shape[0]
    blocks_total = seq_total // BLOCK
    group_total = blocks_total // QB_DEV
    score_scale = HD ** -0.5

    def as_tiles(rows):
        return rows.reshape(blocks_total, BLOCK, HEADS, HD)

    query_tiles = as_tiles(query_rows)
    grad_tiles = as_tiles(out_grad)
    key_tiles = as_tiles(key_rows)
    value_tiles = as_tiles(value_rows)
    slot_pos = jnp.arange(8, dtype=jnp.int32)[None, :]
    block_pos = jnp.arange(QB_DEV, dtype=jnp.int32)[:, None]
    round_mask = (slot_pos >= 5) | ((slot_pos == 0) & (block_pos == 0)) | ((slot_pos == 2) & (block_pos == QB_DEV - 1))

    def group_step(carry, group_index):
        key_acc, value_acc = carry
        start = (group_index * QB_DEV).astype(jnp.int32)
        query_blk = lax.dynamic_slice_in_dim(query_tiles, start, QB_DEV, 0)
        grad_blk = lax.dynamic_slice_in_dim(grad_tiles, start, QB_DEV, 0)
        block_ids = start + jnp.arange(QB_DEV, dtype=jnp.int32)
        window_ids = block_ids[:, None] + jnp.arange(-1, 2, dtype=jnp.int32)[None, :]
        global_pair = jnp.broadcast_to(global_ids.astype(jnp.int32)[None, :], (QB_DEV, 2))
        rand_rows = lax.dynamic_slice_in_dim(random_ids.astype(jnp.int32), start, QB_DEV, 0)
        slot_ids = jnp.concatenate([window_ids, global_pair, rand_rows], axis=1)
        window_ok = (window_ids >= 0) & (window_ids < blocks_total)
        slot_ok = jnp.concatenate([window_ok, jnp.ones((QB_DEV, 5), dtype=jnp.bool_)], axis=1)
        clipped = jnp.clip(slot_ids, 0, blocks_total - 1).astype(jnp.int32)
        flat_ids = clipped.reshape(-1)
        key_sel = jnp.take(key_tiles, flat_ids, axis=0).reshape(QB_DEV, 8, BLOCK, HEADS, HD)
        value_sel = jnp.take(value_tiles, flat_ids, axis=0).reshape(QB_DEV, 8, BLOCK, HEADS, HD)
        attention, query_grad, key_terms, value_terms = block_math(query_blk, grad_blk, key_sel, value_sel, slot_ok, score_scale)
        mask_full = round_mask[:, :, None, None, None]
        key_round = lax.optimization_barrier(key_terms.astype(jnp.bfloat16)).astype(jnp.float32)
        value_round = lax.optimization_barrier(value_terms.astype(jnp.bfloat16)).astype(jnp.float32)
        key_terms = jnp.where(mask_full, key_round, key_terms)
        value_terms = jnp.where(mask_full, value_round, value_terms)
        key_acc = key_acc.at[flat_ids].add(key_terms.reshape(QB_DEV * 8, BLOCK, HEADS, HD))
        value_acc = value_acc.at[flat_ids].add(value_terms.reshape(QB_DEV * 8, BLOCK, HEADS, HD))
        return (key_acc, value_acc), (attention.astype(jnp.bfloat16), query_grad.astype(jnp.bfloat16))

    zeros_acc = jnp.zeros((blocks_total, BLOCK, HEADS, HD), jnp.float32)
    (key_acc, value_acc), (attn_all, qgrad_all) = lax.scan(group_step, (zeros_acc, zeros_acc), jnp.arange(group_total, dtype=jnp.int32))
    width = HEADS * HD
    attn_out = attn_all.reshape(seq_total, width)
    query_grad = qgrad_all.reshape(seq_total, width)
    key_grad = key_acc.astype(jnp.bfloat16).reshape(seq_total, width)
    value_grad = value_acc.astype(jnp.bfloat16).reshape(seq_total, width)
    return (attn_out, query_grad, key_grad, value_grad)
```

```python
import functools

import jax
import jax.numpy as jnp
from jax import lax
from jax.experimental import pallas as pl
from jax.experimental.pallas import tpu as pltpu
from jax.sharding import PartitionSpec as P

HD = 128
BLOCK = 64
QB = 8
NH = 8
NY = 4
NZ = 16
COL = NZ * QB
PLANE = NY * QB
SCALE = HD ** (-0.5)
FLOOR = -1e30
UNROLL = 4
MESH = pl.DeviceIdType.MESH
NT = (((1,), (1,)), ((), ()))
TN = (((0,), (0,)), ((), ()))
NN = (((1,), (0,)), ((), ()))
BF = jnp.bfloat16
F32 = jnp.float32
MIB = 1024 * 1024


def rcopy(src, dst, send, recv, seq, head):
    return pltpu.make_async_remote_copy(
        src_ref=src,
        dst_ref=dst,
        send_sem=send,
        recv_sem=recv,
        device_id=(seq, head),
        device_id_type=MESH,
    )


def place():
    seq = lax.axis_index("seq")
    head = lax.axis_index("head")
    return seq, head, seq // NZ, seq % NZ


def greet(peers):
    barrier = pltpu.get_barrier_semaphore()
    for seq, head in peers:
        pl.semaphore_signal(barrier, inc=1, device_id=(seq, head), device_id_type=MESH)
    pl.semaphore_wait(barrier, len(peers))


def head_peers(seq, head):
    return [(seq, (head + d) % NH) for d in range(1, NH)]


def row_peers(y, z, head):
    return [(((y + d) % NY) * NZ + z, head) for d in range(1, NY)]


def ring_peers(y, z, head):
    return [(y * NZ + (z + 1) % NZ, head), (y * NZ + (z + NZ - 1) % NZ, head)]


def gather_kernel(
    q_ref, k_ref, v_ref, g_ref, kv_ref, qg_ref, kvp, qgp, hs, hr, zs, zr, ys, yr
):
    seq, head, y, z = place()
    greet(head_peers(seq, head) + ring_peers(y, z, head) + row_peers(y, z, head))

    for h in range(NH):
        cols = slice(h * HD, (h + 1) * HD)
        kvp[h, 0] = k_ref[:, cols]
        kvp[h, 1] = v_ref[:, cols]

    def kv_head(d, sender, target):
        return rcopy(
            kvp.at[target], kv_ref.at[z, :, sender], hs.at[0, d - 1], hr.at[0, d - 1], seq, target
        )

    def qg_head(d, sender, target):
        return rcopy(
            qgp.at[target], qg_ref.at[y, :, sender], hs.at[1, d - 1], hr.at[1, d - 1], seq, target
        )

    for d in range(1, NH):
        kv_head(d, head, (head + d) % NH).start()
    kv_ref[z, 0, head] = kvp[head, 0]
    kv_ref[z, 1, head] = kvp[head, 1]
    for h in range(NH):
        cols = slice(h * HD, (h + 1) * HD)
        qgp[h, 0] = q_ref[:, cols]
        qgp[h, 1] = g_ref[:, cols]
    for d in range(1, NH):
        qg_head(d, head, (head + d) % NH).start()
    qg_ref[y, 0, head] = qgp[head, 0]
    qg_ref[y, 1, head] = qgp[head, 1]
    for d in range(1, NH):
        kv_head(d, (head + NH - d) % NH, (head + d) % NH).wait_recv()

    right = y * NZ + (z + 1) % NZ
    left = y * NZ + (z + NZ - 1) % NZ

    def hop(way, step, piece, back):
        if way == 0:
            chunk = (z + 2 * NZ - step - back) % NZ
            target = right
        else:
            chunk = (z + step + back) % NZ
            target = left
        ref = kv_ref.at[chunk, piece]
        return rcopy(ref, ref, zs.at[way, step, piece], zr.at[way, step, piece], target, head)

    half = NZ // 2
    hops = [
        (way, step, piece)
        for step in range(half)
        for piece in range(2)
        for way in range(2)
        if step < half - 1 or piece == way
    ]
    for way, step, piece in hops:
        if step == 0:
            hop(way, step, piece, 0).start()

    def row(d, sender, target):
        ref = qg_ref.at[sender]
        return rcopy(ref, ref, ys.at[d - 1], yr.at[d - 1], target * NZ + z, head)

    for d in range(1, NH):
        qg_head(d, (head + NH - d) % NH, (head + d) % NH).wait_recv()
    for d in range(1, NY):
        row(d, y, (y + d) % NY).start()

    for way, step, piece in hops:
        if step > 0:
            hop(way, step - 1, piece, 1).wait_recv()
            hop(way, step, piece, 0).start()
    for d in range(1, NY):
        row(d, (y + NY - d) % NY, (y + d) % NY).wait_recv()
    for way, step, piece in hops:
        if step == half - 1 or (step == half - 2 and piece != way):
            hop(way, step, piece, 1).wait_recv()
    for d in range(1, NH):
        kv_head(d, head, (head + d) % NH).wait_send()
        qg_head(d, head, (head + d) % NH).wait_send()
    for d in range(1, NY):
        row(d, y, (y + d) % NY).wait_send()
    for way, step, piece in hops:
        hop(way, step, piece, 0).wait_send()


def vmem():
    return pl.BlockSpec(memory_space=pltpu.VMEM)


def smem():
    return pl.BlockSpec(memory_space=pltpu.SMEM)


def gather(q, k, v, g):
    dma = pltpu.SemaphoreType.DMA
    return pl.pallas_call(
        gather_kernel,
        out_shape=(
            jax.ShapeDtypeStruct((NZ, 2, QB, BLOCK, HD), BF),
            jax.ShapeDtypeStruct((NY, 2, QB, BLOCK, HD), BF),
        ),
        in_specs=[vmem()] * 4,
        out_specs=(vmem(), vmem()),
        scratch_shapes=[
            pltpu.VMEM((NH, 2, BLOCK, HD), BF),
            pltpu.VMEM((NH, 2, BLOCK, HD), BF),
            dma((2, NH - 1)),
            dma((2, NH - 1)),
            dma((2, NZ // 2, 2)),
            dma((2, NZ // 2, 2)),
            dma((NY - 1,)),
            dma((NY - 1,)),
        ],
        compiler_params=pltpu.CompilerParams(
            collective_id=0, has_side_effects=True, vmem_limit_bytes=24 * MIB
        ),
        name="gather_rows",
    )(q, k, v, g)


def stats_kernel(ids, gids, kv_ref, qg_ref, st_ref, list_ref, pair_stats):
    y = lax.axis_index("seq") // NZ
    z = lax.axis_index("seq") % NZ
    base = y * COL
    pair_stats[0] = jnp.full((QB + 1, PLANE, BLOCK), FLOOR, F32)
    pair_stats[1] = jnp.zeros((QB + 1, PLANE, BLOCK), F32)
    pair_stats[2] = jnp.zeros((QB + 1, PLANE, BLOCK), F32)

    def note(count, i, slot, block, extra=True):
        rel = block - base
        good = (rel >= 0) & (rel < COL) & extra
        list_ref[count] = (i * QB + slot) * COL + rel
        return count + good.astype(jnp.int32)

    def scan(i, count):
        block = ((i >> 3) * NZ + z) * QB + (i & 7)
        count = note(count, i, 0, block - 1)
        count = note(count, i, 1, block)
        count = note(count, i, 2, block + 1)
        count = note(count, i, 3, gids[0])
        count = note(count, i, 4, gids[1])
        for r in range(3):
            count = note(count, i, 5 + r, ids[block * 3 + r])
        return count

    count = lax.fori_loop(0, PLANE, scan, jnp.int32(0))
    trash = PLANE * QB * COL
    for u in range(UNROLL):
        list_ref[count + u] = jnp.int32(trash)
    rounds = (count + UNROLL - 1) >> 2
    list_ref[PLANE * QB + UNROLL] = rounds

    def pairs(t, carry):
        done = []
        for u in range(UNROLL):
            code = list_ref[t * UNROLL + u]
            pair = code >> 7
            rel = code & (COL - 1)
            i = jnp.minimum(pair >> 3, PLANE - 1)
            live = code < trash
            keys = kv_ref[rel >> 3, 0, rel & 7]
            values = kv_ref[rel >> 3, 1, rel & 7]
            queries = qg_ref[i >> 3, 0, i & 7]
            grads = qg_ref[i >> 3, 1, i & 7]
            scores = lax.dot_general(keys, queries, NT, preferred_element_type=F32) * SCALE
            dprobs = lax.dot_general(values, grads, NT, preferred_element_type=F32)
            top = jnp.max(scores, axis=0, keepdims=True)
            expo = jnp.exp(scores - top)
            total = jnp.sum(expo, axis=0, keepdims=True)
            delta = jnp.sum(expo * dprobs, axis=0, keepdims=True)
            slot = jnp.where(live, pair & (QB - 1), QB)
            done.append((i, slot, top, total, delta))
        for i, slot, top, total, delta in done:
            pair_stats[0, slot, pl.ds(i, 1), :] = top
            pair_stats[1, slot, pl.ds(i, 1), :] = total
            pair_stats[2, slot, pl.ds(i, 1), :] = delta
        return carry

    lax.fori_loop(0, rounds, pairs, 0)
    tops = pair_stats[0, 0:QB]
    top = jnp.max(tops, axis=0)
    factor = jnp.exp(tops - top[None])
    st_ref[0] = top
    st_ref[1] = jnp.sum(pair_stats[1, 0:QB] * factor, axis=0)
    st_ref[2] = jnp.sum(pair_stats[2, 0:QB] * factor, axis=0)


def stats(ids, gids, kv, qg):
    return pl.pallas_call(
        stats_kernel,
        out_shape=(
            jax.ShapeDtypeStruct((3, PLANE, BLOCK), F32),
            jax.ShapeDtypeStruct((PLANE * QB + 2 * UNROLL,), jnp.int32),
        ),
        in_specs=[smem(), smem(), vmem(), vmem()],
        out_specs=(vmem(), smem()),
        scratch_shapes=[pltpu.VMEM((3, QB + 1, PLANE, BLOCK), F32)],
        compiler_params=pltpu.CompilerParams(vmem_limit_bytes=24 * MIB),
        name="pair_stats",
    )(ids, gids, kv, qg)


def share_kernel(st_ref, all_ref, send, recv):
    seq, head, y, z = place()
    greet(row_peers(y, z, head))

    def row(d, sender, target):
        return rcopy(
            st_ref, all_ref.at[sender], send.at[d - 1], recv.at[d - 1], target * NZ + z, head
        )

    for d in range(1, NY):
        row(d, y, (y + d) % NY).start()
    all_ref[y] = st_ref[...]
    for d in range(1, NY):
        row(d, (y + NY - d) % NY, (y + d) % NY).wait_recv()
    for d in range(1, NY):
        row(d, y, (y + d) % NY).wait_send()


def share(st):
    dma = pltpu.SemaphoreType.DMA
    return pl.pallas_call(
        share_kernel,
        out_shape=jax.ShapeDtypeStruct((NY, 3, PLANE, BLOCK), F32),
        in_specs=[vmem()],
        out_specs=vmem(),
        scratch_shapes=[dma((NY - 1,)), dma((NY - 1,))],
        compiler_params=pltpu.CompilerParams(
            collective_id=1, has_side_effects=True, vmem_limit_bytes=8 * MIB
        ),
        name="share_stats",
    )(st)


def terms_kernel(list_ref, all_ref, kv_ref, qg_ref, dkv_ref, oq_ref, row_stats, dkv_acc, oq_acc):
    tops = all_ref[:, 0]
    top = jnp.max(tops, axis=0)
    factor = jnp.exp(tops - top[None])
    inverse = 1.0 / jnp.sum(all_ref[:, 1] * factor, axis=0)
    row_stats[0] = top
    row_stats[1] = inverse
    row_stats[2] = jnp.sum(all_ref[:, 2] * factor, axis=0) * inverse

    def clear_kv(b, carry):
        dkv_acc[b] = jnp.zeros((2, BLOCK, HD), F32)
        return carry

    def clear_oq(b, carry):
        oq_acc[b] = jnp.zeros((2, BLOCK, HD), F32)
        return carry

    lax.fori_loop(0, COL, clear_kv, 0)
    lax.fori_loop(0, PLANE, clear_oq, 0)
    trash = PLANE * QB * COL
    rounds = list_ref[PLANE * QB + UNROLL]

    def pairs(t, carry):
        done = []
        for u in range(UNROLL):
            code = list_ref[t * UNROLL + u]
            pair = code >> 7
            rel = code & (COL - 1)
            live = code < trash
            i = jnp.minimum(pair >> 3, PLANE - 1)
            keys = kv_ref[rel >> 3, 0, rel & 7]
            values = kv_ref[rel >> 3, 1, rel & 7]
            queries = qg_ref[i >> 3, 0, i & 7]
            grads = qg_ref[i >> 3, 1, i & 7]
            scores = lax.dot_general(keys, queries, NT, preferred_element_type=F32) * SCALE
            dprobs = lax.dot_general(values, grads, NT, preferred_element_type=F32)
            weights = jnp.exp(scores - row_stats[0, pl.ds(i, 1), :]) * row_stats[1, pl.ds(i, 1), :]
            probs = weights.astype(BF)
            dscores = (weights * (dprobs - row_stats[2, pl.ds(i, 1), :])).astype(BF)
            dv = lax.dot_general(probs, grads, NN, preferred_element_type=F32)
            dk = lax.dot_general(dscores, queries, NN, preferred_element_type=F32) * SCALE
            out = lax.dot_general(probs, values, TN, preferred_element_type=F32)
            dq = lax.dot_general(dscores, keys, TN, preferred_element_type=F32) * SCALE
            rel = jnp.where(live, rel, COL)
            i = jnp.where(live, i, PLANE)
            done.append((i, rel, dk, dv, out, dq))
        for i, rel, dk, dv, out, dq in done:
            dkv_acc[rel, 0] += dk
            dkv_acc[rel, 1] += dv
            oq_acc[i, 0] += out
            oq_acc[i, 1] += dq
        return carry

    lax.fori_loop(0, rounds, pairs, 0)

    def put_kv(b, carry):
        dkv_ref[b >> 3, 0, b & 7] = dkv_acc[b, 0].astype(BF)
        dkv_ref[b >> 3, 1, b & 7] = dkv_acc[b, 1].astype(BF)
        return carry

    def put_oq(b, carry):
        oq_ref[b >> 3, 0, b & 7] = oq_acc[b, 0].astype(BF)
        oq_ref[b >> 3, 1, b & 7] = oq_acc[b, 1].astype(BF)
        return carry

    lax.fori_loop(0, COL, put_kv, 0)
    lax.fori_loop(0, PLANE, put_oq, 0)


def terms(pair_list, all_stats, kv, qg):
    return pl.pallas_call(
        terms_kernel,
        out_shape=(
            jax.ShapeDtypeStruct((NZ, 2, QB, BLOCK, HD), BF),
            jax.ShapeDtypeStruct((NY, 2, QB, BLOCK, HD), BF),
        ),
        in_specs=[smem(), vmem(), vmem(), vmem()],
        out_specs=(vmem(), vmem()),
        scratch_shapes=[
            pltpu.VMEM((3, PLANE, BLOCK), F32),
            pltpu.VMEM((COL + 1, 2, BLOCK, HD), F32),
            pltpu.VMEM((PLANE + 1, 2, BLOCK, HD), F32),
        ],
        compiler_params=pltpu.CompilerParams(vmem_limit_bytes=40 * MIB),
        name="pair_terms",
    )(pair_list, all_stats, kv, qg)


def reduce_kernel(
    dkv_ref, oq_ref, o_ref, dq_ref, dk_ref, dv_ref, rb, yb, pack, hs, hr, zs, zr, ys, yr
):
    seq, head, y, z = place()
    greet(head_peers(seq, head) + ring_peers(y, z, head) + row_peers(y, z, head))
    right = y * NZ + (z + 1) % NZ
    left = y * NZ + (z + NZ - 1) % NZ
    half = NZ // 2
    outs = (o_ref, dq_ref, dk_ref, dv_ref)

    def chunk_of(way, step):
        if way == 0:
            return (z + half - step) % NZ
        return (z + half + step) % NZ

    def hop(way, step, piece):
        if step == 0 or (step == 1 and piece != way):
            src = dkv_ref.at[chunk_of(way, step), piece]
        else:
            src = rb.at[way, step - 1, piece]
        target = right if way == 0 else left
        return rcopy(
            src,
            rb.at[way, step, piece],
            zs.at[way, step, piece],
            zr.at[way, step, piece],
            target,
            head,
        )

    def row(d, target):
        return rcopy(
            oq_ref.at[target], yb.at[d - 1], ys.at[d - 1], yr.at[d - 1], target * NZ + z, head
        )

    def scatter(a, d, sender, target):
        cols = pl.ds(pl.multiple_of(sender * HD, HD), HD)
        return rcopy(
            pack.at[a, target], outs[a].at[:, cols], hs.at[a, d - 1], hr.at[a, d - 1], seq, target
        )

    def send_heads(a):
        for d in range(1, NH):
            scatter(a, d, head, (head + d) % NH).start()
        cols = pl.ds(pl.multiple_of(head * HD, HD), HD)
        outs[a][:, cols] = pack[a, head]

    hop(0, 0, 0).start()
    hop(1, 0, 1).start()
    for way, piece in ((0, 1), (1, 0)):
        hop(way, 1, piece).start()
    for d in range(1, NY):
        row(d, (y + d) % NY).start()

    for step in range(1, half):
        for piece in range(2):
            for way in range(2):
                if step == 1 and piece != way:
                    continue
                hop(way, step - 1, piece).wait_recv()
                chunk = chunk_of(way, step)

                def add(b, carry, way=way, step=step, piece=piece, chunk=chunk):
                    mine = dkv_ref[chunk, piece, b].astype(F32)
                    rb[way, step - 1, piece, b] = (
                        rb[way, step - 1, piece, b].astype(F32) + mine
                    ).astype(BF)
                    return carry

                lax.fori_loop(0, QB, add, 0)
                hop(way, step, piece).start()
        if step == half - 2:
            for d in range(1, NY):
                row(d, (y + d) % NY).wait_recv()

            def total(b, carry):
                for a in range(2):
                    acc = oq_ref[y, a, b].astype(F32)
                    for d in range(NY - 1):
                        acc = acc + yb[d, a, b].astype(F32)
                    pack[a, b] = acc.astype(BF)
                return carry

            lax.fori_loop(0, QB, total, 0)
            send_heads(0)
            send_heads(1)

    for piece in range(2):
        for way in range(2):
            hop(way, half - 1, piece).wait_recv()

        def last(b, carry, piece=piece):
            acc = dkv_ref[z, piece, b].astype(F32)
            acc = acc + rb[0, half - 1, piece, b].astype(F32)
            acc = acc + rb[1, half - 1, piece, b].astype(F32)
            pack[2 + piece, b] = acc.astype(BF)
            return carry

        lax.fori_loop(0, QB, last, 0)
        send_heads(2 + piece)

    for a in range(4):
        for d in range(1, NH):
            scatter(a, d, (head + NH - d) % NH, (head + d) % NH).wait_recv()
    for a in range(4):
        for d in range(1, NH):
            scatter(a, d, head, (head + d) % NH).wait_send()
    for d in range(1, NY):
        row(d, (y + d) % NY).wait_send()
    for step in range(half):
        for piece in range(2):
            for way in range(2):
                if step > 0 or piece == way:
                    hop(way, step, piece).wait_send()


def reduce(dkv, oq):
    dma = pltpu.SemaphoreType.DMA
    out = jax.ShapeDtypeStruct((BLOCK, NH * HD), BF)
    return pl.pallas_call(
        reduce_kernel,
        out_shape=(out,) * 4,
        in_specs=[vmem()] * 2,
        out_specs=(vmem(),) * 4,
        scratch_shapes=[
            pltpu.VMEM((2, NZ // 2, 2, QB, BLOCK, HD), BF),
            pltpu.VMEM((NY - 1, 2, QB, BLOCK, HD), BF),
            pltpu.VMEM((4, NH, BLOCK, HD), BF),
            dma((4, NH - 1)),
            dma((4, NH - 1)),
            dma((2, NZ // 2, 2)),
            dma((2, NZ // 2, 2)),
            dma((NY - 1,)),
            dma((NY - 1,)),
        ],
        compiler_params=pltpu.CompilerParams(
            collective_id=2, has_side_effects=True, vmem_limit_bytes=32 * MIB
        ),
        name="reduce_rows",
    )(dkv, oq)


def shards(query_rows, key_rows, value_rows, out_grad, random_ids, global_ids):
    kv, qg = gather(query_rows, key_rows, value_rows, out_grad)
    st, pair_list = stats(random_ids.reshape(-1), global_ids, kv, qg)
    dkv, oq = terms(pair_list, share(st), kv, qg)
    return reduce(dkv, oq)


def solution(mesh):
    rows = P(("seq", "head"), None)
    return jax.shard_map(
        shards,
        mesh=mesh,
        in_specs=(rows, rows, rows, rows, P(), P()),
        out_specs=(rows,) * 4,
        check_vma=False,
    )
```

```python
import functools

import jax
import jax.numpy as jnp
from jax import lax
from jax.experimental import pallas as pl
from jax.experimental.pallas import tpu as pltpu
from jax.sharding import PartitionSpec as P

HD = 128
BLOCK = 64
QB = 8
NH = 8
NY = 4
NZ = 16
COL = NZ * QB
PLANE = NY * QB
SCALE = HD ** (-0.5)
FLOOR = -1e30
UNROLL = 4
TILES = PLANE // 4
TRASH = PLANE * 4 * COL
LIST = PLANE * 4 + 8
MESH = pl.DeviceIdType.MESH
NT = (((1,), (1,)), ((), ()))
TN = (((0,), (0,)), ((), ()))
NN = (((1,), (0,)), ((), ()))
BF = jnp.bfloat16
F32 = jnp.float32
MIB = 1024 * 1024


def rcopy(src, dst, send, recv, seq, head):
    return pltpu.make_async_remote_copy(
        src_ref=src,
        dst_ref=dst,
        send_sem=send,
        recv_sem=recv,
        device_id=(seq, head),
        device_id_type=MESH,
    )


def place():
    seq = lax.axis_index("seq")
    head = lax.axis_index("head")
    return seq, head, seq // NZ, seq % NZ


def greet(peers):
    barrier = pltpu.get_barrier_semaphore()
    for seq, head in peers:
        pl.semaphore_signal(barrier, inc=1, device_id=(seq, head), device_id_type=MESH)
    pl.semaphore_wait(barrier, len(peers))


def head_peers(seq, head):
    return [(seq, (head + d) % NH) for d in range(1, NH)]


def row_peers(y, z, head):
    return [(((y + d) % NY) * NZ + z, head) for d in range(1, NY)]


def ring_peers(y, z, head):
    return [(y * NZ + (z + 1) % NZ, head), (y * NZ + (z + NZ - 1) % NZ, head)]


def window_tile(c, kv_ref, qg_ref, y, z):
    lo, hi = max(2 * c - 1, 0), min(2 * c + 3, QB)
    shape = ((hi - lo) * BLOCK, HD)
    keys = kv_ref[z, 0, lo:hi].reshape(shape)
    values = kv_ref[z, 1, lo:hi].reshape(shape)
    queries = qg_ref[y, 0, 2 * c : 2 * c + 2].reshape(2 * BLOCK, HD)
    grads = qg_ref[y, 1, 2 * c : 2 * c + 2].reshape(2 * BLOCK, HD)
    scores = lax.dot_general(keys, queries, NT, preferred_element_type=F32) * SCALE
    dprobs = lax.dot_general(values, grads, NT, preferred_element_type=F32)
    gap = (lo - 2 * c) + (lax.broadcasted_iota(jnp.int32, shape, 0) >> 6)
    gap = gap - (lax.broadcasted_iota(jnp.int32, shape, 1) >> 6)
    near = (gap >= -1) & (gap <= 1)
    return lo, hi, keys, values, queries, grads, jnp.where(near, scores, FLOOR), dprobs


def gather_kernel(
    q_ref, k_ref, v_ref, g_ref, kv_ref, qg_ref, wst_ref, own, hs, hr, zs, zr, ys, yr
):
    seq, head, y, z = place()
    ins = (k_ref, v_ref, q_ref, g_ref)

    def home(a, sender):
        return kv_ref.at[z, a, sender] if a < 2 else qg_ref.at[y, a - 2, sender]

    def cols(h):
        return pl.ds(pl.multiple_of(h * HD, HD), HD)

    def keep(a):
        return pltpu.make_async_copy(ins[a].at[:, cols(head)], home(a, head), own.at[a])

    def give(a, d, sender, target):
        return rcopy(
            ins[a].at[:, cols(target)],
            home(a, sender),
            hs.at[a, d - 1],
            hr.at[a, d - 1],
            seq,
            target,
        )

    def give_all(a):
        for d in range(1, NH):
            give(a, d, head, (head + d) % NH).start()

    def take_all(a):
        for d in range(1, NH):
            give(a, d, (head + NH - d) % NH, (head + d) % NH).wait_recv()
        keep(a).wait()

    for a in range(4):
        keep(a).start()
    greet(head_peers(seq, head) + ring_peers(y, z, head) + row_peers(y, z, head))
    give_all(0)
    give_all(1)

    right = y * NZ + (z + 1) % NZ
    left = y * NZ + (z + NZ - 1) % NZ

    def hop(way, step, piece, back):
        if way == 0:
            chunk = (z + 2 * NZ - step - back) % NZ
            target = right
        else:
            chunk = (z + step + back) % NZ
            target = left
        ref = kv_ref.at[chunk, piece]
        return rcopy(ref, ref, zs.at[way, step, piece], zr.at[way, step, piece], target, head)

    half = NZ // 2
    hops = [
        (way, step, piece)
        for step in range(half)
        for piece in range(2)
        for way in range(2)
        if step < half - 1 or piece == way
    ]
    for piece in range(2):
        take_all(piece)
        for way in range(2):
            hop(way, 0, piece, 0).start()
    give_all(2)
    give_all(3)

    def row(d, sender, target):
        ref = qg_ref.at[sender]
        return rcopy(ref, ref, ys.at[d - 1], yr.at[d - 1], target * NZ + z, head)

    wst_ref[0] = jnp.full((PLANE // 2, HD), FLOOR, F32)
    wst_ref[1] = jnp.zeros((PLANE // 2, HD), F32)
    wst_ref[2] = jnp.zeros((PLANE // 2, HD), F32)

    def window(c):
        _, _, _, _, _, _, scores, dprobs = window_tile(c, kv_ref, qg_ref, y, z)
        top = jnp.max(scores, axis=0, keepdims=True)
        expo = jnp.exp(scores - top)
        at = pl.ds(y * (QB // 2) + c, 1)
        wst_ref[0, at, :] = top
        wst_ref[1, at, :] = jnp.sum(expo, axis=0, keepdims=True)
        wst_ref[2, at, :] = jnp.sum(expo * dprobs, axis=0, keepdims=True)

    for way, step, piece in hops:
        if step == 0:
            continue
        hop(way, step - 1, piece, 1).wait_recv()
        hop(way, step, piece, 0).start()
        if piece == 1 and way == 1:
            if step == 1:
                take_all(2)
                take_all(3)
                for d in range(1, NY):
                    row(d, y, (y + d) % NY).start()
            elif step <= 5:
                window(step - 2)
    for d in range(1, NY):
        row(d, (y + NY - d) % NY, (y + d) % NY).wait_recv()
    for way, step, piece in hops:
        if step == half - 1 or (step == half - 2 and piece != way):
            hop(way, step, piece, 1).wait_recv()
    for a in range(4):
        for d in range(1, NH):
            give(a, d, head, (head + d) % NH).wait_send()
    for d in range(1, NY):
        row(d, y, (y + d) % NY).wait_send()
    for way, step, piece in hops:
        hop(way, step, piece, 0).wait_send()


def vmem():
    return pl.BlockSpec(memory_space=pltpu.VMEM)


def smem():
    return pl.BlockSpec(memory_space=pltpu.SMEM)


def hbm():
    return pl.BlockSpec(memory_space=pltpu.HBM)


def gather(q, k, v, g):
    dma = pltpu.SemaphoreType.DMA
    return pl.pallas_call(
        gather_kernel,
        out_shape=(
            jax.ShapeDtypeStruct((NZ, 2, QB, BLOCK, HD), BF),
            jax.ShapeDtypeStruct((NY, 2, QB, BLOCK, HD), BF),
            jax.ShapeDtypeStruct((3, PLANE // 2, HD), F32),
        ),
        in_specs=[hbm()] * 4,
        out_specs=(vmem(),) * 3,
        scratch_shapes=[
            dma((4,)),
            dma((4, NH - 1)),
            dma((4, NH - 1)),
            dma((2, NZ // 2, 2)),
            dma((2, NZ // 2, 2)),
            dma((NY - 1,)),
            dma((NY - 1,)),
        ],
        compiler_params=pltpu.CompilerParams(
            collective_id=0, has_side_effects=True, vmem_limit_bytes=24 * MIB
        ),
        name="gather_rows",
    )(q, k, v, g)


def stats_kernel(ids, gids, kv_ref, qg_ref, wst_ref, st_ref, list_ref, one, full):
    y = lax.axis_index("seq") // NZ
    z = lax.axis_index("seq") % NZ
    base = y * COL
    one[0] = jnp.full((2, 5, PLANE // 2, HD), FLOOR, F32)
    full[0] = jnp.full((3, PLANE // 2, HD), FLOOR, F32)
    for k in range(1, 3):
        one[k] = jnp.zeros((2, 5, PLANE // 2, HD), F32)
        full[k] = jnp.zeros((3, PLANE // 2, HD), F32)
    for k in range(3):
        full[k, 2] = wst_ref[k]

    def note(count, i, slot, block):
        rel = block - base
        good = (rel >= 0) & (rel < COL)
        list_ref[count] = (i * 4 + slot) * COL + rel
        return count + good.astype(jnp.int32)

    count = jnp.int32(0)
    for g in range(NY):
        first = (g * NZ + z) * QB
        count = note(count, g * QB, 3, first - 1)
        count = note(count, g * QB + QB - 1, 3, first + QB)

        def scan(b, count, g=g, first=first):
            for r in range(3):
                count = note(count, g * QB + b, r, ids[r, first + b])
            return count

        count = lax.fori_loop(0, QB, scan, count, unroll=4)
    for u in range(UNROLL):
        list_ref[count + u] = jnp.int32(TRASH)
    rounds = (count + UNROLL - 1) >> 2
    list_ref[LIST - 1] = rounds

    def pairs(t, carry):
        done = []
        for u in range(UNROLL):
            code = list_ref[t * UNROLL + u]
            pair = code >> 7
            rel = code & (COL - 1)
            i = jnp.minimum(pair >> 2, PLANE - 1)
            keys = kv_ref[rel >> 3, 0, rel & 7]
            values = kv_ref[rel >> 3, 1, rel & 7]
            queries = qg_ref[i >> 3, 0, i & 7]
            grads = qg_ref[i >> 3, 1, i & 7]
            scores = lax.dot_general(keys, queries, NT, preferred_element_type=F32) * SCALE
            dprobs = lax.dot_general(values, grads, NT, preferred_element_type=F32)
            top = jnp.max(scores, axis=0, keepdims=True)
            expo = jnp.exp(scores - top)
            total = jnp.sum(expo, axis=0, keepdims=True)
            delta = jnp.sum(expo * dprobs, axis=0, keepdims=True)
            slot = jnp.where(code < TRASH, pair & 3, 4)
            done.append((i, slot, (top, total, delta)))
        for i, slot, found in done:
            for k in range(3):
                one[k, i & 1, slot, pl.ds(i >> 1, 1), 0:BLOCK] = found[k]
        return carry

    lax.fori_loop(0, rounds, pairs, 0)

    for n in range(2):
        rel = gids[n] - base

        @pl.when((rel >= 0) & (rel < COL))
        def _(n=n, rel=rel):
            keys = kv_ref[rel >> 3, 0, rel & 7]
            values = kv_ref[rel >> 3, 1, rel & 7]
            for t in range(TILES):
                queries, grads = tile_rows(qg_ref, t)
                scores = lax.dot_general(keys, queries, NT, preferred_element_type=F32) * SCALE
                dprobs = lax.dot_general(values, grads, NT, preferred_element_type=F32)
                top = jnp.max(scores, axis=0, keepdims=True)
                expo = jnp.exp(scores - top)
                total = jnp.sum(expo, axis=0, keepdims=True)
                delta = jnp.sum(expo * dprobs, axis=0, keepdims=True)
                for k, found in enumerate((top, total, delta)):
                    for p in range(2):
                        full[k, n, 2 * t + p : 2 * t + p + 1] = found[:, p * HD : (p + 1) * HD]

    def parts(k):
        even = one[k, 0, 0:4]
        odd = pltpu.roll(one[k, 1, 0:4].reshape(2 * PLANE, HD), BLOCK, 1)
        return jnp.concatenate([even, odd.reshape(4, PLANE // 2, HD), full[k]], axis=0)

    tops = parts(0)
    top = jnp.max(tops, axis=0)
    factor = jnp.exp(tops - top[None])
    st_ref[0] = top
    st_ref[1] = jnp.sum(parts(1) * factor, axis=0)
    st_ref[2] = jnp.sum(parts(2) * factor, axis=0)


def tile_rows(qg_ref, t):
    at = slice((t % 2) * 4, (t % 2) * 4 + 4)
    queries = qg_ref[t // 2, 0, at].reshape(4 * BLOCK, HD)
    grads = qg_ref[t // 2, 1, at].reshape(4 * BLOCK, HD)
    return queries, grads


def stats(ids, gids, kv, qg, wst):
    return pl.pallas_call(
        stats_kernel,
        out_shape=(
            jax.ShapeDtypeStruct((3, PLANE // 2, HD), F32),
            jax.ShapeDtypeStruct((LIST,), jnp.int32),
        ),
        in_specs=[smem(), smem(), vmem(), vmem(), vmem()],
        out_specs=(vmem(), smem()),
        scratch_shapes=[
            pltpu.VMEM((3, 2, 5, PLANE // 2, HD), F32),
            pltpu.VMEM((3, 3, PLANE // 2, HD), F32),
        ],
        compiler_params=pltpu.CompilerParams(vmem_limit_bytes=24 * MIB),
        name="pair_stats",
    )(ids, gids, kv, qg, wst)


def share_kernel(st_ref, all_ref, send, recv):
    seq, head, y, z = place()
    greet(row_peers(y, z, head))

    def row(d, sender, target):
        return rcopy(
            st_ref, all_ref.at[sender], send.at[d - 1], recv.at[d - 1], target * NZ + z, head
        )

    for d in range(1, NY):
        row(d, y, (y + d) % NY).start()
    all_ref[y] = st_ref[...]
    for d in range(1, NY):
        row(d, (y + NY - d) % NY, (y + d) % NY).wait_recv()
    for d in range(1, NY):
        row(d, y, (y + d) % NY).wait_send()


def share(st):
    dma = pltpu.SemaphoreType.DMA
    return pl.pallas_call(
        share_kernel,
        out_shape=jax.ShapeDtypeStruct((NY, 3, PLANE // 2, HD), F32),
        in_specs=[vmem()],
        out_specs=vmem(),
        scratch_shapes=[dma((NY - 1,)), dma((NY - 1,))],
        compiler_params=pltpu.CompilerParams(
            collective_id=1, has_side_effects=True, vmem_limit_bytes=8 * MIB
        ),
        name="share_stats",
    )(st)


def terms_kernel(
    list_ref, gids, all_ref, kv_ref, qg_ref, dkv_ref, oq_ref, rows_ref, shifted, oq_acc
):
    base = (lax.axis_index("seq") // NZ) * COL
    tops = all_ref[:, 0]
    top = jnp.max(tops, axis=0)
    factor = jnp.exp(tops - top[None])
    inverse = 1.0 / jnp.sum(all_ref[:, 1] * factor, axis=0)
    delta = jnp.sum(all_ref[:, 2] * factor, axis=0) * inverse
    for k, value in enumerate((top, inverse, delta)):
        rows_ref[k] = value
        shifted[k, 0] = value
        shifted[k, 1] = pltpu.roll(value, BLOCK, 1)

    def clear_kv(b, carry):
        dkv_ref[b] = jnp.zeros((2, QB, BLOCK, HD), BF)
        return carry

    def clear_oq(b, carry):
        oq_acc[b] = jnp.zeros((2, QB, BLOCK, HD), F32)
        return carry

    lax.fori_loop(0, NZ, clear_kv, 0)
    lax.fori_loop(0, NY, clear_oq, 0)
    rounds = list_ref[LIST - 1]

    def add_kv(rel, dk, dv):
        for a, term in enumerate((dk, dv)):
            old = dkv_ref[rel >> 3, a, rel & 7].astype(F32)
            dkv_ref[rel >> 3, a, rel & 7] = (old + term).astype(BF)

    def pairs(t, carry):
        done = []
        for u in range(UNROLL):
            code = list_ref[t * UNROLL + u]
            pair = code >> 7
            rel = code & (COL - 1)
            i = jnp.minimum(pair >> 2, PLANE - 1)
            at = pl.ds(i >> 1, 1)
            keys = kv_ref[rel >> 3, 0, rel & 7]
            values = kv_ref[rel >> 3, 1, rel & 7]
            queries = qg_ref[i >> 3, 0, i & 7]
            grads = qg_ref[i >> 3, 1, i & 7]
            scores = lax.dot_general(keys, queries, NT, preferred_element_type=F32) * SCALE
            dprobs = lax.dot_general(values, grads, NT, preferred_element_type=F32)
            weights = jnp.exp(scores - shifted[0, i & 1, at, 0:BLOCK])
            weights = weights * shifted[1, i & 1, at, 0:BLOCK]
            weights = jnp.where(code < TRASH, weights, 0.0)
            probs = weights.astype(BF)
            dscores = (weights * (dprobs - shifted[2, i & 1, at, 0:BLOCK])).astype(BF)
            dv = lax.dot_general(probs, grads, NN, preferred_element_type=F32)
            dk = lax.dot_general(dscores, queries, NN, preferred_element_type=F32) * SCALE
            out = lax.dot_general(probs, values, TN, preferred_element_type=F32)
            dq = lax.dot_general(dscores, keys, TN, preferred_element_type=F32) * SCALE
            done.append((i, rel, dk, dv, out, dq))
        for i, rel, dk, dv, out, dq in done:
            add_kv(rel, dk, dv)
            oq_acc[i >> 3, 0, i & 7] += out
            oq_acc[i >> 3, 1, i & 7] += dq
        return carry

    lax.fori_loop(0, rounds, pairs, 0)

    for n in range(2):
        rel = gids[n] - base

        @pl.when((rel >= 0) & (rel < COL))
        def _(rel=rel):
            keys = kv_ref[rel >> 3, 0, rel & 7]
            values = kv_ref[rel >> 3, 1, rel & 7]
            dk = jnp.zeros((BLOCK, HD), F32)
            dv = jnp.zeros((BLOCK, HD), F32)
            for t in range(TILES):
                queries, grads = tile_rows(qg_ref, t)

                def wide(k, t=t):
                    pair = [rows_ref[k, 2 * t + p : 2 * t + p + 1] for p in range(2)]
                    return jnp.concatenate(pair, axis=1)

                scores = lax.dot_general(keys, queries, NT, preferred_element_type=F32) * SCALE
                dprobs = lax.dot_general(values, grads, NT, preferred_element_type=F32)
                weights = jnp.exp(scores - wide(0)) * wide(1)
                probs = weights.astype(BF)
                dscores = (weights * (dprobs - wide(2))).astype(BF)
                dv = dv + lax.dot_general(probs, grads, NN, preferred_element_type=F32)
                dk = dk + lax.dot_general(dscores, queries, NN, preferred_element_type=F32) * SCALE
                out = lax.dot_general(probs, values, TN, preferred_element_type=F32)
                dq = lax.dot_general(dscores, keys, TN, preferred_element_type=F32) * SCALE
                at = slice((t % 2) * 4, (t % 2) * 4 + 4)
                oq_acc[t // 2, 0, at] += out.reshape(4, BLOCK, HD)
                oq_acc[t // 2, 1, at] += dq.reshape(4, BLOCK, HD)
            add_kv(rel, dk, dv)

    def put_oq(b, carry):
        oq_ref[b] = oq_acc[b].astype(BF)
        return carry

    lax.fori_loop(0, NY, put_oq, 0)


def terms(pair_list, gids, all_stats, kv, qg):
    return pl.pallas_call(
        terms_kernel,
        out_shape=(
            jax.ShapeDtypeStruct((NZ, 2, QB, BLOCK, HD), BF),
            jax.ShapeDtypeStruct((NY, 2, QB, BLOCK, HD), BF),
            jax.ShapeDtypeStruct((3, PLANE // 2, HD), F32),
        ),
        in_specs=[smem(), smem(), vmem(), vmem(), vmem()],
        out_specs=(vmem(),) * 3,
        scratch_shapes=[
            pltpu.VMEM((3, 2, PLANE // 2, HD), F32),
            pltpu.VMEM((NY, 2, QB, BLOCK, HD), F32),
        ],
        compiler_params=pltpu.CompilerParams(vmem_limit_bytes=32 * MIB),
        name="pair_terms",
    )(pair_list, gids, all_stats, kv, qg)


def reduce_kernel(
    kv_ref,
    qg_ref,
    rows_ref,
    dkv_ref,
    oq_ref,
    o_ref,
    dq_ref,
    dk_ref,
    dv_ref,
    rb,
    yb,
    pack,
    near_kv,
    near_oq,
    hs,
    hr,
    zs,
    zr,
    ys,
    yr,
):
    seq, head, y, z = place()
    greet(head_peers(seq, head) + ring_peers(y, z, head) + row_peers(y, z, head))
    right = y * NZ + (z + 1) % NZ
    left = y * NZ + (z + NZ - 1) % NZ
    half = NZ // 2
    outs = (o_ref, dq_ref, dk_ref, dv_ref)

    def chunk_of(way, step):
        if way == 0:
            return (z + half - step) % NZ
        return (z + half + step) % NZ

    def hop(way, step, piece):
        if step == 0 or (step == 1 and piece != way):
            src = dkv_ref.at[chunk_of(way, step), piece]
        else:
            src = rb.at[way, step - 1, piece]
        target = right if way == 0 else left
        return rcopy(
            src,
            rb.at[way, step, piece],
            zs.at[way, step, piece],
            zr.at[way, step, piece],
            target,
            head,
        )

    def row(d, target):
        return rcopy(
            oq_ref.at[target], yb.at[d - 1], ys.at[d - 1], yr.at[d - 1], target * NZ + z, head
        )

    def scatter(a, d, sender, target):
        cols = pl.ds(pl.multiple_of(sender * HD, HD), HD)
        return rcopy(
            pack.at[a, target], outs[a].at[:, cols], hs.at[a, d - 1], hr.at[a, d - 1], seq, target
        )

    def send_heads(a):
        for d in range(1, NH):
            scatter(a, d, head, (head + d) % NH).start()
        cols = pl.ds(pl.multiple_of(head * HD, HD), HD)
        outs[a][:, cols] = pack[a, head]

    hop(0, 0, 0).start()
    hop(1, 0, 1).start()
    for way, piece in ((0, 1), (1, 0)):
        hop(way, 1, piece).start()
    for d in range(1, NY):
        row(d, (y + d) % NY).start()

    near_kv[...] = jnp.zeros((2, QB, BLOCK, HD), F32)

    def window(c):
        lo, hi, keys, values, queries, grads, scores, dprobs = window_tile(c, kv_ref, qg_ref, y, z)
        at = pl.ds(y * (QB // 2) + c, 1)
        weights = jnp.exp(scores - rows_ref[0, at, :]) * rows_ref[1, at, :]
        probs = weights.astype(BF)
        dscores = (weights * (dprobs - rows_ref[2, at, :])).astype(BF)
        dv = lax.dot_general(probs, grads, NN, preferred_element_type=F32)
        dk = lax.dot_general(dscores, queries, NN, preferred_element_type=F32) * SCALE
        out = lax.dot_general(probs, values, TN, preferred_element_type=F32)
        dq = lax.dot_general(dscores, keys, TN, preferred_element_type=F32) * SCALE
        near_kv[0, lo:hi] += dk.reshape(hi - lo, BLOCK, HD)
        near_kv[1, lo:hi] += dv.reshape(hi - lo, BLOCK, HD)
        near_oq[0, 2 * c : 2 * c + 2] = out.reshape(2, BLOCK, HD)
        near_oq[1, 2 * c : 2 * c + 2] = dq.reshape(2, BLOCK, HD)

    for step in range(1, half):
        for piece in range(2):
            for way in range(2):
                if step == 1 and piece != way:
                    continue
                hop(way, step - 1, piece).wait_recv()
                chunk = chunk_of(way, step)

                def add(b, carry, way=way, step=step, piece=piece, chunk=chunk):
                    mine = dkv_ref[chunk, piece, b].astype(F32)
                    rb[way, step - 1, piece, b] = (
                        rb[way, step - 1, piece, b].astype(F32) + mine
                    ).astype(BF)
                    return carry

                lax.fori_loop(0, QB, add, 0)
                hop(way, step, piece).start()
        if step <= 4:
            window(step - 1)
        if step == half - 2:
            for d in range(1, NY):
                row(d, (y + d) % NY).wait_recv()

            def total(b, carry):
                for a in range(2):
                    acc = near_oq[a, b] + oq_ref[y, a, b].astype(F32)
                    for d in range(NY - 1):
                        acc = acc + yb[d, a, b].astype(F32)
                    pack[a, b] = acc.astype(BF)
                return carry

            lax.fori_loop(0, QB, total, 0)
            send_heads(0)
            send_heads(1)

    for piece in range(2):
        for way in range(2):
            hop(way, half - 1, piece).wait_recv()

        def last(b, carry, piece=piece):
            acc = near_kv[piece, b] + dkv_ref[z, piece, b].astype(F32)
            acc = acc + rb[0, half - 1, piece, b].astype(F32)
            acc = acc + rb[1, half - 1, piece, b].astype(F32)
            pack[2 + piece, b] = acc.astype(BF)
            return carry

        lax.fori_loop(0, QB, last, 0)
        send_heads(2 + piece)

    for a in range(4):
        for d in range(1, NH):
            scatter(a, d, (head + NH - d) % NH, (head + d) % NH).wait_recv()
    for a in range(4):
        for d in range(1, NH):
            scatter(a, d, head, (head + d) % NH).wait_send()
    for d in range(1, NY):
        row(d, (y + d) % NY).wait_send()
    for step in range(half):
        for piece in range(2):
            for way in range(2):
                if step > 0 or piece == way:
                    hop(way, step, piece).wait_send()


def reduce(kv, qg, rows, dkv, oq):
    dma = pltpu.SemaphoreType.DMA
    out = jax.ShapeDtypeStruct((BLOCK, NH * HD), BF)
    return pl.pallas_call(
        reduce_kernel,
        out_shape=(out,) * 4,
        in_specs=[vmem()] * 5,
        out_specs=(vmem(),) * 4,
        scratch_shapes=[
            pltpu.VMEM((2, NZ // 2, 2, QB, BLOCK, HD), BF),
            pltpu.VMEM((NY - 1, 2, QB, BLOCK, HD), BF),
            pltpu.VMEM((4, NH, BLOCK, HD), BF),
            pltpu.VMEM((2, QB, BLOCK, HD), F32),
            pltpu.VMEM((2, QB, BLOCK, HD), F32),
            dma((4, NH - 1)),
            dma((4, NH - 1)),
            dma((2, NZ // 2, 2)),
            dma((2, NZ // 2, 2)),
            dma((NY - 1,)),
            dma((NY - 1,)),
        ],
        compiler_params=pltpu.CompilerParams(
            collective_id=2, has_side_effects=True, vmem_limit_bytes=32 * MIB
        ),
        name="reduce_rows",
    )(kv, qg, rows, dkv, oq)


def deliver_kernel(*refs):
    sems = refs[8]
    copies = [pltpu.make_async_copy(refs[a], refs[4 + a], sems.at[a]) for a in range(4)]
    for copy in copies:
        copy.start()
    for copy in copies:
        copy.wait()


def deliver(outs):
    return pl.pallas_call(
        deliver_kernel,
        out_shape=tuple(jax.ShapeDtypeStruct(o.shape, o.dtype) for o in outs),
        in_specs=[vmem()] * 4,
        out_specs=(hbm(),) * 4,
        scratch_shapes=[pltpu.SemaphoreType.DMA((4,))],
        compiler_params=pltpu.CompilerParams(vmem_limit_bytes=8 * MIB),
        name="deliver_rows",
    )(*outs)


def shards(query_rows, key_rows, value_rows, out_grad, random_ids, global_ids):
    kv, qg, wst = gather(query_rows, key_rows, value_rows, out_grad)
    st, pair_list = stats(random_ids.T, global_ids, kv, qg, wst)
    dkv, oq, rows = terms(pair_list, global_ids, share(st), kv, qg)
    return deliver(reduce(kv, qg, rows, dkv, oq))


def solution(mesh):
    rows = P(("seq", "head"), None)
    return jax.shard_map(
        shards,
        mesh=mesh,
        in_specs=(rows, rows, rows, rows, P(), P()),
        out_specs=(rows,) * 4,
        check_vma=False,
    )
```

```python
import functools

import jax
import jax.numpy as jnp
from jax import lax
from jax.experimental import pallas as pl
from jax.experimental.pallas import tpu as pltpu
from jax.sharding import PartitionSpec as P

HD = 128
BLOCK = 64
QB = 8
NH = 8
NY = 4
NZ = 16
COL = NZ * QB
PLANE = NY * QB
SCALE = HD ** (-0.5)
FLOOR = -1e30
UNROLL = 4
TILES = PLANE // 4
TRASH = PLANE * 4 * COL
LIST = PLANE * 4 + 8
MESH = pl.DeviceIdType.MESH
NT = (((1,), (1,)), ((), ()))
TN = (((0,), (0,)), ((), ()))
NN = (((1,), (0,)), ((), ()))
BF = jnp.bfloat16
F32 = jnp.float32
MIB = 1024 * 1024


def rcopy(src, dst, send, recv, seq, head):
    return pltpu.make_async_remote_copy(
        src_ref=src,
        dst_ref=dst,
        send_sem=send,
        recv_sem=recv,
        device_id=(seq, head),
        device_id_type=MESH,
    )


def place():
    seq = lax.axis_index("seq")
    head = lax.axis_index("head")
    return seq, head, seq // NZ, seq % NZ


def greet(peers):
    barrier = pltpu.get_barrier_semaphore()
    for seq, head in peers:
        pl.semaphore_signal(barrier, inc=1, device_id=(seq, head), device_id_type=MESH)
    pl.semaphore_wait(barrier, len(peers))


def head_peers(seq, head):
    return [(seq, (head + d) % NH) for d in range(1, NH)]


def row_peers(y, z, head):
    return [(((y + d) % NY) * NZ + z, head) for d in range(1, NY)]


def ring_peers(y, z, head):
    return [(y * NZ + (z + 1) % NZ, head), (y * NZ + (z + NZ - 1) % NZ, head)]


def window_tile(c, kv_ref, qg_ref, y, z):
    lo, hi = max(2 * c - 1, 0), min(2 * c + 3, QB)
    shape = ((hi - lo) * BLOCK, HD)
    keys = kv_ref[z, 0, lo:hi].reshape(shape)
    values = kv_ref[z, 1, lo:hi].reshape(shape)
    queries = qg_ref[y, 0, 2 * c : 2 * c + 2].reshape(2 * BLOCK, HD)
    grads = qg_ref[y, 1, 2 * c : 2 * c + 2].reshape(2 * BLOCK, HD)
    scores = lax.dot_general(keys, queries, NT, preferred_element_type=F32) * SCALE
    dprobs = lax.dot_general(values, grads, NT, preferred_element_type=F32)
    gap = (lo - 2 * c) + (lax.broadcasted_iota(jnp.int32, shape, 0) >> 6)
    gap = gap - (lax.broadcasted_iota(jnp.int32, shape, 1) >> 6)
    near = (gap >= -1) & (gap <= 1)
    return lo, hi, keys, values, queries, grads, jnp.where(near, scores, FLOOR), dprobs


def gather_kernel(
    q_ref, k_ref, v_ref, g_ref, kv_ref, qg_ref, wst_ref, own, hs, hr, zs, zr, ys, yr
):
    seq, head, y, z = place()
    ins = (k_ref, v_ref, q_ref, g_ref)

    def home(a, sender):
        return kv_ref.at[z, a, sender] if a < 2 else qg_ref.at[y, a - 2, sender]

    def cols(h):
        return pl.ds(pl.multiple_of(h * HD, HD), HD)

    def keep(a):
        return pltpu.make_async_copy(ins[a].at[:, cols(head)], home(a, head), own.at[a])

    def give(a, d, sender, target):
        return rcopy(
            ins[a].at[:, cols(target)],
            home(a, sender),
            hs.at[a, d - 1],
            hr.at[a, d - 1],
            seq,
            target,
        )

    def give_all(a):
        for d in range(1, NH):
            give(a, d, head, (head + d) % NH).start()

    def take_all(a):
        for d in range(1, NH):
            give(a, d, (head + NH - d) % NH, (head + d) % NH).wait_recv()
        keep(a).wait()

    for a in range(4):
        keep(a).start()
    greet(head_peers(seq, head) + ring_peers(y, z, head) + row_peers(y, z, head))
    give_all(0)
    give_all(1)

    right = y * NZ + (z + 1) % NZ
    left = y * NZ + (z + NZ - 1) % NZ

    def hop(way, step, piece, back):
        if way == 0:
            chunk = (z + 2 * NZ - step - back) % NZ
            target = right
        else:
            chunk = (z + step + back) % NZ
            target = left
        ref = kv_ref.at[chunk, piece]
        return rcopy(ref, ref, zs.at[way, step, piece], zr.at[way, step, piece], target, head)

    half = NZ // 2
    hops = [
        (way, step, piece)
        for step in range(half)
        for piece in range(2)
        for way in range(2)
        if step < half - 1 or piece == way
    ]
    for piece in range(2):
        take_all(piece)
        for way in range(2):
            hop(way, 0, piece, 0).start()
    give_all(2)
    give_all(3)

    def row(d, sender, target):
        ref = qg_ref.at[sender]
        return rcopy(ref, ref, ys.at[d - 1], yr.at[d - 1], target * NZ + z, head)

    wst_ref[0] = jnp.full((PLANE // 2, HD), FLOOR, F32)
    wst_ref[1] = jnp.zeros((PLANE // 2, HD), F32)
    wst_ref[2] = jnp.zeros((PLANE // 2, HD), F32)

    def window(c):
        _, _, _, _, _, _, scores, dprobs = window_tile(c, kv_ref, qg_ref, y, z)
        top = jnp.max(scores, axis=0, keepdims=True)
        expo = jnp.exp(scores - top)
        at = pl.ds(y * (QB // 2) + c, 1)
        wst_ref[0, at, :] = top
        wst_ref[1, at, :] = jnp.sum(expo, axis=0, keepdims=True)
        wst_ref[2, at, :] = jnp.sum(expo * dprobs, axis=0, keepdims=True)

    for way, step, piece in hops:
        if step == 0:
            continue
        hop(way, step - 1, piece, 1).wait_recv()
        hop(way, step, piece, 0).start()
        if piece == 1 and way == 1:
            if step == 1:
                take_all(2)
                take_all(3)
                for d in range(1, NY):
                    row(d, y, (y + d) % NY).start()
            elif step <= 5:
                window(step - 2)
    for d in range(1, NY):
        row(d, (y + NY - d) % NY, (y + d) % NY).wait_recv()
    for way, step, piece in hops:
        if step == half - 1 or (step == half - 2 and piece != way):
            hop(way, step, piece, 1).wait_recv()
    for a in range(4):
        for d in range(1, NH):
            give(a, d, head, (head + d) % NH).wait_send()
    for d in range(1, NY):
        row(d, y, (y + d) % NY).wait_send()
    for way, step, piece in hops:
        hop(way, step, piece, 0).wait_send()


def vmem():
    return pl.BlockSpec(memory_space=pltpu.VMEM)


def smem():
    return pl.BlockSpec(memory_space=pltpu.SMEM)


def hbm():
    return pl.BlockSpec(memory_space=pltpu.HBM)


def gather(q, k, v, g):
    dma = pltpu.SemaphoreType.DMA
    return pl.pallas_call(
        gather_kernel,
        out_shape=(
            jax.ShapeDtypeStruct((NZ, 2, QB, BLOCK, HD), BF),
            jax.ShapeDtypeStruct((NY, 2, QB, BLOCK, HD), BF),
            jax.ShapeDtypeStruct((3, PLANE // 2, HD), F32),
        ),
        in_specs=[hbm()] * 4,
        out_specs=(vmem(),) * 3,
        scratch_shapes=[
            dma((4,)),
            dma((4, NH - 1)),
            dma((4, NH - 1)),
            dma((2, NZ // 2, 2)),
            dma((2, NZ // 2, 2)),
            dma((NY - 1,)),
            dma((NY - 1,)),
        ],
        compiler_params=pltpu.CompilerParams(
            collective_id=0, has_side_effects=True, vmem_limit_bytes=24 * MIB
        ),
        name="gather_rows",
    )(q, k, v, g)


def stats_kernel(ids, gids, kv_ref, qg_ref, wst_ref, st_ref, list_ref, one, full):
    y = lax.axis_index("seq") // NZ
    z = lax.axis_index("seq") % NZ
    base = y * COL
    one[0] = jnp.full((2, 5, PLANE // 2, HD), FLOOR, F32)
    full[0] = jnp.full((3, PLANE // 2, HD), FLOOR, F32)
    for k in range(1, 3):
        one[k] = jnp.zeros((2, 5, PLANE // 2, HD), F32)
        full[k] = jnp.zeros((3, PLANE // 2, HD), F32)
    for k in range(3):
        full[k, 2] = wst_ref[k]

    def note(count, i, slot, block):
        rel = block - base
        good = (rel >= 0) & (rel < COL)
        list_ref[count] = (i * 4 + slot) * COL + rel
        return count + good.astype(jnp.int32)

    count = jnp.int32(0)
    for g in range(NY):
        first = (g * NZ + z) * QB
        count = note(count, g * QB, 3, first - 1)
        count = note(count, g * QB + QB - 1, 3, first + QB)

        def scan(b, count, g=g, first=first):
            for r in range(3):
                count = note(count, g * QB + b, r, ids[r, first + b])
            return count

        count = lax.fori_loop(0, QB, scan, count, unroll=4)
    for u in range(UNROLL):
        list_ref[count + u] = jnp.int32(TRASH)
    rounds = (count + UNROLL - 1) >> 2
    list_ref[LIST - 1] = rounds

    def pairs(t, carry):
        done = []
        for u in range(UNROLL):
            code = list_ref[t * UNROLL + u]
            pair = code >> 7
            rel = code & (COL - 1)
            i = jnp.minimum(pair >> 2, PLANE - 1)
            keys = kv_ref[rel >> 3, 0, rel & 7]
            values = kv_ref[rel >> 3, 1, rel & 7]
            queries = qg_ref[i >> 3, 0, i & 7]
            grads = qg_ref[i >> 3, 1, i & 7]
            scores = lax.dot_general(keys, queries, NT, preferred_element_type=F32) * SCALE
            dprobs = lax.dot_general(values, grads, NT, preferred_element_type=F32)
            top = jnp.max(scores, axis=0, keepdims=True)
            expo = jnp.exp(scores - top)
            total = jnp.sum(expo, axis=0, keepdims=True)
            delta = jnp.sum(expo * dprobs, axis=0, keepdims=True)
            slot = jnp.where(code < TRASH, pair & 3, 4)
            done.append((i, slot, (top, total, delta)))
        for i, slot, found in done:
            for k in range(3):
                one[k, i & 1, slot, pl.ds(i >> 1, 1), 0:BLOCK] = found[k]
        return carry

    lax.fori_loop(0, rounds, pairs, 0)

    for n in range(2):
        rel = gids[n] - base

        @pl.when((rel >= 0) & (rel < COL))
        def _(n=n, rel=rel):
            keys = kv_ref[rel >> 3, 0, rel & 7]
            values = kv_ref[rel >> 3, 1, rel & 7]
            for t in range(TILES):
                queries, grads = tile_rows(qg_ref, t)
                scores = lax.dot_general(keys, queries, NT, preferred_element_type=F32) * SCALE
                dprobs = lax.dot_general(values, grads, NT, preferred_element_type=F32)
                top = jnp.max(scores, axis=0, keepdims=True)
                expo = jnp.exp(scores - top)
                total = jnp.sum(expo, axis=0, keepdims=True)
                delta = jnp.sum(expo * dprobs, axis=0, keepdims=True)
                for k, found in enumerate((top, total, delta)):
                    for p in range(2):
                        full[k, n, 2 * t + p : 2 * t + p + 1] = found[:, p * HD : (p + 1) * HD]

    def parts(k):
        even = one[k, 0, 0:4]
        odd = pltpu.roll(one[k, 1, 0:4].reshape(2 * PLANE, HD), BLOCK, 1)
        return jnp.concatenate([even, odd.reshape(4, PLANE // 2, HD), full[k]], axis=0)

    tops = parts(0)
    top = jnp.max(tops, axis=0)
    factor = jnp.exp(tops - top[None])
    st_ref[0] = top
    st_ref[1] = jnp.sum(parts(1) * factor, axis=0)
    st_ref[2] = jnp.sum(parts(2) * factor, axis=0)


def tile_rows(qg_ref, t):
    at = slice((t % 2) * 4, (t % 2) * 4 + 4)
    queries = qg_ref[t // 2, 0, at].reshape(4 * BLOCK, HD)
    grads = qg_ref[t // 2, 1, at].reshape(4 * BLOCK, HD)
    return queries, grads


def stats(ids, gids, kv, qg, wst):
    return pl.pallas_call(
        stats_kernel,
        out_shape=(
            jax.ShapeDtypeStruct((3, PLANE // 2, HD), F32),
            jax.ShapeDtypeStruct((LIST,), jnp.int32),
        ),
        in_specs=[smem(), smem(), vmem(), vmem(), vmem()],
        out_specs=(vmem(), smem()),
        scratch_shapes=[
            pltpu.VMEM((3, 2, 5, PLANE // 2, HD), F32),
            pltpu.VMEM((3, 3, PLANE // 2, HD), F32),
        ],
        compiler_params=pltpu.CompilerParams(vmem_limit_bytes=24 * MIB),
        name="pair_stats",
    )(ids, gids, kv, qg, wst)


def share_kernel(st_ref, all_ref, send, recv):
    seq, head, y, z = place()
    greet(row_peers(y, z, head))

    def row(d, sender, target):
        return rcopy(
            st_ref, all_ref.at[sender], send.at[d - 1], recv.at[d - 1], target * NZ + z, head
        )

    for d in range(1, NY):
        row(d, y, (y + d) % NY).start()
    all_ref[y] = st_ref[...]
    for d in range(1, NY):
        row(d, (y + NY - d) % NY, (y + d) % NY).wait_recv()
    for d in range(1, NY):
        row(d, y, (y + d) % NY).wait_send()


def share(st):
    dma = pltpu.SemaphoreType.DMA
    return pl.pallas_call(
        share_kernel,
        out_shape=jax.ShapeDtypeStruct((NY, 3, PLANE // 2, HD), F32),
        in_specs=[vmem()],
        out_specs=vmem(),
        scratch_shapes=[dma((NY - 1,)), dma((NY - 1,))],
        compiler_params=pltpu.CompilerParams(
            collective_id=1, has_side_effects=True, vmem_limit_bytes=8 * MIB
        ),
        name="share_stats",
    )(st)


def terms_kernel(
    list_ref, gids, all_ref, kv_ref, qg_ref, dkv_ref, shifted
):
    base = (lax.axis_index("seq") // NZ) * COL
    tops = all_ref[:, 0]
    top = jnp.max(tops, axis=0)
    factor = jnp.exp(tops - top[None])
    inverse = 1.0 / jnp.sum(all_ref[:, 1] * factor, axis=0)
    delta = jnp.sum(all_ref[:, 2] * factor, axis=0) * inverse
    for k, value in enumerate((top, inverse, delta)):
        shifted[k, 0] = value
        shifted[k, 1] = pltpu.roll(value, BLOCK, 1)

    def clear_kv(b, carry):
        dkv_ref[b] = jnp.zeros((2, QB, BLOCK, HD), BF)
        return carry

    lax.fori_loop(0, NZ, clear_kv, 0)
    rounds = list_ref[LIST - 1]

    def add_kv(rel, dk, dv):
        for a, term in enumerate((dk, dv)):
            old = dkv_ref[rel >> 3, a, rel & 7].astype(F32)
            dkv_ref[rel >> 3, a, rel & 7] = (old + term).astype(BF)

    def pairs(t, carry):
        done = []
        for u in range(UNROLL):
            code = list_ref[t * UNROLL + u]
            pair = code >> 7
            rel = code & (COL - 1)
            i = jnp.minimum(pair >> 2, PLANE - 1)
            at = pl.ds(i >> 1, 1)
            keys = kv_ref[rel >> 3, 0, rel & 7]
            values = kv_ref[rel >> 3, 1, rel & 7]
            queries = qg_ref[i >> 3, 0, i & 7]
            grads = qg_ref[i >> 3, 1, i & 7]
            scores = lax.dot_general(keys, queries, NT, preferred_element_type=F32) * SCALE
            dprobs = lax.dot_general(values, grads, NT, preferred_element_type=F32)
            weights = jnp.exp(scores - shifted[0, i & 1, at, 0:BLOCK])
            weights = weights * shifted[1, i & 1, at, 0:BLOCK]
            weights = jnp.where(code < TRASH, weights, 0.0)
            probs = weights.astype(BF)
            dscores = (weights * (dprobs - shifted[2, i & 1, at, 0:BLOCK])).astype(BF)
            dv = lax.dot_general(probs, grads, NN, preferred_element_type=F32)
            dk = lax.dot_general(dscores, queries, NN, preferred_element_type=F32) * SCALE
            done.append((rel, dk, dv))
        for rel, dk, dv in done:
            add_kv(rel, dk, dv)
        return carry

    lax.fori_loop(0, rounds, pairs, 0)

    for n in range(2):
        rel = gids[n] - base

        @pl.when((rel >= 0) & (rel < COL))
        def _(rel=rel):
            keys = kv_ref[rel >> 3, 0, rel & 7]
            values = kv_ref[rel >> 3, 1, rel & 7]
            dk = jnp.zeros((BLOCK, HD), F32)
            dv = jnp.zeros((BLOCK, HD), F32)
            for t in range(TILES):
                queries, grads = tile_rows(qg_ref, t)

                def wide(k, t=t):
                    pair = [shifted[k, 0, 2 * t + p : 2 * t + p + 1] for p in range(2)]
                    return jnp.concatenate(pair, axis=1)

                scores = lax.dot_general(keys, queries, NT, preferred_element_type=F32) * SCALE
                dprobs = lax.dot_general(values, grads, NT, preferred_element_type=F32)
                weights = jnp.exp(scores - wide(0)) * wide(1)
                probs = weights.astype(BF)
                dscores = (weights * (dprobs - wide(2))).astype(BF)
                dv = dv + lax.dot_general(probs, grads, NN, preferred_element_type=F32)
                dk = dk + lax.dot_general(dscores, queries, NN, preferred_element_type=F32) * SCALE
            add_kv(rel, dk, dv)


def terms(pair_list, gids, all_stats, kv, qg):
    return pl.pallas_call(
        terms_kernel,
        out_shape=(
            jax.ShapeDtypeStruct((NZ, 2, QB, BLOCK, HD), BF),
            jax.ShapeDtypeStruct((3, 2, PLANE // 2, HD), F32),
        ),
        in_specs=[smem(), smem(), vmem(), vmem(), vmem()],
        out_specs=(vmem(),) * 2,
        compiler_params=pltpu.CompilerParams(vmem_limit_bytes=32 * MIB),
        name="pair_terms",
    )(pair_list, gids, all_stats, kv, qg)


def reduce_kernel(
    ids,
    gids,
    kv_ref,
    qg_ref,
    rows_ref,
    dkv_ref,
    o_ref,
    dq_ref,
    dk_ref,
    dv_ref,
    rb,
    ob,
    yb,
    pack,
    near_kv,
    near_oq,
    hs,
    hr,
    zs,
    zr,
    ys,
    yr,
):
    seq, head, y, z = place()
    greet(head_peers(seq, head) + ring_peers(y, z, head) + row_peers(y, z, head))
    right = y * NZ + (z + 1) % NZ
    left = y * NZ + (z + NZ - 1) % NZ
    half = NZ // 2
    base = y * COL
    outs = (o_ref, dq_ref, dk_ref, dv_ref)

    def chunk_of(way, step):
        if way == 0:
            return (z + half - step) % NZ
        return (z + half + step) % NZ

    def hop(way, step, piece):
        if step == 0 or (step == 1 and piece != way):
            src = dkv_ref.at[chunk_of(way, step), piece]
        else:
            src = rb.at[way, step - 1, piece]
        target = right if way == 0 else left
        return rcopy(
            src,
            rb.at[way, step, piece],
            zs.at[way, step, piece],
            zr.at[way, step, piece],
            target,
            head,
        )

    def row(d, target):
        return rcopy(
            ob.at[d - 1], yb.at[d - 1], ys.at[d - 1], yr.at[d - 1], target * NZ + z, head
        )

    def scatter(a, d, sender, target):
        cols = pl.ds(pl.multiple_of(sender * HD, HD), HD)
        return rcopy(
            pack.at[a, target], outs[a].at[:, cols], hs.at[a, d - 1], hr.at[a, d - 1], seq, target
        )

    def send_heads(a):
        for d in range(1, NH):
            scatter(a, d, head, (head + d) % NH).start()
        cols = pl.ds(pl.multiple_of(head * HD, HD), HD)
        outs[a][:, cols] = pack[a, head]

    def far(d, b):
        group = (y + d) % NY
        first = (group * NZ + z) * QB
        edge = jnp.where(b == 0, first - 1, jnp.where(b == QB - 1, first + QB, -1))
        blocks = [ids[r, first + b] for r in range(3)] + [gids[0], gids[1], edge]
        at = pl.ds(group * (QB // 2) + (b >> 1), 1)
        top = rows_ref[0, b & 1, at, 0:BLOCK]
        inverse = rows_ref[1, b & 1, at, 0:BLOCK]
        delta = rows_ref[2, b & 1, at, 0:BLOCK]
        rels = [block - base for block in blocks]
        live = [(rel >= 0) & (rel < COL) for rel in rels]
        rels = [jnp.clip(rel, 0, COL - 1) for rel in rels]
        keys = jnp.concatenate([kv_ref[rel >> 3, 0, rel & 7] for rel in rels], axis=0)
        values = jnp.concatenate([kv_ref[rel >> 3, 1, rel & 7] for rel in rels], axis=0)
        scores = lax.dot_general(keys, qg_ref[group, 0, b], NT, preferred_element_type=F32)
        dprobs = lax.dot_general(values, qg_ref[group, 1, b], NT, preferred_element_type=F32)
        weights = jnp.exp(scores * SCALE - top) * inverse
        weights = jnp.concatenate(
            [
                jnp.where(good, weights[n * BLOCK : (n + 1) * BLOCK], 0.0)
                for n, good in enumerate(live)
            ],
            axis=0,
        )
        probs = weights.astype(BF)
        dscores = (weights * (dprobs - delta)).astype(BF)
        out = lax.dot_general(probs, values, TN, preferred_element_type=F32)
        dq = lax.dot_general(dscores, keys, TN, preferred_element_type=F32) * SCALE
        if d < NY:
            ob[d - 1, 0, b] = out.astype(BF)
            ob[d - 1, 1, b] = dq.astype(BF)
        else:
            near_oq[0, b] = out
            near_oq[1, b] = dq

    def far_some(start, count):
        d = start // QB + 1

        def one(b, carry):
            far(d, b)
            return carry

        lax.fori_loop(start % QB, start % QB + count, one, 0, unroll=True)
        if d < NY and start % QB + count == QB:
            row(d, (y + d) % NY).start()

    def window(c):
        lo, hi, keys, values, queries, grads, scores, dprobs = window_tile(c, kv_ref, qg_ref, y, z)
        at = pl.ds(y * (QB // 2) + c, 1)
        weights = jnp.exp(scores - rows_ref[0, 0, at, :]) * rows_ref[1, 0, at, :]
        probs = weights.astype(BF)
        dscores = (weights * (dprobs - rows_ref[2, 0, at, :])).astype(BF)
        dv = lax.dot_general(probs, grads, NN, preferred_element_type=F32)
        dk = lax.dot_general(dscores, queries, NN, preferred_element_type=F32) * SCALE
        out = lax.dot_general(probs, values, TN, preferred_element_type=F32)
        dq = lax.dot_general(dscores, keys, TN, preferred_element_type=F32) * SCALE
        near_kv[0, lo:hi] += dk.reshape(hi - lo, BLOCK, HD)
        near_kv[1, lo:hi] += dv.reshape(hi - lo, BLOCK, HD)
        near_oq[0, 2 * c : 2 * c + 2] += out.reshape(2, BLOCK, HD)
        near_oq[1, 2 * c : 2 * c + 2] += dq.reshape(2, BLOCK, HD)

    def total():
        for d in range(1, NY):
            row(d, (y + d) % NY).wait_recv()

        def add(b, carry):
            for a in range(2):
                acc = near_oq[a, b]
                for d in range(NY - 1):
                    acc = acc + yb[d, a, b].astype(F32)
                pack[a, b] = acc.astype(BF)
            return carry

        lax.fori_loop(0, QB, add, 0)
        send_heads(0)
        send_heads(1)

    jobs = [functools.partial(far_some, n, 2) for n in range(6, NY * QB, 2)]
    for c in range(QB // 2):
        jobs += [functools.partial(window, c)]
    jobs += [lambda: None] * 2 + [total]

    hop(0, 0, 0).start()
    hop(1, 0, 1).start()
    for way, piece in ((0, 1), (1, 0)):
        hop(way, 1, piece).start()
    near_kv[...] = jnp.zeros((2, QB, BLOCK, HD), F32)
    for n in range(0, 6, 2):
        far_some(n, 2)

    for step in range(1, half):
        for piece in range(2):
            for way in range(2):
                if step == 1 and piece != way:
                    continue
                hop(way, step - 1, piece).wait_recv()
                chunk = chunk_of(way, step)

                def add(b, carry, way=way, step=step, piece=piece, chunk=chunk):
                    mine = dkv_ref[chunk, piece, b].astype(F32)
                    rb[way, step - 1, piece, b] = (
                        rb[way, step - 1, piece, b].astype(F32) + mine
                    ).astype(BF)
                    return carry

                lax.fori_loop(0, QB, add, 0)
                hop(way, step, piece).start()
                if jobs:
                    jobs.pop(0)()
    for job in jobs:
        job()

    for piece in range(2):
        for way in range(2):
            hop(way, half - 1, piece).wait_recv()

        def last(b, carry, piece=piece):
            acc = near_kv[piece, b] + dkv_ref[z, piece, b].astype(F32)
            acc = acc + rb[0, half - 1, piece, b].astype(F32)
            acc = acc + rb[1, half - 1, piece, b].astype(F32)
            pack[2 + piece, b] = acc.astype(BF)
            return carry

        lax.fori_loop(0, QB, last, 0)
        send_heads(2 + piece)

    for a in range(4):
        for d in range(1, NH):
            scatter(a, d, (head + NH - d) % NH, (head + d) % NH).wait_recv()
    for a in range(4):
        for d in range(1, NH):
            scatter(a, d, head, (head + d) % NH).wait_send()
    for d in range(1, NY):
        row(d, (y + d) % NY).wait_send()
    for step in range(half):
        for piece in range(2):
            for way in range(2):
                if step > 0 or piece == way:
                    hop(way, step, piece).wait_send()


def reduce(ids, gids, kv, qg, rows, dkv):
    dma = pltpu.SemaphoreType.DMA
    out = jax.ShapeDtypeStruct((BLOCK, NH * HD), BF)
    return pl.pallas_call(
        reduce_kernel,
        out_shape=(out,) * 4,
        in_specs=[smem()] * 2 + [vmem()] * 4,
        out_specs=(vmem(),) * 4,
        scratch_shapes=[
            pltpu.VMEM((2, NZ // 2, 2, QB, BLOCK, HD), BF),
            pltpu.VMEM((NY - 1, 2, QB, BLOCK, HD), BF),
            pltpu.VMEM((NY - 1, 2, QB, BLOCK, HD), BF),
            pltpu.VMEM((4, NH, BLOCK, HD), BF),
            pltpu.VMEM((2, QB, BLOCK, HD), F32),
            pltpu.VMEM((2, QB, BLOCK, HD), F32),
            dma((4, NH - 1)),
            dma((4, NH - 1)),
            dma((2, NZ // 2, 2)),
            dma((2, NZ // 2, 2)),
            dma((NY - 1,)),
            dma((NY - 1,)),
        ],
        compiler_params=pltpu.CompilerParams(
            collective_id=2, has_side_effects=True, vmem_limit_bytes=32 * MIB
        ),
        name="reduce_rows",
    )(ids, gids, kv, qg, rows, dkv)


def deliver_kernel(*refs):
    sems = refs[8]
    copies = [pltpu.make_async_copy(refs[a], refs[4 + a], sems.at[a]) for a in range(4)]
    for copy in copies:
        copy.start()
    for copy in copies:
        copy.wait()


def deliver(outs):
    return pl.pallas_call(
        deliver_kernel,
        out_shape=tuple(jax.ShapeDtypeStruct(o.shape, o.dtype) for o in outs),
        in_specs=[vmem()] * 4,
        out_specs=(hbm(),) * 4,
        scratch_shapes=[pltpu.SemaphoreType.DMA((4,))],
        compiler_params=pltpu.CompilerParams(vmem_limit_bytes=8 * MIB),
        name="deliver_rows",
    )(*outs)


def shards(query_rows, key_rows, value_rows, out_grad, random_ids, global_ids):
    rows = (query_rows, key_rows, value_rows, out_grad)
    kv, qg, wst = gather(*(pltpu.with_memory_space_constraint(r, pltpu.HBM) for r in rows))
    ids = pltpu.with_memory_space_constraint(random_ids.T, pltpu.HBM)
    global_ids = pltpu.with_memory_space_constraint(global_ids, pltpu.HBM)
    st, pair_list = stats(ids, global_ids, kv, qg, wst)
    dkv, row_stats = terms(pair_list, global_ids, share(st), kv, qg)
    return deliver(reduce(ids, global_ids, kv, qg, row_stats, dkv))


def solution(mesh):
    rows = P(("seq", "head"), None)
    return jax.shard_map(
        shards,
        mesh=mesh,
        in_specs=(rows, rows, rows, rows, P(), P()),
        out_specs=(rows,) * 4,
        check_vma=False,
    )
```

```python
import functools

import jax
import jax.numpy as jnp
from jax import lax
from jax.experimental import pallas as pl
from jax.experimental.pallas import tpu as pltpu
from jax.sharding import PartitionSpec as P

HD = 128
BLOCK = 64
QB = 8
NH = 8
NY = 4
NZ = 16
COL = NZ * QB
PLANE = NY * QB
SCALE = HD ** (-0.5)
FLOOR = -1e30
UNROLL = 8
TURNS = (4, 3, 5, 2, 6, 1, 7, 0)
TILES = PLANE // 4
TRASH = PLANE * 4 * COL
LIST = PLANE * 4 + 16
PAIRS = PLANE * 3 + 2 * NY + 8
MESH = pl.DeviceIdType.MESH
NT = (((1,), (1,)), ((), ()))
TN = (((0,), (0,)), ((), ()))
NN = (((1,), (0,)), ((), ()))
BF = jnp.bfloat16
F32 = jnp.float32
MIB = 1024 * 1024


def rcopy(src, dst, send, recv, seq, head):
    return pltpu.make_async_remote_copy(
        src_ref=src,
        dst_ref=dst,
        send_sem=send,
        recv_sem=recv,
        device_id=(seq, head),
        device_id_type=MESH,
    )


def place():
    seq = lax.axis_index("seq")
    head = lax.axis_index("head")
    return seq, head, seq // NZ, seq % NZ


def greet(peers):
    barrier = pltpu.get_barrier_semaphore()
    for seq, head in peers:
        pl.semaphore_signal(barrier, inc=1, device_id=(seq, head), device_id_type=MESH)
    pl.semaphore_wait(barrier, len(peers))


def head_peers(seq, head):
    return [(seq, (head + d) % NH) for d in range(1, NH)]


def row_peers(y, z, head):
    return [(((y + d) % NY) * NZ + z, head) for d in range(1, NY)]


def window_tile(c, kv_ref, qg_ref, y, z):
    lo, hi = max(2 * c - 1, 0), min(2 * c + 3, QB)
    shape = ((hi - lo) * BLOCK, HD)
    keys = kv_ref[z, 0, lo:hi].reshape(shape)
    values = kv_ref[z, 1, lo:hi].reshape(shape)
    queries = qg_ref[y, 0, 2 * c : 2 * c + 2].reshape(2 * BLOCK, HD)
    grads = qg_ref[y, 1, 2 * c : 2 * c + 2].reshape(2 * BLOCK, HD)
    scores = lax.dot_general(keys, queries, NT, preferred_element_type=F32) * SCALE
    dprobs = lax.dot_general(values, grads, NT, preferred_element_type=F32)
    gap = (lo - 2 * c) + (lax.broadcasted_iota(jnp.int32, shape, 0) >> 6)
    gap = gap - (lax.broadcasted_iota(jnp.int32, shape, 1) >> 6)
    near = (gap >= -1) & (gap <= 1)
    return lo, hi, keys, values, queries, grads, jnp.where(near, scores, FLOOR), dprobs


def near_planes(y, z):
    return [(y * NZ + (z + d) % NZ, h) for d in (1, NZ - 1) for h in range(NH)]


def gather_kernel(
    q_ref, k_ref, v_ref, g_ref, kv_ref, qg_ref, wst_ref, own, hs, hr, fs, fr, zs, zr, ys, yr
):
    seq, head, y, z = place()
    ins = (k_ref, v_ref, q_ref, g_ref)

    def home(a, sender):
        return kv_ref.at[z, a, sender] if a < 2 else qg_ref.at[y, a - 2, sender]

    def cols(h):
        return pl.ds(pl.multiple_of(h * HD, HD), HD)

    def keep(a):
        return pltpu.make_async_copy(ins[a].at[:, cols(head)], home(a, head), own.at[a])

    def give(a, d, sender, target):
        return rcopy(
            ins[a].at[:, cols(target)],
            home(a, sender),
            hs.at[a, d - 1],
            hr.at[a, d - 1],
            seq,
            target,
        )

    def give_all(a):
        for d in range(1, NH):
            give(a, d, head, (head + d) % NH).start()

    def take_all(a):
        for d in range(1, NH):
            give(a, d, (head + NH - d) % NH, (head + d) % NH).wait_recv()
        keep(a).wait()

    for a in range(4):
        keep(a).start()
    greet(head_peers(seq, head) + near_planes(y, z) + row_peers(y, z, head))
    right = y * NZ + (z + 1) % NZ
    left = y * NZ + (z + NZ - 1) % NZ
    sides = (right, left)

    def first(way, piece, d):
        target = (head + d) % NH
        return rcopy(
            ins[piece].at[:, cols(target)],
            kv_ref.at[z, piece, head],
            fs.at[way, piece, d],
            fr.at[way, piece, d],
            sides[way],
            target,
        )

    def first_in(way, piece, d):
        sender = (head + NH - d) % NH
        chunk = (z + NZ - 1 + 2 * way) % NZ
        return rcopy(
            ins[piece].at[:, cols(head)],
            kv_ref.at[chunk, piece, sender],
            fs.at[way, piece, d],
            fr.at[way, piece, d],
            sides[way],
            sender,
        )

    def hop(way, step, piece, back):
        if way == 0:
            chunk = (z + 2 * NZ - step - back) % NZ
        else:
            chunk = (z + step + back) % NZ
        ref = kv_ref.at[chunk, piece]
        return rcopy(ref, ref, zs.at[way, step, piece], zr.at[way, step, piece], sides[way], head)

    half = NZ // 2
    hops = [
        (way, step, piece)
        for step in range(1, half)
        for piece in range(2)
        for way in range(2)
        if step < half - 1 or piece == way
    ]
    for piece in range(2):
        for d in TURNS:
            for way in range(2):
                first(way, piece, d).start()
    def row(d, sender, target):
        ref = qg_ref.at[sender]
        return rcopy(ref, ref, ys.at[d - 1], yr.at[d - 1], target * NZ + z, head)

    wst_ref[0] = jnp.full((PLANE // 2, HD), FLOOR, F32)
    wst_ref[1] = jnp.zeros((PLANE // 2, HD), F32)
    wst_ref[2] = jnp.zeros((PLANE // 2, HD), F32)

    def window(c):
        _, _, _, _, _, _, scores, dprobs = window_tile(c, kv_ref, qg_ref, y, z)
        top = jnp.max(scores, axis=0, keepdims=True)
        expo = jnp.exp(scores - top)
        at = pl.ds(y * (QB // 2) + c, 1)
        wst_ref[0, at, :] = top
        wst_ref[1, at, :] = jnp.sum(expo, axis=0, keepdims=True)
        wst_ref[2, at, :] = jnp.sum(expo * dprobs, axis=0, keepdims=True)

    for way, step, piece in hops:
        if step == 1:
            for d in range(NH):
                first_in(way, piece, d).wait_recv()
        else:
            hop(way, step - 1, piece, 1).wait_recv()
        hop(way, step, piece, 0).start()
        if piece == 1 and way == 1:
            if step == 1:
                for a in (2, 3, 0, 1):
                    give_all(a)
            elif step == 3:
                for a in range(4):
                    take_all(a)
                for d in range(1, NY):
                    row(d, y, (y + d) % NY).start()
            elif step >= 4:
                window(step - 4)
    for d in range(1, NY):
        row(d, (y + NY - d) % NY, (y + d) % NY).wait_recv()
    for way, step, piece in hops:
        if step == half - 1 or (step == half - 2 and piece != way):
            hop(way, step, piece, 1).wait_recv()
    for a in range(4):
        for d in range(1, NH):
            give(a, d, head, (head + d) % NH).wait_send()
    for d in range(1, NY):
        row(d, y, (y + d) % NY).wait_send()
    for way in range(2):
        for piece in range(2):
            for d in range(NH):
                first(way, piece, d).wait_send()
    for way, step, piece in hops:
        hop(way, step, piece, 0).wait_send()


def vmem():
    return pl.BlockSpec(memory_space=pltpu.VMEM)


def smem():
    return pl.BlockSpec(memory_space=pltpu.SMEM)


def hbm():
    return pl.BlockSpec(memory_space=pltpu.HBM)


def gather(q, k, v, g):
    dma = pltpu.SemaphoreType.DMA
    return pl.pallas_call(
        gather_kernel,
        out_shape=(
            jax.ShapeDtypeStruct((NZ, 2, QB, BLOCK, HD), BF),
            jax.ShapeDtypeStruct((NY, 2, QB, BLOCK, HD), BF),
            jax.ShapeDtypeStruct((3, PLANE // 2, HD), F32),
        ),
        in_specs=[hbm()] * 4,
        out_specs=(vmem(),) * 3,
        scratch_shapes=[
            dma((4,)),
            dma((4, NH - 1)),
            dma((4, NH - 1)),
            dma((2, 2, NH)),
            dma((2, 2, NH)),
            dma((2, NZ // 2, 2)),
            dma((2, NZ // 2, 2)),
            dma((NY - 1,)),
            dma((NY - 1,)),
        ],
        compiler_params=pltpu.CompilerParams(
            collective_id=0, has_side_effects=True, vmem_limit_bytes=24 * MIB
        ),
        name="gather_rows",
    )(q, k, v, g)


def stats_kernel(
    ids, gids, kv_ref, qg_ref, wst_ref, st_ref, list_ref, one, expo_ref, dprob_ref, full
):
    y = lax.axis_index("seq") // NZ
    z = lax.axis_index("seq") % NZ
    base = y * COL
    one[0] = jnp.full((2, 5, PLANE // 2, HD), FLOOR, F32)
    full[0] = jnp.full((3, PLANE // 2, HD), FLOOR, F32)
    for k in range(1, 3):
        one[k] = jnp.zeros((2, 5, PLANE // 2, HD), F32)
        full[k] = jnp.zeros((3, PLANE // 2, HD), F32)
    for k in range(3):
        full[k, 2] = wst_ref[k]

    def note(count, i, slot, block):
        rel = block - base
        good = (rel >= 0) & (rel < COL)
        list_ref[count] = (i * 4 + slot) * COL + rel
        return count + good.astype(jnp.int32)

    count = jnp.int32(0)
    for g in range(NY):
        first = (g * NZ + z) * QB
        count = note(count, g * QB, 3, first - 1)
        count = note(count, g * QB + QB - 1, 3, first + QB)

        def scan(b, count, g=g, first=first):
            for r in range(3):
                count = note(count, g * QB + b, r, ids[r, first + b])
            return count

        count = lax.fori_loop(0, QB, scan, count, unroll=4)
    for u in range(UNROLL):
        list_ref[count + u] = jnp.int32(TRASH)
    rounds = (count + UNROLL - 1) >> 3
    list_ref[LIST - 1] = rounds

    def pairs(t, carry):
        done = []
        for u in range(UNROLL):
            code = list_ref[t * UNROLL + u]
            pair = code >> 7
            rel = code & (COL - 1)
            i = jnp.minimum(pair >> 2, PLANE - 1)
            keys = kv_ref[rel >> 3, 0, rel & 7]
            values = kv_ref[rel >> 3, 1, rel & 7]
            queries = qg_ref[i >> 3, 0, i & 7]
            grads = qg_ref[i >> 3, 1, i & 7]
            scores = lax.dot_general(keys, queries, NT, preferred_element_type=F32) * SCALE
            dprobs = lax.dot_general(values, grads, NT, preferred_element_type=F32)
            top = jnp.max(scores, axis=0, keepdims=True)
            expo = jnp.exp(scores - top)
            total = jnp.sum(expo, axis=0, keepdims=True)
            delta = jnp.sum(expo * dprobs, axis=0, keepdims=True)
            slot = jnp.where(code < TRASH, pair & 3, 4)
            done.append((i, slot, (top, total, delta), expo, dprobs))
        for u, (i, slot, found, expo, dprobs) in enumerate(done):
            expo_ref[t * UNROLL + u] = expo
            dprob_ref[t * UNROLL + u] = dprobs
            for k in range(3):
                one[k, i & 1, slot, pl.ds(i >> 1, 1), 0:BLOCK] = found[k]
        return carry

    lax.fori_loop(0, rounds, pairs, 0)

    for n in range(2):
        rel = gids[n] - base

        @pl.when((rel >= 0) & (rel < COL))
        def _(n=n, rel=rel):
            keys = kv_ref[rel >> 3, 0, rel & 7]
            values = kv_ref[rel >> 3, 1, rel & 7]
            for t in range(TILES):
                queries, grads = tile_rows(qg_ref, t)
                scores = lax.dot_general(keys, queries, NT, preferred_element_type=F32) * SCALE
                dprobs = lax.dot_general(values, grads, NT, preferred_element_type=F32)
                top = jnp.max(scores, axis=0, keepdims=True)
                expo = jnp.exp(scores - top)
                total = jnp.sum(expo, axis=0, keepdims=True)
                delta = jnp.sum(expo * dprobs, axis=0, keepdims=True)
                for k, found in enumerate((top, total, delta)):
                    for p in range(2):
                        full[k, n, 2 * t + p : 2 * t + p + 1] = found[:, p * HD : (p + 1) * HD]

    def parts(k):
        even = one[k, 0, 0:4]
        odd = pltpu.roll(one[k, 1, 0:4].reshape(2 * PLANE, HD), BLOCK, 1)
        return jnp.concatenate([even, odd.reshape(4, PLANE // 2, HD), full[k]], axis=0)

    tops = parts(0)
    top = jnp.max(tops, axis=0)
    factor = jnp.exp(tops - top[None])
    st_ref[0] = top
    st_ref[1] = jnp.sum(parts(1) * factor, axis=0)
    st_ref[2] = jnp.sum(parts(2) * factor, axis=0)


def tile_rows(qg_ref, t):
    at = slice((t % 2) * 4, (t % 2) * 4 + 4)
    queries = qg_ref[t // 2, 0, at].reshape(4 * BLOCK, HD)
    grads = qg_ref[t // 2, 1, at].reshape(4 * BLOCK, HD)
    return queries, grads


def stats(ids, gids, kv, qg, wst):
    return pl.pallas_call(
        stats_kernel,
        out_shape=(
            jax.ShapeDtypeStruct((3, PLANE // 2, HD), F32),
            jax.ShapeDtypeStruct((LIST,), jnp.int32),
            jax.ShapeDtypeStruct((3, 2, 5, PLANE // 2, HD), F32),
            jax.ShapeDtypeStruct((PAIRS, BLOCK, BLOCK), F32),
            jax.ShapeDtypeStruct((PAIRS, BLOCK, BLOCK), F32),
        ),
        in_specs=[smem(), smem(), vmem(), vmem(), vmem()],
        out_specs=(vmem(), smem(), vmem(), vmem(), vmem()),
        scratch_shapes=[
            pltpu.VMEM((3, 3, PLANE // 2, HD), F32),
        ],
        compiler_params=pltpu.CompilerParams(vmem_limit_bytes=24 * MIB),
        name="pair_stats",
    )(ids, gids, kv, qg, wst)


def share_kernel(st_ref, all_ref, send, recv):
    seq, head, y, z = place()
    greet(row_peers(y, z, head))

    def row(d, sender, target):
        return rcopy(
            st_ref, all_ref.at[sender], send.at[d - 1], recv.at[d - 1], target * NZ + z, head
        )

    for d in range(1, NY):
        row(d, y, (y + d) % NY).start()
    all_ref[y] = st_ref[...]
    for d in range(1, NY):
        row(d, (y + NY - d) % NY, (y + d) % NY).wait_recv()
    for d in range(1, NY):
        row(d, y, (y + d) % NY).wait_send()


def share(st):
    dma = pltpu.SemaphoreType.DMA
    return pl.pallas_call(
        share_kernel,
        out_shape=jax.ShapeDtypeStruct((NY, 3, PLANE // 2, HD), F32),
        in_specs=[vmem()],
        out_specs=vmem(),
        scratch_shapes=[dma((NY - 1,)), dma((NY - 1,))],
        compiler_params=pltpu.CompilerParams(
            collective_id=1, has_side_effects=True, vmem_limit_bytes=8 * MIB
        ),
        name="share_stats",
    )(st)


def terms_kernel(
    list_ref, gids, all_ref, kv_ref, qg_ref, one, expo_ref, dprob_ref, dkv_ref, shifted, scale_ref
):
    base = (lax.axis_index("seq") // NZ) * COL
    tops = all_ref[:, 0]
    top = jnp.max(tops, axis=0)
    factor = jnp.exp(tops - top[None])
    inverse = 1.0 / jnp.sum(all_ref[:, 1] * factor, axis=0)
    delta = jnp.sum(all_ref[:, 2] * factor, axis=0) * inverse
    for k, value in enumerate((top, inverse, delta)):
        shifted[k, 0] = value
        shifted[k, 1] = pltpu.roll(value, BLOCK, 1)

    for p in range(2):
        factor = jnp.exp(one[0, p, 0:4] - shifted[0, p][None]) * shifted[1, p][None]
        scale_ref[p, 0:4] = factor
        scale_ref[p, 4] = jnp.zeros((PLANE // 2, HD), F32)

    def clear_kv(b, carry):
        dkv_ref[b] = jnp.zeros((2, QB, BLOCK, HD), BF)
        return carry

    lax.fori_loop(0, NZ, clear_kv, 0)
    rounds = list_ref[LIST - 1]

    def add_kv(rel, dk, dv):
        for a, term in enumerate((dk, dv)):
            old = dkv_ref[rel >> 3, a, rel & 7].astype(F32)
            dkv_ref[rel >> 3, a, rel & 7] = (old + term).astype(BF)

    def pairs(t, carry):
        done = []
        for u in range(UNROLL):
            code = list_ref[t * UNROLL + u]
            pair = code >> 7
            rel = code & (COL - 1)
            i = jnp.minimum(pair >> 2, PLANE - 1)
            at = pl.ds(i >> 1, 1)
            slot = jnp.where(code < TRASH, pair & 3, 4)
            queries = qg_ref[i >> 3, 0, i & 7]
            grads = qg_ref[i >> 3, 1, i & 7]
            weights = expo_ref[t * UNROLL + u] * scale_ref[i & 1, slot, at, 0:BLOCK]
            dprobs = dprob_ref[t * UNROLL + u]
            probs = weights.astype(BF)
            dscores = (weights * (dprobs - shifted[2, i & 1, at, 0:BLOCK])).astype(BF)
            dv = lax.dot_general(probs, grads, NN, preferred_element_type=F32)
            dk = lax.dot_general(dscores, queries, NN, preferred_element_type=F32) * SCALE
            done.append((rel, dk, dv))
        for rel, dk, dv in done:
            add_kv(rel, dk, dv)
        return carry

    lax.fori_loop(0, rounds, pairs, 0)

    for n in range(2):
        rel = gids[n] - base

        @pl.when((rel >= 0) & (rel < COL))
        def _(rel=rel):
            keys = kv_ref[rel >> 3, 0, rel & 7]
            values = kv_ref[rel >> 3, 1, rel & 7]
            dk = jnp.zeros((BLOCK, HD), F32)
            dv = jnp.zeros((BLOCK, HD), F32)
            for t in range(TILES):
                queries, grads = tile_rows(qg_ref, t)

                def wide(k, t=t):
                    pair = [shifted[k, 0, 2 * t + p : 2 * t + p + 1] for p in range(2)]
                    return jnp.concatenate(pair, axis=1)

                scores = lax.dot_general(keys, queries, NT, preferred_element_type=F32) * SCALE
                dprobs = lax.dot_general(values, grads, NT, preferred_element_type=F32)
                weights = jnp.exp(scores - wide(0)) * wide(1)
                probs = weights.astype(BF)
                dscores = (weights * (dprobs - wide(2))).astype(BF)
                dv = dv + lax.dot_general(probs, grads, NN, preferred_element_type=F32)
                dk = dk + lax.dot_general(dscores, queries, NN, preferred_element_type=F32) * SCALE
            add_kv(rel, dk, dv)


def terms(pair_list, gids, all_stats, kv, qg, pairs):
    return pl.pallas_call(
        terms_kernel,
        out_shape=(
            jax.ShapeDtypeStruct((NZ, 2, QB, BLOCK, HD), BF),
            jax.ShapeDtypeStruct((3, 2, PLANE // 2, HD), F32),
        ),
        in_specs=[smem(), smem()] + [vmem()] * 6,
        out_specs=(vmem(),) * 2,
        scratch_shapes=[pltpu.VMEM((2, 5, PLANE // 2, HD), F32)],
        compiler_params=pltpu.CompilerParams(vmem_limit_bytes=32 * MIB),
        name="pair_terms",
    )(pair_list, gids, all_stats, kv, qg, *pairs)


def reduce_kernel(
    ids,
    gids,
    kv_ref,
    qg_ref,
    rows_ref,
    dkv_ref,
    o_ref,
    dq_ref,
    dk_ref,
    dv_ref,
    rb,
    ob,
    yb,
    pack,
    near_kv,
    near_oq,
    fin,
    hs,
    hr,
    fs,
    fr,
    zs,
    zr,
    ys,
    yr,
):
    seq, head, y, z = place()
    greet(head_peers(seq, head) + near_planes(y, z) + row_peers(y, z, head))
    right = y * NZ + (z + 1) % NZ
    left = y * NZ + (z + NZ - 1) % NZ
    half = NZ // 2
    base = y * COL
    outs = (o_ref, dq_ref, dk_ref, dv_ref)

    def chunk_of(way, step):
        if way == 0:
            return (z + half - step) % NZ
        return (z + half + step) % NZ

    def hop(way, step, piece):
        if step == 0 or (step == 1 and piece != way):
            src = dkv_ref.at[chunk_of(way, step), piece]
        else:
            src = rb.at[way, step - 1, piece]
        target = right if way == 0 else left
        return rcopy(
            src,
            rb.at[way, step, piece],
            zs.at[way, step, piece],
            zr.at[way, step, piece],
            target,
            head,
        )

    def row(d, target):
        return rcopy(
            ob.at[d - 1], yb.at[d - 1], ys.at[d - 1], yr.at[d - 1], target * NZ + z, head
        )

    def cols(h):
        return pl.ds(pl.multiple_of(h * HD, HD), HD)

    def scatter(a, d, sender, target):
        home = outs[a].at[:, cols(sender)] if a < 2 else fin.at[2, a - 2, sender]
        return rcopy(pack.at[a, target], home, hs.at[a, d - 1], hr.at[a, d - 1], seq, target)

    def send_heads(a):
        for d in range(1, NH):
            scatter(a, d, head, (head + d) % NH).start()
        if a < 2:
            outs[a][:, cols(head)] = pack[a, head]
        else:
            fin[2, a - 2, head] = pack[a, head]

    def final(way, piece, d, sender, target):
        return rcopy(
            rb.at[way, half - 2, piece, target],
            fin.at[way, piece, sender],
            fs.at[way, piece, d],
            fr.at[way, piece, d],
            right if way == 0 else left,
            target,
        )

    def far(d, b):
        group = (y + d) % NY
        first = (group * NZ + z) * QB
        edge = jnp.where(b == 0, first - 1, jnp.where(b == QB - 1, first + QB, -1))
        blocks = [ids[r, first + b] for r in range(3)] + [gids[0], gids[1], edge]
        at = pl.ds(group * (QB // 2) + (b >> 1), 1)
        top = rows_ref[0, b & 1, at, 0:BLOCK]
        inverse = rows_ref[1, b & 1, at, 0:BLOCK]
        delta = rows_ref[2, b & 1, at, 0:BLOCK]
        rels = [block - base for block in blocks]
        live = [(rel >= 0) & (rel < COL) for rel in rels]
        rels = [jnp.clip(rel, 0, COL - 1) for rel in rels]
        keys = jnp.concatenate([kv_ref[rel >> 3, 0, rel & 7] for rel in rels], axis=0)
        values = jnp.concatenate([kv_ref[rel >> 3, 1, rel & 7] for rel in rels], axis=0)
        scores = lax.dot_general(keys, qg_ref[group, 0, b], NT, preferred_element_type=F32)
        dprobs = lax.dot_general(values, qg_ref[group, 1, b], NT, preferred_element_type=F32)
        weights = jnp.exp(scores * SCALE - top) * inverse
        weights = jnp.concatenate(
            [
                jnp.where(good, weights[n * BLOCK : (n + 1) * BLOCK], 0.0)
                for n, good in enumerate(live)
            ],
            axis=0,
        )
        probs = weights.astype(BF)
        dscores = (weights * (dprobs - delta)).astype(BF)
        out = lax.dot_general(probs, values, TN, preferred_element_type=F32)
        dq = lax.dot_general(dscores, keys, TN, preferred_element_type=F32) * SCALE
        if d < NY:
            ob[d - 1, 0, b] = out.astype(BF)
            ob[d - 1, 1, b] = dq.astype(BF)
        else:
            near_oq[0, b] = out
            near_oq[1, b] = dq

    def far_some(start, count):
        d = start // QB + 1

        def one(b, carry):
            far(d, b)
            return carry

        lax.fori_loop(start % QB, start % QB + count, one, 0, unroll=True)
        if d < NY and start % QB + count == QB:
            row(d, (y + d) % NY).start()

    def window(c):
        lo, hi, keys, values, queries, grads, scores, dprobs = window_tile(c, kv_ref, qg_ref, y, z)
        at = pl.ds(y * (QB // 2) + c, 1)
        weights = jnp.exp(scores - rows_ref[0, 0, at, :]) * rows_ref[1, 0, at, :]
        probs = weights.astype(BF)
        dscores = (weights * (dprobs - rows_ref[2, 0, at, :])).astype(BF)
        dv = lax.dot_general(probs, grads, NN, preferred_element_type=F32)
        dk = lax.dot_general(dscores, queries, NN, preferred_element_type=F32) * SCALE
        out = lax.dot_general(probs, values, TN, preferred_element_type=F32)
        dq = lax.dot_general(dscores, keys, TN, preferred_element_type=F32) * SCALE
        near_kv[0, lo:hi] += dk.reshape(hi - lo, BLOCK, HD)
        near_kv[1, lo:hi] += dv.reshape(hi - lo, BLOCK, HD)
        near_oq[0, 2 * c : 2 * c + 2] += out.reshape(2, BLOCK, HD)
        near_oq[1, 2 * c : 2 * c + 2] += dq.reshape(2, BLOCK, HD)

    def total():
        for d in range(1, NY):
            row(d, (y + d) % NY).wait_recv()

        def add(b, carry):
            for a in range(2):
                acc = near_oq[a, b]
                for d in range(NY - 1):
                    acc = acc + yb[d, a, b].astype(F32)
                pack[a, b] = acc.astype(BF)
            return carry

        lax.fori_loop(0, QB, add, 0)
        send_heads(0)
        send_heads(1)

    def give_near():
        def add(b, carry):
            for piece in range(2):
                acc = near_kv[piece, b] + dkv_ref[z, piece, b].astype(F32)
                pack[2 + piece, b] = acc.astype(BF)
            return carry

        lax.fori_loop(0, QB, add, 0)
        send_heads(2)
        send_heads(3)

    jobs = [functools.partial(far_some, n, 2) for n in range(6, NY * QB, 2)]
    for c in range(QB // 2):
        jobs += [functools.partial(window, c)]
    jobs += [give_near, lambda: None, total]

    hop(0, 0, 0).start()
    hop(1, 0, 1).start()
    for way, piece in ((0, 1), (1, 0)):
        hop(way, 1, piece).start()
    near_kv[...] = jnp.zeros((2, QB, BLOCK, HD), F32)
    for n in range(0, 6, 2):
        far_some(n, 2)

    for step in range(1, half):
        for piece in range(2):
            for way in range(2):
                if step == 1 and piece != way:
                    continue
                hop(way, step - 1, piece).wait_recv()
                chunk = chunk_of(way, step)

                def add(b, carry, way=way, step=step, piece=piece, chunk=chunk):
                    mine = dkv_ref[chunk, piece, b].astype(F32)
                    rb[way, step - 1, piece, b] = (
                        rb[way, step - 1, piece, b].astype(F32) + mine
                    ).astype(BF)
                    return carry

                lax.fori_loop(0, QB, add, 0)
                if step < half - 1:
                    hop(way, step, piece).start()
                else:
                    for d in TURNS:
                        final(way, piece, d, head, (head + d) % NH).start()
                if jobs:
                    jobs.pop(0)()
    for job in jobs:
        job()

    for a in range(4):
        for d in range(1, NH):
            scatter(a, d, (head + NH - d) % NH, (head + d) % NH).wait_recv()
    for piece in range(2):
        for way in range(2):
            for d in range(NH):
                final(way, piece, d, (head + NH - d) % NH, (head + d) % NH).wait_recv()

        for h in range(NH):
            acc = fin[2, piece, h].astype(F32)
            acc = acc + fin[0, piece, h].astype(F32)
            acc = acc + fin[1, piece, h].astype(F32)
            outs[2 + piece][:, h * HD : (h + 1) * HD] = acc.astype(BF)

    for a in range(4):
        for d in range(1, NH):
            scatter(a, d, head, (head + d) % NH).wait_send()
    for d in range(1, NY):
        row(d, (y + d) % NY).wait_send()
    for way in range(2):
        for piece in range(2):
            for d in range(NH):
                final(way, piece, d, head, (head + d) % NH).wait_send()
    for step in range(half - 1):
        for piece in range(2):
            for way in range(2):
                if step > 0 or piece == way:
                    hop(way, step, piece).wait_send()


def reduce(ids, gids, kv, qg, rows, dkv):
    dma = pltpu.SemaphoreType.DMA
    out = jax.ShapeDtypeStruct((BLOCK, NH * HD), BF)
    return pl.pallas_call(
        reduce_kernel,
        out_shape=(out,) * 4,
        in_specs=[smem()] * 2 + [vmem()] * 4,
        out_specs=(vmem(),) * 4,
        scratch_shapes=[
            pltpu.VMEM((2, NZ // 2, 2, QB, BLOCK, HD), BF),
            pltpu.VMEM((NY - 1, 2, QB, BLOCK, HD), BF),
            pltpu.VMEM((NY - 1, 2, QB, BLOCK, HD), BF),
            pltpu.VMEM((4, NH, BLOCK, HD), BF),
            pltpu.VMEM((2, QB, BLOCK, HD), F32),
            pltpu.VMEM((2, QB, BLOCK, HD), F32),
            pltpu.VMEM((3, 2, NH, BLOCK, HD), BF),
            dma((4, NH - 1)),
            dma((4, NH - 1)),
            dma((2, 2, NH)),
            dma((2, 2, NH)),
            dma((2, NZ // 2, 2)),
            dma((2, NZ // 2, 2)),
            dma((NY - 1,)),
            dma((NY - 1,)),
        ],
        compiler_params=pltpu.CompilerParams(
            collective_id=2, has_side_effects=True, vmem_limit_bytes=32 * MIB
        ),
        name="reduce_rows",
    )(ids, gids, kv, qg, rows, dkv)


def deliver_kernel(*refs):
    sems = refs[8]
    copies = [pltpu.make_async_copy(refs[a], refs[4 + a], sems.at[a]) for a in range(4)]
    for copy in copies:
        copy.start()
    for copy in copies:
        copy.wait()


def deliver(outs):
    return pl.pallas_call(
        deliver_kernel,
        out_shape=tuple(jax.ShapeDtypeStruct(o.shape, o.dtype) for o in outs),
        in_specs=[vmem()] * 4,
        out_specs=(hbm(),) * 4,
        scratch_shapes=[pltpu.SemaphoreType.DMA((4,))],
        compiler_params=pltpu.CompilerParams(vmem_limit_bytes=8 * MIB),
        name="deliver_rows",
    )(*outs)


def shards(query_rows, key_rows, value_rows, out_grad, random_ids, global_ids):
    rows = (query_rows, key_rows, value_rows, out_grad)
    kv, qg, wst = gather(*(pltpu.with_memory_space_constraint(r, pltpu.HBM) for r in rows))
    ids = pltpu.with_memory_space_constraint(random_ids.T, pltpu.HBM)
    global_ids = pltpu.with_memory_space_constraint(global_ids, pltpu.HBM)
    st, pair_list, *pairs = stats(ids, global_ids, kv, qg, wst)
    dkv, row_stats = terms(pair_list, global_ids, share(st), kv, qg, pairs)
    return deliver(reduce(ids, global_ids, kv, qg, row_stats, dkv))


def solution(mesh):
    rows = P(("seq", "head"), None)
    return jax.shard_map(
        shards,
        mesh=mesh,
        in_specs=(rows, rows, rows, rows, P(), P()),
        out_specs=(rows,) * 4,
        check_vma=False,
    )
```

```python
import functools

import jax
import jax.numpy as jnp
from jax import lax
from jax.experimental import pallas as pl
from jax.experimental.pallas import tpu as pltpu
from jax.sharding import PartitionSpec as P

HD = 128
BLOCK = 64
QB = 8
NH = 8
NY = 4
NZ = 16
COL = NZ * QB
PLANE = NY * QB
SCALE = HD ** (-0.5)
FLOOR = -1e30
UNROLL = 8
TURNS = (4, 3, 5, 2, 6, 1, 7, 0)
TILES = PLANE // 4
TRASH = PLANE * 4 * COL
LIST = PLANE * 4 + 16
PAIRS = PLANE * 3 + 2 * NY + 8
MESH = pl.DeviceIdType.MESH
NT = (((1,), (1,)), ((), ()))
TN = (((0,), (0,)), ((), ()))
NN = (((1,), (0,)), ((), ()))
BF = jnp.bfloat16
F32 = jnp.float32
MIB = 1024 * 1024


def rcopy(src, dst, send, recv, seq, head):
    return pltpu.make_async_remote_copy(
        src_ref=src,
        dst_ref=dst,
        send_sem=send,
        recv_sem=recv,
        device_id=(seq, head),
        device_id_type=MESH,
    )


def place():
    seq = lax.axis_index("seq")
    head = lax.axis_index("head")
    return seq, head, seq // NZ, seq % NZ


def greet(peers, meanwhile=lambda: None):
    barrier = pltpu.get_barrier_semaphore()
    for seq, head in peers:
        pl.semaphore_signal(barrier, inc=1, device_id=(seq, head), device_id_type=MESH)
    meanwhile()
    pl.semaphore_wait(barrier, len(peers))


def head_peers(seq, head):
    return [(seq, (head + d) % NH) for d in range(1, NH)]


def row_peers(y, z, head):
    return [(((y + d) % NY) * NZ + z, head) for d in range(1, NY)]


def window_tile(c, kv_ref, qg_ref, y, z):
    lo, hi = max(2 * c - 1, 0), min(2 * c + 3, QB)
    shape = ((hi - lo) * BLOCK, HD)
    keys = kv_ref[z, 0, lo:hi].reshape(shape)
    values = kv_ref[z, 1, lo:hi].reshape(shape)
    queries = qg_ref[y, 0, 2 * c : 2 * c + 2].reshape(2 * BLOCK, HD)
    grads = qg_ref[y, 1, 2 * c : 2 * c + 2].reshape(2 * BLOCK, HD)
    scores = lax.dot_general(keys, queries, NT, preferred_element_type=F32) * SCALE
    dprobs = lax.dot_general(values, grads, NT, preferred_element_type=F32)
    gap = (lo - 2 * c) + (lax.broadcasted_iota(jnp.int32, shape, 0) >> 6)
    gap = gap - (lax.broadcasted_iota(jnp.int32, shape, 1) >> 6)
    near = (gap >= -1) & (gap <= 1)
    return lo, hi, keys, values, queries, grads, jnp.where(near, scores, FLOOR), dprobs


def near_planes(y, z):
    return [(y * NZ + (z + d) % NZ, h) for d in (1, NZ - 1) for h in range(NH)]


def gather_kernel(
    q_ref, k_ref, v_ref, g_ref, kv_ref, qg_ref, wst_ref, own, hs, hr, fs, fr, zs, zr, ys, yr
):
    seq, head, y, z = place()
    ins = (k_ref, v_ref, q_ref, g_ref)

    def home(a, sender):
        return kv_ref.at[z, a, sender] if a < 2 else qg_ref.at[y, a - 2, sender]

    def cols(h):
        return pl.ds(pl.multiple_of(h * HD, HD), HD)

    def keep(a):
        return pltpu.make_async_copy(ins[a].at[:, cols(head)], home(a, head), own.at[a])

    def give(a, d, sender, target):
        return rcopy(
            ins[a].at[:, cols(target)],
            home(a, sender),
            hs.at[a, d - 1],
            hr.at[a, d - 1],
            seq,
            target,
        )

    def give_all(a):
        for d in range(1, NH):
            give(a, d, head, (head + d) % NH).start()

    def take_all(a):
        for d in range(1, NH):
            give(a, d, (head + NH - d) % NH, (head + d) % NH).wait_recv()
        keep(a).wait()

    for a in range(4):
        keep(a).start()
    greet(head_peers(seq, head) + near_planes(y, z) + row_peers(y, z, head))
    right = y * NZ + (z + 1) % NZ
    left = y * NZ + (z + NZ - 1) % NZ
    sides = (right, left)

    def first(way, piece, d):
        target = (head + d) % NH
        return rcopy(
            ins[piece].at[:, cols(target)],
            kv_ref.at[z, piece, head],
            fs.at[way, piece, d],
            fr.at[way, piece, d],
            sides[way],
            target,
        )

    def first_in(way, piece, d):
        sender = (head + NH - d) % NH
        chunk = (z + NZ - 1 + 2 * way) % NZ
        return rcopy(
            ins[piece].at[:, cols(head)],
            kv_ref.at[chunk, piece, sender],
            fs.at[way, piece, d],
            fr.at[way, piece, d],
            sides[way],
            sender,
        )

    def hop(way, step, piece, back):
        if way == 0:
            chunk = (z + 2 * NZ - step - back) % NZ
        else:
            chunk = (z + step + back) % NZ
        ref = kv_ref.at[chunk, piece]
        return rcopy(ref, ref, zs.at[way, step, piece], zr.at[way, step, piece], sides[way], head)

    half = NZ // 2
    hops = [
        (way, step, piece)
        for step in range(1, half)
        for piece in range(2)
        for way in range(2)
        if step < half - 1 or piece == way
    ]
    for piece in range(2):
        for d in TURNS:
            for way in range(2):
                first(way, piece, d).start()
    def row(d, sender, target):
        ref = qg_ref.at[sender]
        return rcopy(ref, ref, ys.at[d - 1], yr.at[d - 1], target * NZ + z, head)

    wst_ref[0] = jnp.full((PLANE // 2, HD), FLOOR, F32)
    wst_ref[1] = jnp.zeros((PLANE // 2, HD), F32)
    wst_ref[2] = jnp.zeros((PLANE // 2, HD), F32)

    def window(c):
        _, _, _, _, _, _, scores, dprobs = window_tile(c, kv_ref, qg_ref, y, z)
        top = jnp.max(scores, axis=0, keepdims=True)
        expo = jnp.exp(scores - top)
        at = pl.ds(y * (QB // 2) + c, 1)
        wst_ref[0, at, :] = top
        wst_ref[1, at, :] = jnp.sum(expo, axis=0, keepdims=True)
        wst_ref[2, at, :] = jnp.sum(expo * dprobs, axis=0, keepdims=True)

    for way, step, piece in hops:
        if step == 1:
            for d in range(NH):
                first_in(way, piece, d).wait_recv()
        else:
            hop(way, step - 1, piece, 1).wait_recv()
        hop(way, step, piece, 0).start()
        if piece == 1 and way == 1:
            if step == 1:
                for a in (2, 3, 0, 1):
                    give_all(a)
            elif step == 3:
                for a in range(4):
                    take_all(a)
                for d in range(1, NY):
                    row(d, y, (y + d) % NY).start()
            elif step >= 4:
                window(step - 4)
    for d in range(1, NY):
        row(d, (y + NY - d) % NY, (y + d) % NY).wait_recv()
    for way, step, piece in hops:
        if step == half - 1 or (step == half - 2 and piece != way):
            hop(way, step, piece, 1).wait_recv()
    for a in range(4):
        for d in range(1, NH):
            give(a, d, head, (head + d) % NH).wait_send()
    for d in range(1, NY):
        row(d, y, (y + d) % NY).wait_send()
    for way in range(2):
        for piece in range(2):
            for d in range(NH):
                first(way, piece, d).wait_send()
    for way, step, piece in hops:
        hop(way, step, piece, 0).wait_send()


def vmem():
    return pl.BlockSpec(memory_space=pltpu.VMEM)


def smem():
    return pl.BlockSpec(memory_space=pltpu.SMEM)


def hbm():
    return pl.BlockSpec(memory_space=pltpu.HBM)


def gather(q, k, v, g):
    dma = pltpu.SemaphoreType.DMA
    return pl.pallas_call(
        gather_kernel,
        out_shape=(
            jax.ShapeDtypeStruct((NZ, 2, QB, BLOCK, HD), BF),
            jax.ShapeDtypeStruct((NY, 2, QB, BLOCK, HD), BF),
            jax.ShapeDtypeStruct((3, PLANE // 2, HD), F32),
        ),
        in_specs=[hbm()] * 4,
        out_specs=(vmem(),) * 3,
        scratch_shapes=[
            dma((4,)),
            dma((4, NH - 1)),
            dma((4, NH - 1)),
            dma((2, 2, NH)),
            dma((2, 2, NH)),
            dma((2, NZ // 2, 2)),
            dma((2, NZ // 2, 2)),
            dma((NY - 1,)),
            dma((NY - 1,)),
        ],
        compiler_params=pltpu.CompilerParams(
            collective_id=0, has_side_effects=True, vmem_limit_bytes=24 * MIB
        ),
        name="gather_rows",
    )(q, k, v, g)


def stats_kernel(ids_ref, kv_ref, qg_ref, list_ref, one, expo_ref, dprob_ref, ids, sem):
    y = lax.axis_index("seq") // NZ
    z = lax.axis_index("seq") % NZ
    base = y * COL
    fetch = pltpu.make_async_copy(ids_ref, ids, sem)
    fetch.start()
    one[0] = jnp.full((2, 5, PLANE // 2, HD), FLOOR, F32)
    for k in range(1, 3):
        one[k] = jnp.zeros((2, 5, PLANE // 2, HD), F32)
    fetch.wait()

    def note(count, i, slot, block):
        rel = block - base
        good = (rel >= 0) & (rel < COL)
        list_ref[count] = (i * 4 + slot) * COL + rel
        return count + good.astype(jnp.int32)

    count = jnp.int32(0)
    for g in range(NY):
        first = (g * NZ + z) * QB
        count = note(count, g * QB, 3, first - 1)
        count = note(count, g * QB + QB - 1, 3, first + QB)

        def scan(b, count, g=g, first=first):
            for r in range(3):
                count = note(count, g * QB + b, r, ids[r, first + b])
            return count

        count = lax.fori_loop(0, QB, scan, count, unroll=4)
    for u in range(UNROLL):
        list_ref[count + u] = jnp.int32(TRASH)
    rounds = (count + UNROLL - 1) >> 3
    list_ref[LIST - 1] = rounds

    def pairs(t, carry):
        done = []
        for u in range(UNROLL):
            code = list_ref[t * UNROLL + u]
            pair = code >> 7
            rel = code & (COL - 1)
            i = jnp.minimum(pair >> 2, PLANE - 1)
            keys = kv_ref[rel >> 3, 0, rel & 7]
            values = kv_ref[rel >> 3, 1, rel & 7]
            queries = qg_ref[i >> 3, 0, i & 7]
            grads = qg_ref[i >> 3, 1, i & 7]
            scores = lax.dot_general(keys, queries, NT, preferred_element_type=F32) * SCALE
            dprobs = lax.dot_general(values, grads, NT, preferred_element_type=F32)
            top = jnp.max(scores, axis=0, keepdims=True)
            expo = jnp.exp(scores - top)
            total = jnp.sum(expo, axis=0, keepdims=True)
            delta = jnp.sum(expo * dprobs, axis=0, keepdims=True)
            slot = jnp.where(code < TRASH, pair & 3, 4)
            done.append((i, slot, (top, total, delta), expo, dprobs))
        for u, (i, slot, found, expo, dprobs) in enumerate(done):
            expo_ref[t * UNROLL + u] = expo
            dprob_ref[t * UNROLL + u] = dprobs
            for k in range(3):
                one[k, i & 1, slot, pl.ds(i >> 1, 1), 0:BLOCK] = found[k]
        return carry

    lax.fori_loop(0, rounds, pairs, 0)


def tile_rows(qg_ref, t):
    at = slice((t % 2) * 4, (t % 2) * 4 + 4)
    queries = qg_ref[t // 2, 0, at].reshape(4 * BLOCK, HD)
    grads = qg_ref[t // 2, 1, at].reshape(4 * BLOCK, HD)
    return queries, grads


def stats(ids, kv, qg):
    return pl.pallas_call(
        stats_kernel,
        out_shape=(
            jax.ShapeDtypeStruct((LIST,), jnp.int32),
            jax.ShapeDtypeStruct((3, 2, 5, PLANE // 2, HD), F32),
            jax.ShapeDtypeStruct((PAIRS, BLOCK, BLOCK), F32),
            jax.ShapeDtypeStruct((PAIRS, BLOCK, BLOCK), F32),
        ),
        in_specs=[hbm(), vmem(), vmem()],
        out_specs=(smem(), vmem(), vmem(), vmem()),
        scratch_shapes=[
            pltpu.SMEM((3, NZ * NY * QB), jnp.int32),
            pltpu.SemaphoreType.DMA,
        ],
        compiler_params=pltpu.CompilerParams(vmem_limit_bytes=24 * MIB),
        name="pair_stats",
    )(ids, kv, qg)


def share_kernel(
    gids_ref, wst_ref, one, kv_ref, qg_ref, all_ref, full, st, gids, sem, send, recv
):
    seq, head, y, z = place()
    base = y * COL
    fetch = pltpu.make_async_copy(gids_ref, gids, sem)
    fetch.start()

    def total():
        fetch.wait()
        for n in range(2):
            rel = gids[n] - base
            good = (rel >= 0) & (rel < COL)
            rel = jnp.clip(rel, 0, COL - 1)
            keys = kv_ref[rel >> 3, 0, rel & 7]
            values = kv_ref[rel >> 3, 1, rel & 7]
            for t in range(TILES):
                queries, grads = tile_rows(qg_ref, t)
                scores = lax.dot_general(keys, queries, NT, preferred_element_type=F32) * SCALE
                dprobs = lax.dot_general(values, grads, NT, preferred_element_type=F32)
                top = jnp.max(scores, axis=0, keepdims=True)
                expo = jnp.exp(scores - top)
                found = (
                    jnp.where(good, top, FLOOR),
                    jnp.where(good, jnp.sum(expo, axis=0, keepdims=True), 0.0),
                    jnp.where(good, jnp.sum(expo * dprobs, axis=0, keepdims=True), 0.0),
                )
                for k in range(3):
                    for p in range(2):
                        full[k, n, 2 * t + p : 2 * t + p + 1] = found[k][:, p * HD : (p + 1) * HD]

        def parts(k):
            even = one[k, 0, 0:4]
            odd = pltpu.roll(one[k, 1, 0:4].reshape(2 * PLANE, HD), BLOCK, 1)
            odd = odd.reshape(4, PLANE // 2, HD)
            return jnp.concatenate([even, odd, full[k], wst_ref[k][None]], axis=0)

        tops = parts(0)
        top = jnp.max(tops, axis=0)
        factor = jnp.exp(tops - top[None])
        st[0] = top
        st[1] = jnp.sum(parts(1) * factor, axis=0)
        st[2] = jnp.sum(parts(2) * factor, axis=0)

    greet(row_peers(y, z, head), total)

    def row(d, sender, target):
        return rcopy(st, all_ref.at[sender], send.at[d - 1], recv.at[d - 1], target * NZ + z, head)

    for d in range(1, NY):
        row(d, y, (y + d) % NY).start()
    all_ref[y] = st[...]
    for d in range(1, NY):
        row(d, (y + NY - d) % NY, (y + d) % NY).wait_recv()
    for d in range(1, NY):
        row(d, y, (y + d) % NY).wait_send()


def share(gids, wst, one, kv, qg):
    dma = pltpu.SemaphoreType.DMA
    return pl.pallas_call(
        share_kernel,
        out_shape=jax.ShapeDtypeStruct((NY, 3, PLANE // 2, HD), F32),
        in_specs=[hbm()] + [vmem()] * 4,
        out_specs=vmem(),
        scratch_shapes=[
            pltpu.VMEM((3, 2, PLANE // 2, HD), F32),
            pltpu.VMEM((3, PLANE // 2, HD), F32),
            pltpu.SMEM((2,), jnp.int32),
            dma,
            dma((NY - 1,)),
            dma((NY - 1,)),
        ],
        compiler_params=pltpu.CompilerParams(
            collective_id=1, has_side_effects=True, vmem_limit_bytes=8 * MIB
        ),
        name="share_stats",
    )(gids, wst, one, kv, qg)


def terms_kernel(
    list_hbm,
    gids_hbm,
    all_ref,
    kv_ref,
    qg_ref,
    one,
    expo_ref,
    dprob_ref,
    dkv_ref,
    shifted,
    scale_ref,
    list_ref,
    gids,
    fetched,
):
    base = (lax.axis_index("seq") // NZ) * COL
    fetches = [
        pltpu.make_async_copy(list_hbm, list_ref, fetched.at[0]),
        pltpu.make_async_copy(gids_hbm, gids, fetched.at[1]),
    ]
    for fetch in fetches:
        fetch.start()
    tops = all_ref[:, 0]
    top = jnp.max(tops, axis=0)
    factor = jnp.exp(tops - top[None])
    inverse = 1.0 / jnp.sum(all_ref[:, 1] * factor, axis=0)
    delta = jnp.sum(all_ref[:, 2] * factor, axis=0) * inverse
    for k, value in enumerate((top, inverse, delta)):
        shifted[k, 0] = value
        shifted[k, 1] = pltpu.roll(value, BLOCK, 1)

    for p in range(2):
        factor = jnp.exp(one[0, p, 0:4] - shifted[0, p][None]) * shifted[1, p][None]
        scale_ref[p, 0:4] = factor
        scale_ref[p, 4] = jnp.zeros((PLANE // 2, HD), F32)

    def clear_kv(b, carry):
        dkv_ref[b] = jnp.zeros((2, QB, BLOCK, HD), BF)
        return carry

    lax.fori_loop(0, NZ, clear_kv, 0)
    for fetch in fetches:
        fetch.wait()
    rounds = list_ref[LIST - 1]

    def add_kv(rel, dk, dv):
        for a, term in enumerate((dk, dv)):
            old = dkv_ref[rel >> 3, a, rel & 7].astype(F32)
            dkv_ref[rel >> 3, a, rel & 7] = (old + term).astype(BF)

    def pairs(t, carry):
        done = []
        for u in range(UNROLL):
            code = list_ref[t * UNROLL + u]
            pair = code >> 7
            rel = code & (COL - 1)
            i = jnp.minimum(pair >> 2, PLANE - 1)
            at = pl.ds(i >> 1, 1)
            slot = jnp.where(code < TRASH, pair & 3, 4)
            queries = qg_ref[i >> 3, 0, i & 7]
            grads = qg_ref[i >> 3, 1, i & 7]
            weights = expo_ref[t * UNROLL + u] * scale_ref[i & 1, slot, at, 0:BLOCK]
            dprobs = dprob_ref[t * UNROLL + u]
            probs = weights.astype(BF)
            dscores = (weights * (dprobs - shifted[2, i & 1, at, 0:BLOCK])).astype(BF)
            dv = lax.dot_general(probs, grads, NN, preferred_element_type=F32)
            dk = lax.dot_general(dscores, queries, NN, preferred_element_type=F32) * SCALE
            done.append((rel, dk, dv))
        for rel, dk, dv in done:
            add_kv(rel, dk, dv)
        return carry

    lax.fori_loop(0, rounds, pairs, 0)

    for n in range(2):
        rel = gids[n] - base

        @pl.when((rel >= 0) & (rel < COL))
        def _(rel=rel):
            keys = kv_ref[rel >> 3, 0, rel & 7]
            values = kv_ref[rel >> 3, 1, rel & 7]
            dk = jnp.zeros((BLOCK, HD), F32)
            dv = jnp.zeros((BLOCK, HD), F32)
            for t in range(TILES):
                queries, grads = tile_rows(qg_ref, t)

                def wide(k, t=t):
                    pair = [shifted[k, 0, 2 * t + p : 2 * t + p + 1] for p in range(2)]
                    return jnp.concatenate(pair, axis=1)

                scores = lax.dot_general(keys, queries, NT, preferred_element_type=F32) * SCALE
                dprobs = lax.dot_general(values, grads, NT, preferred_element_type=F32)
                weights = jnp.exp(scores - wide(0)) * wide(1)
                probs = weights.astype(BF)
                dscores = (weights * (dprobs - wide(2))).astype(BF)
                dv = dv + lax.dot_general(probs, grads, NN, preferred_element_type=F32)
                dk = dk + lax.dot_general(dscores, queries, NN, preferred_element_type=F32) * SCALE
            add_kv(rel, dk, dv)


def terms(pair_list, gids, all_stats, kv, qg, pairs):
    return pl.pallas_call(
        terms_kernel,
        out_shape=(
            jax.ShapeDtypeStruct((NZ, 2, QB, BLOCK, HD), BF),
            jax.ShapeDtypeStruct((3, 2, PLANE // 2, HD), F32),
        ),
        in_specs=[pl.BlockSpec(memory_space=pl.ANY), hbm()] + [vmem()] * 6,
        out_specs=(vmem(),) * 2,
        scratch_shapes=[
            pltpu.VMEM((2, 5, PLANE // 2, HD), F32),
            pltpu.SMEM((LIST,), jnp.int32),
            pltpu.SMEM((2,), jnp.int32),
            pltpu.SemaphoreType.DMA((2,)),
        ],
        compiler_params=pltpu.CompilerParams(vmem_limit_bytes=32 * MIB),
        name="pair_terms",
    )(pair_list, gids, all_stats, kv, qg, *pairs)


def reduce_kernel(
    ids_ref,
    gids_ref,
    kv_ref,
    qg_ref,
    rows_ref,
    dkv_ref,
    o_ref,
    dq_ref,
    dk_ref,
    dv_ref,
    rb,
    ob,
    yb,
    pack,
    near_kv,
    near_oq,
    fin,
    ids,
    gids,
    fetched,
    hs,
    hr,
    fs,
    fr,
    zs,
    zr,
    ys,
    yr,
):
    seq, head, y, z = place()
    fetches = [
        pltpu.make_async_copy(ids_ref, ids, fetched.at[0]),
        pltpu.make_async_copy(gids_ref, gids, fetched.at[1]),
    ]
    for fetch in fetches:
        fetch.start()
    greet(head_peers(seq, head) + near_planes(y, z) + row_peers(y, z, head))
    right = y * NZ + (z + 1) % NZ
    left = y * NZ + (z + NZ - 1) % NZ
    half = NZ // 2
    base = y * COL
    outs = (o_ref, dq_ref, dk_ref, dv_ref)

    def chunk_of(way, step):
        if way == 0:
            return (z + half - step) % NZ
        return (z + half + step) % NZ

    def hop(way, step, piece):
        if step == 0 or (step == 1 and piece != way):
            src = dkv_ref.at[chunk_of(way, step), piece]
        else:
            src = rb.at[way, step - 1, piece]
        target = right if way == 0 else left
        return rcopy(
            src,
            rb.at[way, step, piece],
            zs.at[way, step, piece],
            zr.at[way, step, piece],
            target,
            head,
        )

    def row(d, target):
        return rcopy(
            ob.at[d - 1], yb.at[d - 1], ys.at[d - 1], yr.at[d - 1], target * NZ + z, head
        )

    def cols(h):
        return pl.ds(pl.multiple_of(h * HD, HD), HD)

    def scatter(a, d, sender, target):
        home = outs[a].at[:, cols(sender)] if a < 2 else fin.at[2, a - 2, sender]
        return rcopy(pack.at[a, target], home, hs.at[a, d - 1], hr.at[a, d - 1], seq, target)

    def send_heads(a):
        for d in range(1, NH):
            scatter(a, d, head, (head + d) % NH).start()
        if a < 2:
            outs[a][:, cols(head)] = pack[a, head]
        else:
            fin[2, a - 2, head] = pack[a, head]

    def final(way, piece, d, sender, target):
        return rcopy(
            rb.at[way, half - 2, piece, target],
            fin.at[way, piece, sender],
            fs.at[way, piece, d],
            fr.at[way, piece, d],
            right if way == 0 else left,
            target,
        )

    def far(d, b):
        group = (y + d) % NY
        first = (group * NZ + z) * QB
        edge = jnp.where(b == 0, first - 1, jnp.where(b == QB - 1, first + QB, -1))
        blocks = [ids[r, first + b] for r in range(3)] + [gids[0], gids[1], edge]
        at = pl.ds(group * (QB // 2) + (b >> 1), 1)
        top = rows_ref[0, b & 1, at, 0:BLOCK]
        inverse = rows_ref[1, b & 1, at, 0:BLOCK]
        delta = rows_ref[2, b & 1, at, 0:BLOCK]
        rels = [block - base for block in blocks]
        live = [(rel >= 0) & (rel < COL) for rel in rels]
        rels = [jnp.clip(rel, 0, COL - 1) for rel in rels]
        keys = jnp.concatenate([kv_ref[rel >> 3, 0, rel & 7] for rel in rels], axis=0)
        values = jnp.concatenate([kv_ref[rel >> 3, 1, rel & 7] for rel in rels], axis=0)
        scores = lax.dot_general(keys, qg_ref[group, 0, b], NT, preferred_element_type=F32)
        dprobs = lax.dot_general(values, qg_ref[group, 1, b], NT, preferred_element_type=F32)
        weights = jnp.exp(scores * SCALE - top) * inverse
        weights = jnp.concatenate(
            [
                jnp.where(good, weights[n * BLOCK : (n + 1) * BLOCK], 0.0)
                for n, good in enumerate(live)
            ],
            axis=0,
        )
        probs = weights.astype(BF)
        dscores = (weights * (dprobs - delta)).astype(BF)
        out = lax.dot_general(probs, values, TN, preferred_element_type=F32)
        dq = lax.dot_general(dscores, keys, TN, preferred_element_type=F32) * SCALE
        if d < NY:
            ob[d - 1, 0, b] = out.astype(BF)
            ob[d - 1, 1, b] = dq.astype(BF)
        else:
            near_oq[0, b] = out
            near_oq[1, b] = dq

    def far_some(start, count):
        d = start // QB + 1

        def one(b, carry):
            far(d, b)
            return carry

        lax.fori_loop(start % QB, start % QB + count, one, 0, unroll=True)
        if d < NY and start % QB + count == QB:
            row(d, (y + d) % NY).start()

    def window(c):
        lo, hi, keys, values, queries, grads, scores, dprobs = window_tile(c, kv_ref, qg_ref, y, z)
        at = pl.ds(y * (QB // 2) + c, 1)
        weights = jnp.exp(scores - rows_ref[0, 0, at, :]) * rows_ref[1, 0, at, :]
        probs = weights.astype(BF)
        dscores = (weights * (dprobs - rows_ref[2, 0, at, :])).astype(BF)
        dv = lax.dot_general(probs, grads, NN, preferred_element_type=F32)
        dk = lax.dot_general(dscores, queries, NN, preferred_element_type=F32) * SCALE
        out = lax.dot_general(probs, values, TN, preferred_element_type=F32)
        dq = lax.dot_general(dscores, keys, TN, preferred_element_type=F32) * SCALE
        near_kv[0, lo:hi] += dk.reshape(hi - lo, BLOCK, HD)
        near_kv[1, lo:hi] += dv.reshape(hi - lo, BLOCK, HD)
        near_oq[0, 2 * c : 2 * c + 2] += out.reshape(2, BLOCK, HD)
        near_oq[1, 2 * c : 2 * c + 2] += dq.reshape(2, BLOCK, HD)

    def total():
        for d in range(1, NY):
            row(d, (y + d) % NY).wait_recv()

        def add(b, carry):
            for a in range(2):
                acc = near_oq[a, b]
                for d in range(NY - 1):
                    acc = acc + yb[d, a, b].astype(F32)
                pack[a, b] = acc.astype(BF)
            return carry

        lax.fori_loop(0, QB, add, 0)
        send_heads(0)
        send_heads(1)

    def give_near():
        def add(b, carry):
            for piece in range(2):
                acc = near_kv[piece, b] + dkv_ref[z, piece, b].astype(F32)
                pack[2 + piece, b] = acc.astype(BF)
            return carry

        lax.fori_loop(0, QB, add, 0)
        send_heads(2)
        send_heads(3)

    jobs = [functools.partial(far_some, n, 2) for n in range(6, NY * QB, 2)]
    for c in range(QB // 2):
        jobs += [functools.partial(window, c)]
    jobs += [give_near, lambda: None, total]

    hop(0, 0, 0).start()
    hop(1, 0, 1).start()
    for way, piece in ((0, 1), (1, 0)):
        hop(way, 1, piece).start()
    near_kv[...] = jnp.zeros((2, QB, BLOCK, HD), F32)
    for fetch in fetches:
        fetch.wait()
    for n in range(0, 6, 2):
        far_some(n, 2)

    for step in range(1, half):
        for piece in range(2):
            for way in range(2):
                if step == 1 and piece != way:
                    continue
                hop(way, step - 1, piece).wait_recv()
                chunk = chunk_of(way, step)

                def add(b, carry, way=way, step=step, piece=piece, chunk=chunk):
                    mine = dkv_ref[chunk, piece, b].astype(F32)
                    rb[way, step - 1, piece, b] = (
                        rb[way, step - 1, piece, b].astype(F32) + mine
                    ).astype(BF)
                    return carry

                lax.fori_loop(0, QB, add, 0)
                if step < half - 1:
                    hop(way, step, piece).start()
                else:
                    for d in TURNS:
                        final(way, piece, d, head, (head + d) % NH).start()
                if jobs:
                    jobs.pop(0)()
    for job in jobs:
        job()

    for a in range(4):
        for d in range(1, NH):
            scatter(a, d, (head + NH - d) % NH, (head + d) % NH).wait_recv()
    for piece in range(2):
        for way in range(2):
            for d in range(NH):
                final(way, piece, d, (head + NH - d) % NH, (head + d) % NH).wait_recv()

        for h in range(NH):
            acc = fin[2, piece, h].astype(F32)
            acc = acc + fin[0, piece, h].astype(F32)
            acc = acc + fin[1, piece, h].astype(F32)
            outs[2 + piece][:, h * HD : (h + 1) * HD] = acc.astype(BF)

    for a in range(4):
        for d in range(1, NH):
            scatter(a, d, head, (head + d) % NH).wait_send()
    for d in range(1, NY):
        row(d, (y + d) % NY).wait_send()
    for way in range(2):
        for piece in range(2):
            for d in range(NH):
                final(way, piece, d, head, (head + d) % NH).wait_send()
    for step in range(half - 1):
        for piece in range(2):
            for way in range(2):
                if step > 0 or piece == way:
                    hop(way, step, piece).wait_send()


def reduce(ids, gids, kv, qg, rows, dkv):
    dma = pltpu.SemaphoreType.DMA
    out = jax.ShapeDtypeStruct((BLOCK, NH * HD), BF)
    return pl.pallas_call(
        reduce_kernel,
        out_shape=(out,) * 4,
        in_specs=[hbm()] * 2 + [vmem()] * 4,
        out_specs=(vmem(),) * 4,
        scratch_shapes=[
            pltpu.VMEM((2, NZ // 2, 2, QB, BLOCK, HD), BF),
            pltpu.VMEM((NY - 1, 2, QB, BLOCK, HD), BF),
            pltpu.VMEM((NY - 1, 2, QB, BLOCK, HD), BF),
            pltpu.VMEM((4, NH, BLOCK, HD), BF),
            pltpu.VMEM((2, QB, BLOCK, HD), F32),
            pltpu.VMEM((2, QB, BLOCK, HD), F32),
            pltpu.VMEM((3, 2, NH, BLOCK, HD), BF),
            pltpu.SMEM((3, NZ * NY * QB), jnp.int32),
            pltpu.SMEM((2,), jnp.int32),
            dma((2,)),
            dma((4, NH - 1)),
            dma((4, NH - 1)),
            dma((2, 2, NH)),
            dma((2, 2, NH)),
            dma((2, NZ // 2, 2)),
            dma((2, NZ // 2, 2)),
            dma((NY - 1,)),
            dma((NY - 1,)),
        ],
        compiler_params=pltpu.CompilerParams(
            collective_id=2, has_side_effects=True, vmem_limit_bytes=32 * MIB
        ),
        name="reduce_rows",
    )(ids, gids, kv, qg, rows, dkv)


def deliver_kernel(*refs):
    sems = refs[8]
    copies = [pltpu.make_async_copy(refs[a], refs[4 + a], sems.at[a]) for a in range(4)]
    for copy in copies:
        copy.start()
    for copy in copies:
        copy.wait()


def deliver(outs):
    return pl.pallas_call(
        deliver_kernel,
        out_shape=tuple(jax.ShapeDtypeStruct(o.shape, o.dtype) for o in outs),
        in_specs=[vmem()] * 4,
        out_specs=(hbm(),) * 4,
        scratch_shapes=[pltpu.SemaphoreType.DMA((4,))],
        compiler_params=pltpu.CompilerParams(vmem_limit_bytes=8 * MIB),
        name="deliver_rows",
    )(*outs)


def shards(query_rows, key_rows, value_rows, out_grad, random_ids, global_ids):
    rows = (query_rows, key_rows, value_rows, out_grad)
    kv, qg, wst = gather(*(pltpu.with_memory_space_constraint(r, pltpu.HBM) for r in rows))
    ids = pltpu.with_memory_space_constraint(random_ids.T, pltpu.HBM)
    global_ids = pltpu.with_memory_space_constraint(global_ids, pltpu.HBM)
    pair_list, one, *pairs = stats(ids, kv, qg)
    sums = share(global_ids, wst, one, kv, qg)
    dkv, row_stats = terms(pair_list, global_ids, sums, kv, qg, (one, *pairs))
    return deliver(reduce(ids, global_ids, kv, qg, row_stats, dkv))


def solution(mesh):
    rows = P(("seq", "head"), None)
    return jax.shard_map(
        shards,
        mesh=mesh,
        in_specs=(rows, rows, rows, rows, P(), P()),
        out_specs=(rows,) * 4,
        check_vma=False,
    )
```

```python
import functools

import jax
import jax.numpy as jnp
from jax import lax
from jax.experimental import pallas as pl
from jax.experimental.pallas import tpu as pltpu
from jax.sharding import PartitionSpec as P

HD = 128
BLOCK = 64
QB = 8
NH = 8
NY = 4
NZ = 16
COL = NZ * QB
PLANE = NY * QB
SCALE = HD ** (-0.5)
FLOOR = -1e30
UNROLL = 8
TURNS = (4, 3, 5, 2, 6, 1, 7, 0)
TILES = PLANE // 4
TRASH = PLANE * 4 * COL
LIST = PLANE * 4 + 16
PAIRS = PLANE * 3 + 2 * NY + 8
MESH = pl.DeviceIdType.MESH
NT = (((1,), (1,)), ((), ()))
TN = (((0,), (0,)), ((), ()))
NN = (((1,), (0,)), ((), ()))
BF = jnp.bfloat16
F32 = jnp.float32
MIB = 1024 * 1024


def rcopy(src, dst, send, recv, seq, head):
    return pltpu.make_async_remote_copy(
        src_ref=src,
        dst_ref=dst,
        send_sem=send,
        recv_sem=recv,
        device_id=(seq, head),
        device_id_type=MESH,
    )


def place():
    seq = lax.axis_index("seq")
    head = lax.axis_index("head")
    return seq, head, seq // NZ, seq % NZ


def greet(peers, meanwhile=lambda: None):
    barrier = pltpu.get_barrier_semaphore()
    for seq, head in peers:
        pl.semaphore_signal(barrier, inc=1, device_id=(seq, head), device_id_type=MESH)
    meanwhile()
    pl.semaphore_wait(barrier, len(peers))


def head_peers(seq, head):
    return [(seq, (head + d) % NH) for d in range(1, NH)]


def row_peers(y, z, head):
    return [(((y + d) % NY) * NZ + z, head) for d in range(1, NY)]


def window_tile(c, kv_ref, qg_ref, y, z):
    lo, hi = max(2 * c - 1, 0), min(2 * c + 3, QB)
    shape = ((hi - lo) * BLOCK, HD)
    keys = kv_ref[z, 0, lo:hi].reshape(shape)
    values = kv_ref[z, 1, lo:hi].reshape(shape)
    queries = qg_ref[y, 0, 2 * c : 2 * c + 2].reshape(2 * BLOCK, HD)
    grads = qg_ref[y, 1, 2 * c : 2 * c + 2].reshape(2 * BLOCK, HD)
    scores = lax.dot_general(keys, queries, NT, preferred_element_type=F32) * SCALE
    dprobs = lax.dot_general(values, grads, NT, preferred_element_type=F32)
    gap = (lo - 2 * c) + (lax.broadcasted_iota(jnp.int32, shape, 0) >> 6)
    gap = gap - (lax.broadcasted_iota(jnp.int32, shape, 1) >> 6)
    near = (gap >= -1) & (gap <= 1)
    return lo, hi, keys, values, queries, grads, jnp.where(near, scores, FLOOR), dprobs


def near_planes(y, z):
    return [(y * NZ + (z + d) % NZ, h) for d in (1, NZ - 1) for h in range(NH)]


def gather_kernel(
    q_ref, k_ref, v_ref, g_ref, kv_ref, qg_ref, wst_ref, own, hs, hr, fs, fr, zs, zr, ys, yr
):
    seq, head, y, z = place()
    ins = (k_ref, v_ref, q_ref, g_ref)

    def home(a, sender):
        return kv_ref.at[z, a, sender] if a < 2 else qg_ref.at[y, a - 2, sender]

    def cols(h):
        return pl.ds(pl.multiple_of(h * HD, HD), HD)

    def keep(a):
        return pltpu.make_async_copy(ins[a].at[:, cols(head)], home(a, head), own.at[a])

    def give(a, d, sender, target):
        return rcopy(
            ins[a].at[:, cols(target)],
            home(a, sender),
            hs.at[a, d - 1],
            hr.at[a, d - 1],
            seq,
            target,
        )

    def give_all(a):
        for d in range(1, NH):
            give(a, d, head, (head + d) % NH).start()

    def take_all(a):
        for d in range(1, NH):
            give(a, d, (head + NH - d) % NH, (head + d) % NH).wait_recv()
        keep(a).wait()

    for a in range(4):
        keep(a).start()
    greet(head_peers(seq, head) + near_planes(y, z) + row_peers(y, z, head))
    right = y * NZ + (z + 1) % NZ
    left = y * NZ + (z + NZ - 1) % NZ
    sides = (right, left)

    def first(way, piece, d):
        target = (head + d) % NH
        return rcopy(
            ins[piece].at[:, cols(target)],
            kv_ref.at[z, piece, head],
            fs.at[way, piece, d],
            fr.at[way, piece, d],
            sides[way],
            target,
        )

    def first_in(way, piece, d):
        sender = (head + NH - d) % NH
        chunk = (z + NZ - 1 + 2 * way) % NZ
        return rcopy(
            ins[piece].at[:, cols(head)],
            kv_ref.at[chunk, piece, sender],
            fs.at[way, piece, d],
            fr.at[way, piece, d],
            sides[way],
            sender,
        )

    def hop(way, step, piece, back):
        if way == 0:
            chunk = (z + 2 * NZ - step - back) % NZ
        else:
            chunk = (z + step + back) % NZ
        ref = kv_ref.at[chunk, piece]
        return rcopy(ref, ref, zs.at[way, step, piece], zr.at[way, step, piece], sides[way], head)

    half = NZ // 2
    hops = [
        (way, step, piece)
        for step in range(1, half)
        for piece in range(2)
        for way in range(2)
        if step < half - 1 or piece == way
    ]
    for piece in range(2):
        for d in TURNS:
            for way in range(2):
                first(way, piece, d).start()
    def row(d, sender, target):
        ref = qg_ref.at[sender]
        return rcopy(ref, ref, ys.at[d - 1], yr.at[d - 1], target * NZ + z, head)

    wst_ref[0] = jnp.full((PLANE // 2, HD), FLOOR, F32)
    wst_ref[1] = jnp.zeros((PLANE // 2, HD), F32)
    wst_ref[2] = jnp.zeros((PLANE // 2, HD), F32)

    def window(c):
        _, _, _, _, _, _, scores, dprobs = window_tile(c, kv_ref, qg_ref, y, z)
        top = jnp.max(scores, axis=0, keepdims=True)
        expo = jnp.exp(scores - top)
        at = pl.ds(y * (QB // 2) + c, 1)
        wst_ref[0, at, :] = top
        wst_ref[1, at, :] = jnp.sum(expo, axis=0, keepdims=True)
        wst_ref[2, at, :] = jnp.sum(expo * dprobs, axis=0, keepdims=True)

    for way, step, piece in hops:
        if step == 1:
            for d in range(NH):
                first_in(way, piece, d).wait_recv()
        else:
            hop(way, step - 1, piece, 1).wait_recv()
        hop(way, step, piece, 0).start()
        if piece == 1 and way == 1:
            if step == 1:
                for a in (2, 3, 0, 1):
                    give_all(a)
            elif step == 3:
                for a in range(4):
                    take_all(a)
                for d in range(1, NY):
                    row(d, y, (y + d) % NY).start()
            elif step >= 4:
                window(step - 4)
    for d in range(1, NY):
        row(d, (y + NY - d) % NY, (y + d) % NY).wait_recv()
    for way, step, piece in hops:
        if step == half - 1 or (step == half - 2 and piece != way):
            hop(way, step, piece, 1).wait_recv()
    for a in range(4):
        for d in range(1, NH):
            give(a, d, head, (head + d) % NH).wait_send()
    for d in range(1, NY):
        row(d, y, (y + d) % NY).wait_send()
    for way in range(2):
        for piece in range(2):
            for d in range(NH):
                first(way, piece, d).wait_send()
    for way, step, piece in hops:
        hop(way, step, piece, 0).wait_send()


def vmem():
    return pl.BlockSpec(memory_space=pltpu.VMEM)


def smem():
    return pl.BlockSpec(memory_space=pltpu.SMEM)


def hbm():
    return pl.BlockSpec(memory_space=pltpu.HBM)


def gather(q, k, v, g):
    dma = pltpu.SemaphoreType.DMA
    return pl.pallas_call(
        gather_kernel,
        out_shape=(
            jax.ShapeDtypeStruct((NZ, 2, QB, BLOCK, HD), BF),
            jax.ShapeDtypeStruct((NY, 2, QB, BLOCK, HD), BF),
            jax.ShapeDtypeStruct((3, PLANE // 2, HD), F32),
        ),
        in_specs=[hbm()] * 4,
        out_specs=(vmem(),) * 3,
        scratch_shapes=[
            dma((4,)),
            dma((4, NH - 1)),
            dma((4, NH - 1)),
            dma((2, 2, NH)),
            dma((2, 2, NH)),
            dma((2, NZ // 2, 2)),
            dma((2, NZ // 2, 2)),
            dma((NY - 1,)),
            dma((NY - 1,)),
        ],
        compiler_params=pltpu.CompilerParams(
            collective_id=0, has_side_effects=True, vmem_limit_bytes=24 * MIB
        ),
        name="gather_rows",
    )(q, k, v, g)


def stats_kernel(ids_ref, kv_ref, qg_ref, list_ref, one, expo_ref, dprob_ref, ids, sem):
    y = lax.axis_index("seq") // NZ
    z = lax.axis_index("seq") % NZ
    base = y * COL
    fetch = pltpu.make_async_copy(ids_ref, ids, sem)
    fetch.start()
    one[0] = jnp.full((2, 5, PLANE // 2, HD), FLOOR, F32)
    for k in range(1, 3):
        one[k] = jnp.zeros((2, 5, PLANE // 2, HD), F32)
    fetch.wait()

    def note(count, i, slot, block):
        rel = block - base
        good = (rel >= 0) & (rel < COL)
        list_ref[count] = (i * 4 + slot) * COL + rel
        return count + good.astype(jnp.int32)

    count = jnp.int32(0)
    for g in range(NY):
        first = (g * NZ + z) * QB
        count = note(count, g * QB, 3, first - 1)
        count = note(count, g * QB + QB - 1, 3, first + QB)

        def scan(b, count, g=g, first=first):
            for r in range(3):
                count = note(count, g * QB + b, r, ids[r, first + b])
            return count

        count = lax.fori_loop(0, QB, scan, count, unroll=4)
    for u in range(UNROLL):
        list_ref[count + u] = jnp.int32(TRASH)
    rounds = (count + UNROLL - 1) >> 3
    list_ref[LIST - 1] = rounds

    def pairs(t, carry):
        done = []
        for u in range(UNROLL):
            code = list_ref[t * UNROLL + u]
            pair = code >> 7
            rel = code & (COL - 1)
            i = jnp.minimum(pair >> 2, PLANE - 1)
            keys = kv_ref[rel >> 3, 0, rel & 7]
            values = kv_ref[rel >> 3, 1, rel & 7]
            queries = qg_ref[i >> 3, 0, i & 7]
            grads = qg_ref[i >> 3, 1, i & 7]
            scores = lax.dot_general(keys, queries, NT, preferred_element_type=F32) * SCALE
            dprobs = lax.dot_general(values, grads, NT, preferred_element_type=F32)
            top = jnp.max(scores, axis=0, keepdims=True)
            expo = jnp.exp(scores - top)
            total = jnp.sum(expo, axis=0, keepdims=True)
            delta = jnp.sum(expo * dprobs, axis=0, keepdims=True)
            slot = jnp.where(code < TRASH, pair & 3, 4)
            done.append((i, slot, (top, total, delta), expo, dprobs))
        for u, (i, slot, found, expo, dprobs) in enumerate(done):
            expo_ref[t * UNROLL + u] = expo
            dprob_ref[t * UNROLL + u] = dprobs
            for k in range(3):
                one[k, i & 1, slot, pl.ds(i >> 1, 1), 0:BLOCK] = found[k]
        return carry

    lax.fori_loop(0, rounds, pairs, 0)


def tile_rows(qg_ref, t):
    at = slice((t % 2) * 4, (t % 2) * 4 + 4)
    queries = qg_ref[t // 2, 0, at].reshape(4 * BLOCK, HD)
    grads = qg_ref[t // 2, 1, at].reshape(4 * BLOCK, HD)
    return queries, grads


def stats(ids, kv, qg):
    return pl.pallas_call(
        stats_kernel,
        out_shape=(
            jax.ShapeDtypeStruct((LIST,), jnp.int32),
            jax.ShapeDtypeStruct((3, 2, 5, PLANE // 2, HD), F32),
            jax.ShapeDtypeStruct((PAIRS, BLOCK, BLOCK), F32),
            jax.ShapeDtypeStruct((PAIRS, BLOCK, BLOCK), F32),
        ),
        in_specs=[hbm(), vmem(), vmem()],
        out_specs=(smem(), vmem(), vmem(), vmem()),
        scratch_shapes=[
            pltpu.SMEM((3, NZ * NY * QB), jnp.int32),
            pltpu.SemaphoreType.DMA,
        ],
        compiler_params=pltpu.CompilerParams(vmem_limit_bytes=24 * MIB),
        name="pair_stats",
    )(ids, kv, qg)


def share_kernel(
    gids_ref, wst_ref, one, kv_ref, qg_ref, all_ref, full, st, gids, sem, send, recv
):
    seq, head, y, z = place()
    base = y * COL
    fetch = pltpu.make_async_copy(gids_ref, gids, sem)
    fetch.start()

    def total():
        fetch.wait()
        for n in range(2):
            rel = gids[n] - base
            good = (rel >= 0) & (rel < COL)
            rel = jnp.clip(rel, 0, COL - 1)
            keys = kv_ref[rel >> 3, 0, rel & 7]
            values = kv_ref[rel >> 3, 1, rel & 7]
            for t in range(TILES):
                queries, grads = tile_rows(qg_ref, t)
                scores = lax.dot_general(keys, queries, NT, preferred_element_type=F32) * SCALE
                dprobs = lax.dot_general(values, grads, NT, preferred_element_type=F32)
                top = jnp.max(scores, axis=0, keepdims=True)
                expo = jnp.exp(scores - top)
                found = (
                    jnp.where(good, top, FLOOR),
                    jnp.where(good, jnp.sum(expo, axis=0, keepdims=True), 0.0),
                    jnp.where(good, jnp.sum(expo * dprobs, axis=0, keepdims=True), 0.0),
                )
                for k in range(3):
                    for p in range(2):
                        full[k, n, 2 * t + p : 2 * t + p + 1] = found[k][:, p * HD : (p + 1) * HD]

        def parts(k):
            even = one[k, 0, 0:4]
            odd = pltpu.roll(one[k, 1, 0:4].reshape(2 * PLANE, HD), BLOCK, 1)
            odd = odd.reshape(4, PLANE // 2, HD)
            return jnp.concatenate([even, odd, full[k], wst_ref[k][None]], axis=0)

        tops = parts(0)
        top = jnp.max(tops, axis=0)
        factor = jnp.exp(tops - top[None])
        st[0] = top
        st[1] = jnp.sum(parts(1) * factor, axis=0)
        st[2] = jnp.sum(parts(2) * factor, axis=0)

    greet(row_peers(y, z, head), total)

    def row(d, sender, target):
        return rcopy(st, all_ref.at[sender], send.at[d - 1], recv.at[d - 1], target * NZ + z, head)

    for d in range(1, NY):
        row(d, y, (y + d) % NY).start()
    all_ref[y] = st[...]
    for d in range(1, NY):
        row(d, (y + NY - d) % NY, (y + d) % NY).wait_recv()
    for d in range(1, NY):
        row(d, y, (y + d) % NY).wait_send()


def share(gids, wst, one, kv, qg):
    dma = pltpu.SemaphoreType.DMA
    return pl.pallas_call(
        share_kernel,
        out_shape=jax.ShapeDtypeStruct((NY, 3, PLANE // 2, HD), F32),
        in_specs=[hbm()] + [vmem()] * 4,
        out_specs=vmem(),
        scratch_shapes=[
            pltpu.VMEM((3, 2, PLANE // 2, HD), F32),
            pltpu.VMEM((3, PLANE // 2, HD), F32),
            pltpu.SMEM((2,), jnp.int32),
            dma,
            dma((NY - 1,)),
            dma((NY - 1,)),
        ],
        compiler_params=pltpu.CompilerParams(
            collective_id=1, has_side_effects=True, vmem_limit_bytes=8 * MIB
        ),
        name="share_stats",
    )(gids, wst, one, kv, qg)


def terms_kernel(
    list_hbm,
    gids_hbm,
    all_ref,
    kv_ref,
    qg_ref,
    one,
    expo_ref,
    dprob_ref,
    dkv_ref,
    shifted,
    scale_ref,
    list_ref,
    gids,
    fetched,
):
    base = (lax.axis_index("seq") // NZ) * COL
    fetches = [
        pltpu.make_async_copy(list_hbm, list_ref, fetched.at[0]),
        pltpu.make_async_copy(gids_hbm, gids, fetched.at[1]),
    ]
    for fetch in fetches:
        fetch.start()
    tops = all_ref[:, 0]
    top = jnp.max(tops, axis=0)
    factor = jnp.exp(tops - top[None])
    inverse = 1.0 / jnp.sum(all_ref[:, 1] * factor, axis=0)
    delta = jnp.sum(all_ref[:, 2] * factor, axis=0) * inverse
    for k, value in enumerate((top, inverse, delta)):
        shifted[k, 0] = value
        shifted[k, 1] = pltpu.roll(value, BLOCK, 1)

    for p in range(2):
        factor = jnp.exp(one[0, p, 0:4] - shifted[0, p][None]) * shifted[1, p][None]
        scale_ref[p, 0:4] = factor
        scale_ref[p, 4] = jnp.zeros((PLANE // 2, HD), F32)

    def clear_kv(b, carry):
        dkv_ref[b] = jnp.zeros((2, QB, BLOCK, HD), BF)
        return carry

    lax.fori_loop(0, NZ, clear_kv, 0)
    for fetch in fetches:
        fetch.wait()
    rounds = list_ref[LIST - 1]

    def add_kv(rel, dk, dv):
        for a, term in enumerate((dk, dv)):
            old = dkv_ref[rel >> 3, a, rel & 7].astype(F32)
            dkv_ref[rel >> 3, a, rel & 7] = (old + term).astype(BF)

    def pairs(t, carry):
        done = []
        for u in range(UNROLL):
            code = list_ref[t * UNROLL + u]
            pair = code >> 7
            rel = code & (COL - 1)
            i = jnp.minimum(pair >> 2, PLANE - 1)
            at = pl.ds(i >> 1, 1)
            slot = jnp.where(code < TRASH, pair & 3, 4)
            queries = qg_ref[i >> 3, 0, i & 7]
            grads = qg_ref[i >> 3, 1, i & 7]
            weights = expo_ref[t * UNROLL + u] * scale_ref[i & 1, slot, at, 0:BLOCK]
            dprobs = dprob_ref[t * UNROLL + u]
            probs = weights.astype(BF)
            dscores = (weights * (dprobs - shifted[2, i & 1, at, 0:BLOCK])).astype(BF)
            dv = lax.dot_general(probs, grads, NN, preferred_element_type=F32)
            dk = lax.dot_general(dscores, queries, NN, preferred_element_type=F32) * SCALE
            done.append((rel, dk, dv))
        for rel, dk, dv in done:
            add_kv(rel, dk, dv)
        return carry

    lax.fori_loop(0, rounds, pairs, 0)

    for n in range(2):
        rel = gids[n] - base

        @pl.when((rel >= 0) & (rel < COL))
        def _(rel=rel):
            keys = kv_ref[rel >> 3, 0, rel & 7]
            values = kv_ref[rel >> 3, 1, rel & 7]
            dk = jnp.zeros((BLOCK, HD), F32)
            dv = jnp.zeros((BLOCK, HD), F32)
            for t in range(TILES):
                queries, grads = tile_rows(qg_ref, t)

                def wide(k, t=t):
                    pair = [shifted[k, 0, 2 * t + p : 2 * t + p + 1] for p in range(2)]
                    return jnp.concatenate(pair, axis=1)

                scores = lax.dot_general(keys, queries, NT, preferred_element_type=F32) * SCALE
                dprobs = lax.dot_general(values, grads, NT, preferred_element_type=F32)
                weights = jnp.exp(scores - wide(0)) * wide(1)
                probs = weights.astype(BF)
                dscores = (weights * (dprobs - wide(2))).astype(BF)
                dv = dv + lax.dot_general(probs, grads, NN, preferred_element_type=F32)
                dk = dk + lax.dot_general(dscores, queries, NN, preferred_element_type=F32) * SCALE
            add_kv(rel, dk, dv)


def terms(pair_list, gids, all_stats, kv, qg, pairs):
    return pl.pallas_call(
        terms_kernel,
        out_shape=(
            jax.ShapeDtypeStruct((NZ, 2, QB, BLOCK, HD), BF),
            jax.ShapeDtypeStruct((3, 2, PLANE // 2, HD), F32),
        ),
        in_specs=[pl.BlockSpec(memory_space=pl.ANY), hbm()] + [vmem()] * 6,
        out_specs=(vmem(),) * 2,
        scratch_shapes=[
            pltpu.VMEM((2, 5, PLANE // 2, HD), F32),
            pltpu.SMEM((LIST,), jnp.int32),
            pltpu.SMEM((2,), jnp.int32),
            pltpu.SemaphoreType.DMA((2,)),
        ],
        compiler_params=pltpu.CompilerParams(vmem_limit_bytes=32 * MIB),
        name="pair_terms",
    )(pair_list, gids, all_stats, kv, qg, *pairs)


def reduce_kernel(
    ids_ref,
    gids_ref,
    kv_ref,
    qg_ref,
    rows_ref,
    dkv_ref,
    o_ref,
    dq_ref,
    dk_ref,
    dv_ref,
    rb,
    ob,
    yb,
    pack,
    near_kv,
    near_oq,
    fin,
    ids,
    gids,
    fetched,
    hs,
    hr,
    fs,
    fr,
    zs,
    zr,
    ys,
    yr,
):
    seq, head, y, z = place()
    fetches = [
        pltpu.make_async_copy(ids_ref, ids, fetched.at[0]),
        pltpu.make_async_copy(gids_ref, gids, fetched.at[1]),
    ]
    for fetch in fetches:
        fetch.start()
    greet(head_peers(seq, head) + near_planes(y, z) + row_peers(y, z, head))
    right = y * NZ + (z + 1) % NZ
    left = y * NZ + (z + NZ - 1) % NZ
    half = NZ // 2
    base = y * COL
    outs = (o_ref, dq_ref, dk_ref, dv_ref)

    def chunk_of(way, step):
        if way == 0:
            return (z + half - step) % NZ
        return (z + half + step) % NZ

    def hop(way, step, piece):
        if step == 0 or (step == 1 and piece != way):
            src = dkv_ref.at[chunk_of(way, step), piece]
        else:
            src = rb.at[way, step - 1, piece]
        target = right if way == 0 else left
        return rcopy(
            src,
            rb.at[way, step, piece],
            zs.at[way, step, piece],
            zr.at[way, step, piece],
            target,
            head,
        )

    def row(d, target):
        return rcopy(
            ob.at[d - 1], yb.at[d - 1], ys.at[d - 1], yr.at[d - 1], target * NZ + z, head
        )

    def cols(h):
        return pl.ds(pl.multiple_of(h * HD, HD), HD)

    def scatter(a, d, sender, target):
        home = outs[a].at[:, cols(sender)] if a < 2 else fin.at[2, a - 2, sender]
        return rcopy(pack.at[a, target], home, hs.at[a, d - 1], hr.at[a, d - 1], seq, target)

    def send_heads(a):
        for d in range(1, NH):
            scatter(a, d, head, (head + d) % NH).start()
        if a < 2:
            outs[a][:, cols(head)] = pack[a, head]
        else:
            fin[2, a - 2, head] = pack[a, head]

    def final(way, piece, d, sender, target):
        return rcopy(
            rb.at[way, half - 2, piece, target],
            fin.at[way, piece, sender],
            fs.at[way, piece, d],
            fr.at[way, piece, d],
            right if way == 0 else left,
            target,
        )

    def far(d, b):
        group = (y + d) % NY
        first = (group * NZ + z) * QB
        edge = jnp.where(b == 0, first - 1, jnp.where(b == QB - 1, first + QB, -1))
        blocks = [ids[r, first + b] for r in range(3)] + [gids[0], gids[1], edge]
        at = pl.ds(group * (QB // 2) + (b >> 1), 1)
        top = rows_ref[0, b & 1, at, 0:BLOCK]
        inverse = rows_ref[1, b & 1, at, 0:BLOCK]
        delta = rows_ref[2, b & 1, at, 0:BLOCK]
        rels = [block - base for block in blocks]
        live = [(rel >= 0) & (rel < COL) for rel in rels]
        rels = [jnp.clip(rel, 0, COL - 1) for rel in rels]
        keys = jnp.concatenate([kv_ref[rel >> 3, 0, rel & 7] for rel in rels], axis=0)
        values = jnp.concatenate([kv_ref[rel >> 3, 1, rel & 7] for rel in rels], axis=0)
        scores = lax.dot_general(keys, qg_ref[group, 0, b], NT, preferred_element_type=F32)
        dprobs = lax.dot_general(values, qg_ref[group, 1, b], NT, preferred_element_type=F32)
        weights = jnp.exp(scores * SCALE - top) * inverse
        weights = jnp.concatenate(
            [
                jnp.where(good, weights[n * BLOCK : (n + 1) * BLOCK], 0.0)
                for n, good in enumerate(live)
            ],
            axis=0,
        )
        probs = weights.astype(BF)
        dscores = (weights * (dprobs - delta)).astype(BF)
        out = lax.dot_general(probs, values, TN, preferred_element_type=F32)
        dq = lax.dot_general(dscores, keys, TN, preferred_element_type=F32) * SCALE
        if d < NY:
            ob[d - 1, 0, b] = out.astype(BF)
            ob[d - 1, 1, b] = dq.astype(BF)
        else:
            near_oq[0, b] = out
            near_oq[1, b] = dq

    def far_some(start, count):
        d = start // QB + 1

        def one(b, carry):
            far(d, b)
            return carry

        lax.fori_loop(start % QB, start % QB + count, one, 0)
        if d < NY and start % QB + count == QB:
            row(d, (y + d) % NY).start()

    def window(c):
        lo, hi, keys, values, queries, grads, scores, dprobs = window_tile(c, kv_ref, qg_ref, y, z)
        at = pl.ds(y * (QB // 2) + c, 1)
        weights = jnp.exp(scores - rows_ref[0, 0, at, :]) * rows_ref[1, 0, at, :]
        probs = weights.astype(BF)
        dscores = (weights * (dprobs - rows_ref[2, 0, at, :])).astype(BF)
        dv = lax.dot_general(probs, grads, NN, preferred_element_type=F32)
        dk = lax.dot_general(dscores, queries, NN, preferred_element_type=F32) * SCALE
        out = lax.dot_general(probs, values, TN, preferred_element_type=F32)
        dq = lax.dot_general(dscores, keys, TN, preferred_element_type=F32) * SCALE
        near_kv[0, lo:hi] += dk.reshape(hi - lo, BLOCK, HD)
        near_kv[1, lo:hi] += dv.reshape(hi - lo, BLOCK, HD)
        near_oq[0, 2 * c : 2 * c + 2] += out.reshape(2, BLOCK, HD)
        near_oq[1, 2 * c : 2 * c + 2] += dq.reshape(2, BLOCK, HD)

    def total():
        for d in range(1, NY):
            row(d, (y + d) % NY).wait_recv()

        def add(b, carry):
            for a in range(2):
                acc = near_oq[a, b]
                for d in range(NY - 1):
                    acc = acc + yb[d, a, b].astype(F32)
                pack[a, b] = acc.astype(BF)
            return carry

        lax.fori_loop(0, QB, add, 0)
        send_heads(0)
        send_heads(1)

    def give_near():
        def add(b, carry):
            for piece in range(2):
                acc = near_kv[piece, b] + dkv_ref[z, piece, b].astype(F32)
                pack[2 + piece, b] = acc.astype(BF)
            return carry

        lax.fori_loop(0, QB, add, 0)
        send_heads(2)
        send_heads(3)

    jobs = [functools.partial(far_some, n, 2) for n in range(6, NY * QB, 2)]
    for c in range(QB // 2):
        jobs += [functools.partial(window, c)]
    jobs += [give_near, lambda: None, total]

    hop(0, 0, 0).start()
    hop(1, 0, 1).start()
    for way, piece in ((0, 1), (1, 0)):
        hop(way, 1, piece).start()
    near_kv[...] = jnp.zeros((2, QB, BLOCK, HD), F32)
    for fetch in fetches:
        fetch.wait()
    for n in range(0, 6, 2):
        far_some(n, 2)

    for step in range(1, half):
        for piece in range(2):
            for way in range(2):
                if step == 1 and piece != way:
                    continue
                hop(way, step - 1, piece).wait_recv()
                chunk = chunk_of(way, step)

                def add(b, carry, way=way, step=step, piece=piece, chunk=chunk):
                    mine = dkv_ref[chunk, piece, b].astype(F32)
                    rb[way, step - 1, piece, b] = (
                        rb[way, step - 1, piece, b].astype(F32) + mine
                    ).astype(BF)
                    return carry

                lax.fori_loop(0, QB, add, 0)
                if step < half - 1:
                    hop(way, step, piece).start()
                else:
                    for d in TURNS:
                        final(way, piece, d, head, (head + d) % NH).start()
                if jobs:
                    jobs.pop(0)()
    for job in jobs:
        job()

    for a in range(4):
        for d in range(1, NH):
            scatter(a, d, (head + NH - d) % NH, (head + d) % NH).wait_recv()
    for piece in range(2):
        for way in range(2):
            for d in range(NH):
                final(way, piece, d, (head + NH - d) % NH, (head + d) % NH).wait_recv()

        for h in range(NH):
            acc = fin[2, piece, h].astype(F32)
            acc = acc + fin[0, piece, h].astype(F32)
            acc = acc + fin[1, piece, h].astype(F32)
            outs[2 + piece][:, h * HD : (h + 1) * HD] = acc.astype(BF)

    for a in range(4):
        for d in range(1, NH):
            scatter(a, d, head, (head + d) % NH).wait_send()
    for d in range(1, NY):
        row(d, (y + d) % NY).wait_send()
    for way in range(2):
        for piece in range(2):
            for d in range(NH):
                final(way, piece, d, head, (head + d) % NH).wait_send()
    for step in range(half - 1):
        for piece in range(2):
            for way in range(2):
                if step > 0 or piece == way:
                    hop(way, step, piece).wait_send()


def reduce(ids, gids, kv, qg, rows, dkv):
    dma = pltpu.SemaphoreType.DMA
    out = jax.ShapeDtypeStruct((BLOCK, NH * HD), BF)
    return pl.pallas_call(
        reduce_kernel,
        out_shape=(out,) * 4,
        in_specs=[hbm()] * 2 + [vmem()] * 4,
        out_specs=(vmem(),) * 4,
        scratch_shapes=[
            pltpu.VMEM((2, NZ // 2, 2, QB, BLOCK, HD), BF),
            pltpu.VMEM((NY - 1, 2, QB, BLOCK, HD), BF),
            pltpu.VMEM((NY - 1, 2, QB, BLOCK, HD), BF),
            pltpu.VMEM((4, NH, BLOCK, HD), BF),
            pltpu.VMEM((2, QB, BLOCK, HD), F32),
            pltpu.VMEM((2, QB, BLOCK, HD), F32),
            pltpu.VMEM((3, 2, NH, BLOCK, HD), BF),
            pltpu.SMEM((3, NZ * NY * QB), jnp.int32),
            pltpu.SMEM((2,), jnp.int32),
            dma((2,)),
            dma((4, NH - 1)),
            dma((4, NH - 1)),
            dma((2, 2, NH)),
            dma((2, 2, NH)),
            dma((2, NZ // 2, 2)),
            dma((2, NZ // 2, 2)),
            dma((NY - 1,)),
            dma((NY - 1,)),
        ],
        compiler_params=pltpu.CompilerParams(
            collective_id=2, has_side_effects=True, vmem_limit_bytes=32 * MIB
        ),
        name="reduce_rows",
    )(ids, gids, kv, qg, rows, dkv)


def deliver_kernel(*refs):
    sems = refs[8]
    copies = [pltpu.make_async_copy(refs[a], refs[4 + a], sems.at[a]) for a in range(4)]
    for copy in copies:
        copy.start()
    for copy in copies:
        copy.wait()


def deliver(outs):
    return pl.pallas_call(
        deliver_kernel,
        out_shape=tuple(jax.ShapeDtypeStruct(o.shape, o.dtype) for o in outs),
        in_specs=[vmem()] * 4,
        out_specs=(hbm(),) * 4,
        scratch_shapes=[pltpu.SemaphoreType.DMA((4,))],
        compiler_params=pltpu.CompilerParams(vmem_limit_bytes=8 * MIB),
        name="deliver_rows",
    )(*outs)


def shards(query_rows, key_rows, value_rows, out_grad, random_ids, global_ids):
    rows = (query_rows, key_rows, value_rows, out_grad)
    kv, qg, wst = gather(*(pltpu.with_memory_space_constraint(r, pltpu.HBM) for r in rows))
    ids = pltpu.with_memory_space_constraint(random_ids.T, pltpu.HBM)
    global_ids = pltpu.with_memory_space_constraint(global_ids, pltpu.HBM)
    pair_list, one, *pairs = stats(ids, kv, qg)
    sums = share(global_ids, wst, one, kv, qg)
    dkv, row_stats = terms(pair_list, global_ids, sums, kv, qg, (one, *pairs))
    return deliver(reduce(ids, global_ids, kv, qg, row_stats, dkv))


def solution(mesh):
    rows = P(("seq", "head"), None)
    return jax.shard_map(
        shards,
        mesh=mesh,
        in_specs=(rows, rows, rows, rows, P(), P()),
        out_specs=(rows,) * 4,
        check_vma=False,
    )
```

```python
import functools

import jax
import jax.numpy as jnp
from jax import lax
from jax.experimental import pallas as pl
from jax.experimental.pallas import tpu as pltpu
from jax.sharding import PartitionSpec as P

HD = 128
BLOCK = 64
QB = 8
NH = 8
NY = 4
NZ = 16
COL = NZ * QB
PLANE = NY * QB
SCALE = HD ** (-0.5)
FLOOR = -1e30
UNROLL = 8
TURNS = (4, 3, 5, 2, 6, 1, 7, 0)
TILES = PLANE // 4
TRASH = PLANE * 4 * COL
LIST = PLANE * 4 + 16
PAIRS = PLANE * 3 + 2 * NY + 8
MESH = pl.DeviceIdType.MESH
NT = (((1,), (1,)), ((), ()))
TN = (((0,), (0,)), ((), ()))
NN = (((1,), (0,)), ((), ()))
BF = jnp.bfloat16
F32 = jnp.float32
MIB = 1024 * 1024


def rcopy(src, dst, send, recv, seq, head):
    return pltpu.make_async_remote_copy(
        src_ref=src,
        dst_ref=dst,
        send_sem=send,
        recv_sem=recv,
        device_id=(seq, head),
        device_id_type=MESH,
    )


def place():
    seq = lax.axis_index("seq")
    head = lax.axis_index("head")
    return seq, head, seq // NZ, seq % NZ


def greet(peers, meanwhile=lambda: None):
    barrier = pltpu.get_barrier_semaphore()
    for seq, head in peers:
        pl.semaphore_signal(barrier, inc=1, device_id=(seq, head), device_id_type=MESH)
    meanwhile()
    pl.semaphore_wait(barrier, len(peers))


def head_peers(seq, head):
    return [(seq, (head + d) % NH) for d in range(1, NH)]


def row_peers(y, z, head):
    return [(((y + d) % NY) * NZ + z, head) for d in range(1, NY)]


def window_tile(c, kv_ref, qg_ref, y, z):
    lo, hi = max(2 * c - 1, 0), min(2 * c + 3, QB)
    shape = ((hi - lo) * BLOCK, HD)
    keys = kv_ref[z, 0, lo:hi].reshape(shape)
    values = kv_ref[z, 1, lo:hi].reshape(shape)
    queries = qg_ref[y, 0, 2 * c : 2 * c + 2].reshape(2 * BLOCK, HD)
    grads = qg_ref[y, 1, 2 * c : 2 * c + 2].reshape(2 * BLOCK, HD)
    scores = lax.dot_general(keys, queries, NT, preferred_element_type=F32) * SCALE
    dprobs = lax.dot_general(values, grads, NT, preferred_element_type=F32)
    gap = (lo - 2 * c) + (lax.broadcasted_iota(jnp.int32, shape, 0) >> 6)
    gap = gap - (lax.broadcasted_iota(jnp.int32, shape, 1) >> 6)
    near = (gap >= -1) & (gap <= 1)
    return lo, hi, keys, values, queries, grads, jnp.where(near, scores, FLOOR), dprobs


def near_planes(y, z):
    return [(y * NZ + (z + d) % NZ, h) for d in (1, NZ - 1) for h in range(NH)]


def gather_kernel(
    q_ref, k_ref, v_ref, g_ref, kv_ref, qg_ref, wst_ref, own, hs, hr, fs, fr, zs, zr, ys, yr
):
    seq, head, y, z = place()
    ins = (k_ref, v_ref, q_ref, g_ref)

    def home(a, sender):
        return kv_ref.at[z, a, sender] if a < 2 else qg_ref.at[y, a - 2, sender]

    def cols(h):
        return pl.ds(pl.multiple_of(h * HD, HD), HD)

    def keep(a):
        return pltpu.make_async_copy(ins[a].at[:, cols(head)], home(a, head), own.at[a])

    def give(a, d, sender, target):
        return rcopy(
            ins[a].at[:, cols(target)],
            home(a, sender),
            hs.at[a, d - 1],
            hr.at[a, d - 1],
            seq,
            target,
        )

    def give_all(a):
        for d in range(1, NH):
            give(a, d, head, (head + d) % NH).start()

    def take_all(a):
        for d in range(1, NH):
            give(a, d, (head + NH - d) % NH, (head + d) % NH).wait_recv()
        keep(a).wait()

    for a in range(4):
        keep(a).start()
    greet(head_peers(seq, head) + near_planes(y, z) + row_peers(y, z, head))
    right = y * NZ + (z + 1) % NZ
    left = y * NZ + (z + NZ - 1) % NZ
    sides = (right, left)

    def first(way, piece, d):
        target = (head + d) % NH
        return rcopy(
            ins[piece].at[:, cols(target)],
            kv_ref.at[z, piece, head],
            fs.at[way, piece, d],
            fr.at[way, piece, d],
            sides[way],
            target,
        )

    def first_in(way, piece, d):
        sender = (head + NH - d) % NH
        chunk = (z + NZ - 1 + 2 * way) % NZ
        return rcopy(
            ins[piece].at[:, cols(head)],
            kv_ref.at[chunk, piece, sender],
            fs.at[way, piece, d],
            fr.at[way, piece, d],
            sides[way],
            sender,
        )

    def hop(way, step, piece, back):
        if way == 0:
            chunk = (z + 2 * NZ - step - back) % NZ
        else:
            chunk = (z + step + back) % NZ
        ref = kv_ref.at[chunk, piece]
        return rcopy(ref, ref, zs.at[way, step, piece], zr.at[way, step, piece], sides[way], head)

    half = NZ // 2
    hops = [
        (way, step, piece)
        for step in range(1, half)
        for piece in range(2)
        for way in range(2)
        if step < half - 1 or piece == way
    ]
    for piece in range(2):
        for d in TURNS:
            for way in range(2):
                first(way, piece, d).start()
    def row(d, sender, target):
        ref = qg_ref.at[sender]
        return rcopy(ref, ref, ys.at[d - 1], yr.at[d - 1], target * NZ + z, head)

    wst_ref[0] = jnp.full((PLANE // 2, HD), FLOOR, F32)
    wst_ref[1] = jnp.zeros((PLANE // 2, HD), F32)
    wst_ref[2] = jnp.zeros((PLANE // 2, HD), F32)

    def window(c):
        _, _, _, _, _, _, scores, dprobs = window_tile(c, kv_ref, qg_ref, y, z)
        top = jnp.max(scores, axis=0, keepdims=True)
        expo = jnp.exp(scores - top)
        at = pl.ds(y * (QB // 2) + c, 1)
        wst_ref[0, at, :] = top
        wst_ref[1, at, :] = jnp.sum(expo, axis=0, keepdims=True)
        wst_ref[2, at, :] = jnp.sum(expo * dprobs, axis=0, keepdims=True)

    for way, step, piece in hops:
        if step == 1:
            for d in range(NH):
                first_in(way, piece, d).wait_recv()
        else:
            hop(way, step - 1, piece, 1).wait_recv()
        hop(way, step, piece, 0).start()
        if piece == 1 and way == 1:
            if step == 1:
                for a in (2, 3, 0, 1):
                    give_all(a)
            elif step == 3:
                for a in range(4):
                    take_all(a)
                for d in range(1, NY):
                    row(d, y, (y + d) % NY).start()
            elif step >= 4:
                window(step - 4)
    for d in range(1, NY):
        row(d, (y + NY - d) % NY, (y + d) % NY).wait_recv()
    for way, step, piece in hops:
        if step == half - 1 or (step == half - 2 and piece != way):
            hop(way, step, piece, 1).wait_recv()
    for a in range(4):
        for d in range(1, NH):
            give(a, d, head, (head + d) % NH).wait_send()
    for d in range(1, NY):
        row(d, y, (y + d) % NY).wait_send()
    for way in range(2):
        for piece in range(2):
            for d in range(NH):
                first(way, piece, d).wait_send()
    for way, step, piece in hops:
        hop(way, step, piece, 0).wait_send()


def vmem():
    return pl.BlockSpec(memory_space=pltpu.VMEM)


def smem():
    return pl.BlockSpec(memory_space=pltpu.SMEM)


def hbm():
    return pl.BlockSpec(memory_space=pltpu.HBM)


def gather(q, k, v, g):
    dma = pltpu.SemaphoreType.DMA
    return pl.pallas_call(
        gather_kernel,
        out_shape=(
            jax.ShapeDtypeStruct((NZ, 2, QB, BLOCK, HD), BF),
            jax.ShapeDtypeStruct((NY, 2, QB, BLOCK, HD), BF),
            jax.ShapeDtypeStruct((3, PLANE // 2, HD), F32),
        ),
        in_specs=[hbm()] * 4,
        out_specs=(vmem(),) * 3,
        scratch_shapes=[
            dma((4,)),
            dma((4, NH - 1)),
            dma((4, NH - 1)),
            dma((2, 2, NH)),
            dma((2, 2, NH)),
            dma((2, NZ // 2, 2)),
            dma((2, NZ // 2, 2)),
            dma((NY - 1,)),
            dma((NY - 1,)),
        ],
        compiler_params=pltpu.CompilerParams(
            collective_id=0, has_side_effects=True, vmem_limit_bytes=24 * MIB
        ),
        name="gather_rows",
    )(q, k, v, g)


def stats_kernel(ids_ref, kv_ref, qg_ref, list_ref, one, expo_ref, dprob_ref, ids, sem):
    y = lax.axis_index("seq") // NZ
    z = lax.axis_index("seq") % NZ
    base = y * COL
    fetch = pltpu.make_async_copy(ids_ref, ids, sem)
    fetch.start()
    one[0] = jnp.full((2, 5, PLANE // 2, HD), FLOOR, F32)
    for k in range(1, 3):
        one[k] = jnp.zeros((2, 5, PLANE // 2, HD), F32)
    fetch.wait()

    def note(count, i, slot, block):
        rel = block - base
        good = (rel >= 0) & (rel < COL)
        list_ref[count] = (i * 4 + slot) * COL + rel
        return count + good.astype(jnp.int32)

    count = jnp.int32(0)
    for g in range(NY):
        first = (g * NZ + z) * QB
        count = note(count, g * QB, 3, first - 1)
        count = note(count, g * QB + QB - 1, 3, first + QB)

        def scan(b, count, g=g, first=first):
            for r in range(3):
                count = note(count, g * QB + b, r, ids[r, first + b])
            return count

        count = lax.fori_loop(0, QB, scan, count, unroll=8)
    for u in range(UNROLL):
        list_ref[count + u] = jnp.int32(TRASH)
    rounds = (count + UNROLL - 1) >> 3
    list_ref[LIST - 1] = rounds

    def pairs(t, carry):
        done = []
        for u in range(UNROLL):
            code = list_ref[t * UNROLL + u]
            pair = code >> 7
            rel = code & (COL - 1)
            i = jnp.minimum(pair >> 2, PLANE - 1)
            keys = kv_ref[rel >> 3, 0, rel & 7]
            values = kv_ref[rel >> 3, 1, rel & 7]
            queries = qg_ref[i >> 3, 0, i & 7]
            grads = qg_ref[i >> 3, 1, i & 7]
            scores = lax.dot_general(keys, queries, NT, preferred_element_type=F32) * SCALE
            dprobs = lax.dot_general(values, grads, NT, preferred_element_type=F32)
            top = jnp.max(scores, axis=0, keepdims=True)
            expo = jnp.exp(scores - top)
            total = jnp.sum(expo, axis=0, keepdims=True)
            delta = jnp.sum(expo * dprobs, axis=0, keepdims=True)
            slot = jnp.where(code < TRASH, pair & 3, 4)
            done.append((i, slot, (top, total, delta), expo, dprobs))
        for u, (i, slot, found, expo, dprobs) in enumerate(done):
            expo_ref[t * UNROLL + u] = expo
            dprob_ref[t * UNROLL + u] = dprobs
            for k in range(3):
                one[k, i & 1, slot, pl.ds(i >> 1, 1), 0:BLOCK] = found[k]
        return carry

    lax.fori_loop(0, rounds, pairs, 0)


def tile_rows(qg_ref, t):
    at = slice((t % 2) * 4, (t % 2) * 4 + 4)
    queries = qg_ref[t // 2, 0, at].reshape(4 * BLOCK, HD)
    grads = qg_ref[t // 2, 1, at].reshape(4 * BLOCK, HD)
    return queries, grads


def stats(ids, kv, qg):
    return pl.pallas_call(
        stats_kernel,
        out_shape=(
            jax.ShapeDtypeStruct((LIST,), jnp.int32),
            jax.ShapeDtypeStruct((3, 2, 5, PLANE // 2, HD), F32),
            jax.ShapeDtypeStruct((PAIRS, BLOCK, BLOCK), F32),
            jax.ShapeDtypeStruct((PAIRS, BLOCK, BLOCK), F32),
        ),
        in_specs=[hbm(), vmem(), vmem()],
        out_specs=(smem(), vmem(), vmem(), vmem()),
        scratch_shapes=[
            pltpu.SMEM((3, NZ * NY * QB), jnp.int32),
            pltpu.SemaphoreType.DMA,
        ],
        compiler_params=pltpu.CompilerParams(vmem_limit_bytes=24 * MIB),
        name="pair_stats",
    )(ids, kv, qg)


def share_kernel(
    gids_ref, wst_ref, one, kv_ref, qg_ref, all_ref, full, st, gids, sem, send, recv
):
    seq, head, y, z = place()
    base = y * COL
    fetch = pltpu.make_async_copy(gids_ref, gids, sem)
    fetch.start()

    def total():
        fetch.wait()
        for n in range(2):
            rel = gids[n] - base
            good = (rel >= 0) & (rel < COL)
            rel = jnp.clip(rel, 0, COL - 1)
            keys = kv_ref[rel >> 3, 0, rel & 7]
            values = kv_ref[rel >> 3, 1, rel & 7]
            for t in range(TILES):
                queries, grads = tile_rows(qg_ref, t)
                scores = lax.dot_general(keys, queries, NT, preferred_element_type=F32) * SCALE
                dprobs = lax.dot_general(values, grads, NT, preferred_element_type=F32)
                top = jnp.max(scores, axis=0, keepdims=True)
                expo = jnp.exp(scores - top)
                found = (
                    jnp.where(good, top, FLOOR),
                    jnp.where(good, jnp.sum(expo, axis=0, keepdims=True), 0.0),
                    jnp.where(good, jnp.sum(expo * dprobs, axis=0, keepdims=True), 0.0),
                )
                for k in range(3):
                    for p in range(2):
                        full[k, n, 2 * t + p : 2 * t + p + 1] = found[k][:, p * HD : (p + 1) * HD]

        def parts(k):
            even = one[k, 0, 0:4]
            odd = pltpu.roll(one[k, 1, 0:4].reshape(2 * PLANE, HD), BLOCK, 1)
            odd = odd.reshape(4, PLANE // 2, HD)
            return jnp.concatenate([even, odd, full[k], wst_ref[k][None]], axis=0)

        tops = parts(0)
        top = jnp.max(tops, axis=0)
        factor = jnp.exp(tops - top[None])
        st[0] = top
        st[1] = jnp.sum(parts(1) * factor, axis=0)
        st[2] = jnp.sum(parts(2) * factor, axis=0)

    greet(row_peers(y, z, head), total)

    def row(d, sender, target):
        return rcopy(st, all_ref.at[sender], send.at[d - 1], recv.at[d - 1], target * NZ + z, head)

    for d in range(1, NY):
        row(d, y, (y + d) % NY).start()
    all_ref[y] = st[...]
    for d in range(1, NY):
        row(d, (y + NY - d) % NY, (y + d) % NY).wait_recv()
    for d in range(1, NY):
        row(d, y, (y + d) % NY).wait_send()


def share(gids, wst, one, kv, qg):
    dma = pltpu.SemaphoreType.DMA
    return pl.pallas_call(
        share_kernel,
        out_shape=jax.ShapeDtypeStruct((NY, 3, PLANE // 2, HD), F32),
        in_specs=[hbm()] + [vmem()] * 4,
        out_specs=vmem(),
        scratch_shapes=[
            pltpu.VMEM((3, 2, PLANE // 2, HD), F32),
            pltpu.VMEM((3, PLANE // 2, HD), F32),
            pltpu.SMEM((2,), jnp.int32),
            dma,
            dma((NY - 1,)),
            dma((NY - 1,)),
        ],
        compiler_params=pltpu.CompilerParams(
            collective_id=1, has_side_effects=True, vmem_limit_bytes=8 * MIB
        ),
        name="share_stats",
    )(gids, wst, one, kv, qg)


def terms_kernel(
    list_hbm,
    gids_hbm,
    all_ref,
    kv_ref,
    qg_ref,
    one,
    expo_ref,
    dprob_ref,
    dkv_ref,
    shifted,
    scale_ref,
    list_ref,
    gids,
    fetched,
):
    base = (lax.axis_index("seq") // NZ) * COL
    fetches = [
        pltpu.make_async_copy(list_hbm, list_ref, fetched.at[0]),
        pltpu.make_async_copy(gids_hbm, gids, fetched.at[1]),
    ]
    for fetch in fetches:
        fetch.start()
    tops = all_ref[:, 0]
    top = jnp.max(tops, axis=0)
    factor = jnp.exp(tops - top[None])
    inverse = 1.0 / jnp.sum(all_ref[:, 1] * factor, axis=0)
    delta = jnp.sum(all_ref[:, 2] * factor, axis=0) * inverse
    for k, value in enumerate((top, inverse, delta)):
        shifted[k, 0] = value
        shifted[k, 1] = pltpu.roll(value, BLOCK, 1)

    for p in range(2):
        factor = jnp.exp(one[0, p, 0:4] - shifted[0, p][None]) * shifted[1, p][None]
        scale_ref[p, 0:4] = factor
        scale_ref[p, 4] = jnp.zeros((PLANE // 2, HD), F32)

    def clear_kv(b, carry):
        dkv_ref[b] = jnp.zeros((2, QB, BLOCK, HD), BF)
        return carry

    lax.fori_loop(0, NZ, clear_kv, 0, unroll=4)
    for fetch in fetches:
        fetch.wait()
    rounds = list_ref[LIST - 1]

    def add_kv(rel, dk, dv):
        for a, term in enumerate((dk, dv)):
            old = dkv_ref[rel >> 3, a, rel & 7].astype(F32)
            dkv_ref[rel >> 3, a, rel & 7] = (old + term).astype(BF)

    def pairs(t, carry):
        done = []
        for u in range(UNROLL):
            code = list_ref[t * UNROLL + u]
            pair = code >> 7
            rel = code & (COL - 1)
            i = jnp.minimum(pair >> 2, PLANE - 1)
            at = pl.ds(i >> 1, 1)
            slot = jnp.where(code < TRASH, pair & 3, 4)
            queries = qg_ref[i >> 3, 0, i & 7]
            grads = qg_ref[i >> 3, 1, i & 7]
            weights = expo_ref[t * UNROLL + u] * scale_ref[i & 1, slot, at, 0:BLOCK]
            dprobs = dprob_ref[t * UNROLL + u]
            probs = weights.astype(BF)
            dscores = (weights * (dprobs - shifted[2, i & 1, at, 0:BLOCK])).astype(BF)
            dv = lax.dot_general(probs, grads, NN, preferred_element_type=F32)
            dk = lax.dot_general(dscores, queries, NN, preferred_element_type=F32) * SCALE
            done.append((rel, dk, dv))
        for rel, dk, dv in done:
            add_kv(rel, dk, dv)
        return carry

    lax.fori_loop(0, rounds, pairs, 0)

    for n in range(2):
        rel = gids[n] - base

        @pl.when((rel >= 0) & (rel < COL))
        def _(rel=rel):
            keys = kv_ref[rel >> 3, 0, rel & 7]
            values = kv_ref[rel >> 3, 1, rel & 7]
            dk = jnp.zeros((BLOCK, HD), F32)
            dv = jnp.zeros((BLOCK, HD), F32)
            for t in range(TILES):
                queries, grads = tile_rows(qg_ref, t)

                def wide(k, t=t):
                    pair = [shifted[k, 0, 2 * t + p : 2 * t + p + 1] for p in range(2)]
                    return jnp.concatenate(pair, axis=1)

                scores = lax.dot_general(keys, queries, NT, preferred_element_type=F32) * SCALE
                dprobs = lax.dot_general(values, grads, NT, preferred_element_type=F32)
                weights = jnp.exp(scores - wide(0)) * wide(1)
                probs = weights.astype(BF)
                dscores = (weights * (dprobs - wide(2))).astype(BF)
                dv = dv + lax.dot_general(probs, grads, NN, preferred_element_type=F32)
                dk = dk + lax.dot_general(dscores, queries, NN, preferred_element_type=F32) * SCALE
            add_kv(rel, dk, dv)


def terms(pair_list, gids, all_stats, kv, qg, pairs):
    return pl.pallas_call(
        terms_kernel,
        out_shape=(
            jax.ShapeDtypeStruct((NZ, 2, QB, BLOCK, HD), BF),
            jax.ShapeDtypeStruct((3, 2, PLANE // 2, HD), F32),
        ),
        in_specs=[pl.BlockSpec(memory_space=pl.ANY), hbm()] + [vmem()] * 6,
        out_specs=(vmem(),) * 2,
        scratch_shapes=[
            pltpu.VMEM((2, 5, PLANE // 2, HD), F32),
            pltpu.SMEM((LIST,), jnp.int32),
            pltpu.SMEM((2,), jnp.int32),
            pltpu.SemaphoreType.DMA((2,)),
        ],
        compiler_params=pltpu.CompilerParams(vmem_limit_bytes=32 * MIB),
        name="pair_terms",
    )(pair_list, gids, all_stats, kv, qg, *pairs)


def reduce_kernel(
    ids_ref,
    gids_ref,
    kv_ref,
    qg_ref,
    rows_ref,
    dkv_ref,
    o_ref,
    dq_ref,
    dk_ref,
    dv_ref,
    rb,
    ob,
    yb,
    pack,
    near_kv,
    near_oq,
    fin,
    ids,
    gids,
    fetched,
    hs,
    hr,
    fs,
    fr,
    zs,
    zr,
    ys,
    yr,
):
    seq, head, y, z = place()
    fetches = [
        pltpu.make_async_copy(ids_ref, ids, fetched.at[0]),
        pltpu.make_async_copy(gids_ref, gids, fetched.at[1]),
    ]
    for fetch in fetches:
        fetch.start()
    greet(head_peers(seq, head) + near_planes(y, z) + row_peers(y, z, head))
    right = y * NZ + (z + 1) % NZ
    left = y * NZ + (z + NZ - 1) % NZ
    half = NZ // 2
    base = y * COL
    outs = (o_ref, dq_ref, dk_ref, dv_ref)

    def chunk_of(way, step):
        if way == 0:
            return (z + half - step) % NZ
        return (z + half + step) % NZ

    def hop(way, step, piece):
        if step == 0 or (step == 1 and piece != way):
            src = dkv_ref.at[chunk_of(way, step), piece]
        else:
            src = rb.at[way, step - 1, piece]
        target = right if way == 0 else left
        return rcopy(
            src,
            rb.at[way, step, piece],
            zs.at[way, step, piece],
            zr.at[way, step, piece],
            target,
            head,
        )

    def row(d, target):
        return rcopy(
            ob.at[d - 1], yb.at[d - 1], ys.at[d - 1], yr.at[d - 1], target * NZ + z, head
        )

    def cols(h):
        return pl.ds(pl.multiple_of(h * HD, HD), HD)

    def scatter(a, d, sender, target):
        home = outs[a].at[:, cols(sender)] if a < 2 else fin.at[2, a - 2, sender]
        return rcopy(pack.at[a, target], home, hs.at[a, d - 1], hr.at[a, d - 1], seq, target)

    def send_heads(a):
        for d in range(1, NH):
            scatter(a, d, head, (head + d) % NH).start()
        if a < 2:
            outs[a][:, cols(head)] = pack[a, head]
        else:
            fin[2, a - 2, head] = pack[a, head]

    def final(way, piece, d, sender, target):
        return rcopy(
            rb.at[way, half - 2, piece, target],
            fin.at[way, piece, sender],
            fs.at[way, piece, d],
            fr.at[way, piece, d],
            right if way == 0 else left,
            target,
        )

    def far(d, b):
        group = (y + d) % NY
        first = (group * NZ + z) * QB
        edge = jnp.where(b == 0, first - 1, jnp.where(b == QB - 1, first + QB, -1))
        blocks = [ids[r, first + b] for r in range(3)] + [gids[0], gids[1], edge]
        at = pl.ds(group * (QB // 2) + (b >> 1), 1)
        top = rows_ref[0, b & 1, at, 0:BLOCK]
        inverse = rows_ref[1, b & 1, at, 0:BLOCK]
        delta = rows_ref[2, b & 1, at, 0:BLOCK]
        rels = [block - base for block in blocks]
        live = [(rel >= 0) & (rel < COL) for rel in rels]
        rels = [jnp.clip(rel, 0, COL - 1) for rel in rels]
        keys = jnp.concatenate([kv_ref[rel >> 3, 0, rel & 7] for rel in rels], axis=0)
        values = jnp.concatenate([kv_ref[rel >> 3, 1, rel & 7] for rel in rels], axis=0)
        scores = lax.dot_general(keys, qg_ref[group, 0, b], NT, preferred_element_type=F32)
        dprobs = lax.dot_general(values, qg_ref[group, 1, b], NT, preferred_element_type=F32)
        weights = jnp.exp(scores * SCALE - top) * inverse
        weights = jnp.concatenate(
            [
                jnp.where(good, weights[n * BLOCK : (n + 1) * BLOCK], 0.0)
                for n, good in enumerate(live)
            ],
            axis=0,
        )
        probs = weights.astype(BF)
        dscores = (weights * (dprobs - delta)).astype(BF)
        out = lax.dot_general(probs, values, TN, preferred_element_type=F32)
        dq = lax.dot_general(dscores, keys, TN, preferred_element_type=F32) * SCALE
        if d < NY:
            ob[d - 1, 0, b] = out.astype(BF)
            ob[d - 1, 1, b] = dq.astype(BF)
        else:
            near_oq[0, b] = out
            near_oq[1, b] = dq

    def far_some(start, count):
        d = start // QB + 1

        def one(b, carry):
            far(d, b)
            return carry

        lax.fori_loop(start % QB, start % QB + count, one, 0, unroll=True)
        if d < NY and start % QB + count == QB:
            row(d, (y + d) % NY).start()

    def window(c):
        lo, hi, keys, values, queries, grads, scores, dprobs = window_tile(c, kv_ref, qg_ref, y, z)
        at = pl.ds(y * (QB // 2) + c, 1)
        weights = jnp.exp(scores - rows_ref[0, 0, at, :]) * rows_ref[1, 0, at, :]
        probs = weights.astype(BF)
        dscores = (weights * (dprobs - rows_ref[2, 0, at, :])).astype(BF)
        dv = lax.dot_general(probs, grads, NN, preferred_element_type=F32)
        dk = lax.dot_general(dscores, queries, NN, preferred_element_type=F32) * SCALE
        out = lax.dot_general(probs, values, TN, preferred_element_type=F32)
        dq = lax.dot_general(dscores, keys, TN, preferred_element_type=F32) * SCALE
        near_kv[0, lo:hi] += dk.reshape(hi - lo, BLOCK, HD)
        near_kv[1, lo:hi] += dv.reshape(hi - lo, BLOCK, HD)
        near_oq[0, 2 * c : 2 * c + 2] += out.reshape(2, BLOCK, HD)
        near_oq[1, 2 * c : 2 * c + 2] += dq.reshape(2, BLOCK, HD)

    def total():
        for d in range(1, NY):
            row(d, (y + d) % NY).wait_recv()

        def add(b, carry):
            for a in range(2):
                acc = near_oq[a, b]
                for d in range(NY - 1):
                    acc = acc + yb[d, a, b].astype(F32)
                pack[a, b] = acc.astype(BF)
            return carry

        lax.fori_loop(0, QB, add, 0)
        send_heads(0)
        send_heads(1)

    def give_near():
        def add(b, carry):
            for piece in range(2):
                acc = near_kv[piece, b] + dkv_ref[z, piece, b].astype(F32)
                pack[2 + piece, b] = acc.astype(BF)
            return carry

        lax.fori_loop(0, QB, add, 0)
        send_heads(2)
        send_heads(3)

    jobs = [functools.partial(far_some, n, 2) for n in range(6, NY * QB, 2)]
    for c in range(QB // 2):
        jobs += [functools.partial(window, c)]
    jobs += [give_near, lambda: None, total]

    hop(0, 0, 0).start()
    hop(1, 0, 1).start()
    for way, piece in ((0, 1), (1, 0)):
        hop(way, 1, piece).start()
    near_kv[...] = jnp.zeros((2, QB, BLOCK, HD), F32)
    for fetch in fetches:
        fetch.wait()
    for n in range(0, 6, 2):
        far_some(n, 2)

    for step in range(1, half):
        for piece in range(2):
            for way in range(2):
                if step == 1 and piece != way:
                    continue
                hop(way, step - 1, piece).wait_recv()
                chunk = chunk_of(way, step)

                def add(b, carry, way=way, step=step, piece=piece, chunk=chunk):
                    mine = dkv_ref[chunk, piece, b].astype(F32)
                    rb[way, step - 1, piece, b] = (
                        rb[way, step - 1, piece, b].astype(F32) + mine
                    ).astype(BF)
                    return carry

                lax.fori_loop(0, QB, add, 0)
                if step < half - 1:
                    hop(way, step, piece).start()
                else:
                    for d in TURNS:
                        final(way, piece, d, head, (head + d) % NH).start()
                if jobs:
                    jobs.pop(0)()
    for job in jobs:
        job()

    for a in range(4):
        for d in range(1, NH):
            scatter(a, d, (head + NH - d) % NH, (head + d) % NH).wait_recv()
    for piece in range(2):
        for way in range(2):
            for d in range(NH):
                final(way, piece, d, (head + NH - d) % NH, (head + d) % NH).wait_recv()

        for h in range(NH):
            acc = fin[2, piece, h].astype(F32)
            acc = acc + fin[0, piece, h].astype(F32)
            acc = acc + fin[1, piece, h].astype(F32)
            outs[2 + piece][:, h * HD : (h + 1) * HD] = acc.astype(BF)

    for a in range(4):
        for d in range(1, NH):
            scatter(a, d, head, (head + d) % NH).wait_send()
    for d in range(1, NY):
        row(d, (y + d) % NY).wait_send()
    for way in range(2):
        for piece in range(2):
            for d in range(NH):
                final(way, piece, d, head, (head + d) % NH).wait_send()
    for step in range(half - 1):
        for piece in range(2):
            for way in range(2):
                if step > 0 or piece == way:
                    hop(way, step, piece).wait_send()


def reduce(ids, gids, kv, qg, rows, dkv):
    dma = pltpu.SemaphoreType.DMA
    out = jax.ShapeDtypeStruct((BLOCK, NH * HD), BF)
    return pl.pallas_call(
        reduce_kernel,
        out_shape=(out,) * 4,
        in_specs=[hbm()] * 2 + [vmem()] * 4,
        out_specs=(vmem(),) * 4,
        scratch_shapes=[
            pltpu.VMEM((2, NZ // 2, 2, QB, BLOCK, HD), BF),
            pltpu.VMEM((NY - 1, 2, QB, BLOCK, HD), BF),
            pltpu.VMEM((NY - 1, 2, QB, BLOCK, HD), BF),
            pltpu.VMEM((4, NH, BLOCK, HD), BF),
            pltpu.VMEM((2, QB, BLOCK, HD), F32),
            pltpu.VMEM((2, QB, BLOCK, HD), F32),
            pltpu.VMEM((3, 2, NH, BLOCK, HD), BF),
            pltpu.SMEM((3, NZ * NY * QB), jnp.int32),
            pltpu.SMEM((2,), jnp.int32),
            dma((2,)),
            dma((4, NH - 1)),
            dma((4, NH - 1)),
            dma((2, 2, NH)),
            dma((2, 2, NH)),
            dma((2, NZ // 2, 2)),
            dma((2, NZ // 2, 2)),
            dma((NY - 1,)),
            dma((NY - 1,)),
        ],
        compiler_params=pltpu.CompilerParams(
            collective_id=2, has_side_effects=True, vmem_limit_bytes=32 * MIB
        ),
        name="reduce_rows",
    )(ids, gids, kv, qg, rows, dkv)


def deliver_kernel(*refs):
    sems = refs[8]
    copies = [pltpu.make_async_copy(refs[a], refs[4 + a], sems.at[a]) for a in range(4)]
    for copy in copies:
        copy.start()
    for copy in copies:
        copy.wait()


def deliver(outs):
    return pl.pallas_call(
        deliver_kernel,
        out_shape=tuple(jax.ShapeDtypeStruct(o.shape, o.dtype) for o in outs),
        in_specs=[vmem()] * 4,
        out_specs=(hbm(),) * 4,
        scratch_shapes=[pltpu.SemaphoreType.DMA((4,))],
        compiler_params=pltpu.CompilerParams(vmem_limit_bytes=8 * MIB),
        name="deliver_rows",
    )(*outs)


def shards(query_rows, key_rows, value_rows, out_grad, random_ids, global_ids):
    rows = (query_rows, key_rows, value_rows, out_grad)
    kv, qg, wst = gather(*(pltpu.with_memory_space_constraint(r, pltpu.HBM) for r in rows))
    ids = pltpu.with_memory_space_constraint(random_ids.T, pltpu.HBM)
    global_ids = pltpu.with_memory_space_constraint(global_ids, pltpu.HBM)
    pair_list, one, *pairs = stats(ids, kv, qg)
    sums = share(global_ids, wst, one, kv, qg)
    dkv, row_stats = terms(pair_list, global_ids, sums, kv, qg, (one, *pairs))
    return deliver(reduce(ids, global_ids, kv, qg, row_stats, dkv))


def solution(mesh):
    rows = P(("seq", "head"), None)
    return jax.shard_map(
        shards,
        mesh=mesh,
        in_specs=(rows, rows, rows, rows, P(), P()),
        out_specs=(rows,) * 4,
        check_vma=False,
    )
```
